32 devices in a mesh: dp: 4 (over y, core), fsdp: 8 (over z, x).
Axes of the slice: x: 2, y: 2, z: 4, core: 2. Of those that a mesh axis runs over, the one named last changes fastest.
Arguments:
- inputs: bfloat16 [128, 392, 512], P(('dp', 'fsdp')), may hold values from -6 to 6
- extents: int32 [128, 3], P(('dp', 'fsdp')), may hold values from 1 to 8, as said below
- cotangent: bfloat16 [128, 392, 512], P(('dp', 'fsdp')), may hold values from -6 to 6
- ln1_gain: bfloat16 [512], P(('dp', 'fsdp')), may hold values from 0.25 to 1.75
- ln1_shift: bfloat16 [512], P(('dp', 'fsdp')), may hold values from -3 to 3
- qkv_weight: bfloat16 [512, 1536], P(('dp', 'fsdp')), may hold values from -0.25 to 0.25
- query_bias: bfloat16 [512], P(('dp', 'fsdp')), may hold values from -3 to 3
- value_bias: bfloat16 [512], P(('dp', 'fsdp')), may hold values from -3 to 3
- bias_table: bfloat16 [2535, 16], replicated, may hold values from -4 to 4
- proj_weight: bfloat16 [512, 512], P(('dp', 'fsdp')), may hold values from -2 to 2
- proj_shift: bfloat16 [512], P(('dp', 'fsdp')), may hold values from -3 to 3
- ln2_gain: bfloat16 [512], P(('dp', 'fsdp')), may hold values from 0.25 to 1.75
- ln2_shift: bfloat16 [512], P(('dp', 'fsdp')), may hold values from -3 to 3
- fc1_weight: bfloat16 [512, 2048], P(('dp', 'fsdp')), may hold values from -0.25 to 0.25
- fc1_shift: bfloat16 [2048], P(('dp', 'fsdp')), may hold values from -3 to 3
- fc2_weight: bfloat16 [2048, 512], P(('dp', 'fsdp')), may hold values from -0.125 to 0.125
- fc2_shift: bfloat16 [512], P(('dp', 'fsdp')), may hold values from -3 to 3
Outputs:
- output: bfloat16 [128, 392, 512], P(('dp', 'fsdp'))
- input_grad: bfloat16 [128, 392, 512], P(('dp', 'fsdp'))
- ln1_gain_grad: float32 [512], P(('dp', 'fsdp'))
- ln1_shift_grad: float32 [512], P(('dp', 'fsdp'))
- qkv_weight_grad: float32 [512, 1536], P(('dp', 'fsdp'))
- query_bias_grad: float32 [512], P(('dp', 'fsdp'))
- value_bias_grad: float32 [512], P(('dp', 'fsdp'))
- bias_table_grad: float32 [2535, 16], replicated
- proj_weight_grad: float32 [512, 512], P(('dp', 'fsdp'))
- proj_shift_grad: float32 [512], P(('dp', 'fsdp'))
- ln2_gain_grad: float32 [512], P(('dp', 'fsdp'))
- ln2_shift_grad: float32 [512], P(('dp', 'fsdp'))
- fc1_weight_grad: float32 [512, 2048], P(('dp', 'fsdp'))
- fc1_shift_grad: float32 [2048], P(('dp', 'fsdp'))
- fc2_weight_grad: float32 [2048, 512], P(('dp', 'fsdp'))
- fc2_shift_grad: float32 [512], P(('dp', 'fsdp'))
The draws below stay inside these ranges and needn't reach their ends.
Inputs may be any that keep to these rules, and one draw needn't show every extreme that they name: `extents`: each row gives a window's valid frames, patch rows and patch columns, each at least 1 and at most the window's extent along it; the first window of the whole array is complete.
All inputs are finite; a program needn't handle non-finite values.
Results may differ from the reference program's by a relative error of at most 0.012.
Values may be sent and summed in bfloat16 or wider, within the bound.
A program may use at most 448 MiB of HBM per device.

```python
import jax
import jax.numpy as jnp
from jax import lax

D = 512
HEADS = 16
HDIM = 32
FF = 2048
WIN_T = 8
WIN_H = 7
WIN_W = 7
W_DEV = 4
WIN = 392
TABLE = 2535
WINDOWS = 128


def draw_extents(key, part):
    keys = jax.random.split(jax.random.fold_in(key, 11), 4)
    depth = jax.random.randint(keys[0], (WINDOWS,), 1, WIN_T + 1)
    height = jax.random.randint(keys[1], (WINDOWS,), 1, WIN_H + 1)
    across = jax.random.randint(keys[2], (WINDOWS,), 1, WIN_W + 1)
    drawn = jnp.stack([depth, height, across], axis=1)
    complete = jax.random.randint(keys[3], (WINDOWS, 1), 0, 2)
    first = jnp.arange(WINDOWS, dtype=jnp.int32)[:, None] == 0
    full_row = jnp.array([WIN_T, WIN_H, WIN_W], dtype=jnp.int32)[None, :]
    return jnp.where((complete > 0) | first, full_row, drawn).astype(jnp.int32)


def raised(values, own_key, source, target, shards_of, factor):
    def block_of(position):
        return (jnp.arange(values.shape[position]) // (values.shape[position] // shards_of)).reshape((-1,) + (1,) * (values.ndim - 1 - position))

    first = jax.random.permutation(own_key, shards_of)[block_of(target)]
    far = (block_of(target) + shards_of // 2) % shards_of
    return jnp.where((block_of(source) == first) | (block_of(source) == far), factor * values, values)


def shard_levels(key, dims, pieces, least, largest):
    level, own = 1.0, jax.random.fold_in(key, 6)
    for axis_at, parts in pieces:
        draws = jnp.exp(jax.random.uniform(jax.random.fold_in(own, axis_at), (parts,), jnp.float32, least / len(pieces), largest / len(pieces)))
        level = level * jnp.repeat(draws, dims[axis_at] // parts).reshape([-1 if axis == axis_at else 1 for axis in range(len(dims))])
    return level


def noise(stream_key, dims, width, reach, shards=(), kind=jnp.bfloat16):
    gain = shard_levels(stream_key, dims, shards, -0.22, 0.18) if shards else 1.0
    entries = jax.random.normal(stream_key, dims, jnp.float32) * width * gain
    return jnp.minimum(jnp.maximum(entries, -reach), reach).astype(kind)


def bell_draw_with(key, shape, spread, bound, cuts, heavy, held_as=jnp.bfloat16):
    values = spread * jax.random.normal(key, shape, jnp.float32)
    if cuts:
        values = values * shard_levels(key, shape, cuts, -0.22, 0.18)
    return jnp.clip(raised(values, jax.random.fold_in(key, 3), *heavy), -bound, bound).astype(held_as)


def setup_inputs(seed: int = 0) -> dict:
    key_of = jax.random.split(jax.random.key(seed), 18)
    return {
        "inputs": noise(key_of[0], (WINDOWS, WIN, D), 1.0, 6.0, ((0, 32),)),
        "extents": draw_extents(jax.random.fold_in(key_of[17], 71), 0),
        "cotangent": bell_draw_with(key_of[2], (WINDOWS, WIN, D), 1.0, 6.0, ((0, 32),), (0, 2, 32, 2.75)),
        "ln1_gain": jnp.clip(1.0 + 0.15 * jax.random.normal(key_of[3], (D,), jnp.float32), 0.25, 1.75).astype(jnp.bfloat16),
        "ln1_shift": noise(key_of[4], (D,), 0.3, 3.0, ((0, 32),)),
        "qkv_weight": noise(key_of[5], (D, 3 * D), D ** -0.5, 0.25, ((0, 32),)),
        "query_bias": noise(key_of[6], (D,), 0.5, 3.0, ((0, 32),)),
        "value_bias": noise(key_of[7], (D,), 0.5, 3.0, ((0, 32),)),
        "bias_table": noise(key_of[8], (TABLE, HEADS), 1.0, 4.0),
        "proj_weight": noise(key_of[9], (D, D), (D // 64) ** -0.5, 2.0, ((0, 32),)),
        "proj_shift": noise(key_of[10], (D,), 0.5, 3.0, ((0, 32),)),
        "ln2_gain": jnp.clip(1.0 + 0.15 * jax.random.normal(key_of[11], (D,), jnp.float32), 0.25, 1.75).astype(jnp.bfloat16),
        "ln2_shift": noise(key_of[12], (D,), 0.3, 3.0, ((0, 32),)),
        "fc1_weight": noise(key_of[13], (D, FF), D ** -0.5, 0.25, ((0, 32),)),
        "fc1_shift": noise(key_of[14], (FF,), 0.5, 3.0, ((0, 32),)),
        "fc2_weight": noise(key_of[15], (FF, D), FF ** -0.5, 0.125, ((0, 32),)),
        "fc2_shift": noise(key_of[16], (D,), 0.5, 3.0, ((0, 32),)),
    }


EPS = 1e-05
HIGHEST = lax.Precision.HIGHEST

@jax.custom_vjp
def low(v):
    return lax.optimization_barrier(v.astype(jnp.bfloat16)).astype(jnp.float32)

@jax.custom_vjp
def low_back(v):
    return v

def low_keep(v):
    return (low(v), None)

def low_pass(kept, grad):
    return (grad,)

def back_keep(v):
    return (v, None)

def back_low(kept, grad):
    return (low(grad),)
low.defvjp(low_keep, low_pass)
low_back.defvjp(back_keep, back_low)

def positions():
    spots = jnp.arange(WIN, dtype=jnp.int32)
    return (spots // (WIN_H * WIN_W), spots // WIN_W % WIN_H, spots % WIN_W)

def relative_index():
    depth, height, across = positions()
    span_h = 2 * WIN_H - 1
    span_w = 2 * WIN_W - 1
    return ((depth[:, None] - depth[None, :] + WIN_T - 1) * (span_h * span_w) + (height[:, None] - height[None, :] + WIN_H - 1) * span_w + (across[:, None] - across[None, :] + WIN_W - 1)).astype(jnp.int32)

def valid_mask(extents):
    depth, height, across = positions()
    return (depth[None, :] < extents[:, 0:1]) & (height[None, :] < extents[:, 1:2]) & (across[None, :] < extents[:, 2:3])

def layer_norm(values, gain_vec, shift_vec):
    average = lax.optimization_barrier(jnp.mean(values, axis=-1, keepdims=True))
    centered = values - average
    variance = lax.optimization_barrier(jnp.mean(centered * centered, axis=-1, keepdims=True))
    return centered * lax.rsqrt(variance + EPS) * gain_vec + shift_vec

def exact_gelu(values):
    return jax.nn.gelu(values, approximate=False)

def window_attention(qkv_block, keep_block, bias):
    count = qkv_block.shape[0]
    split = qkv_block.reshape(count, WIN, 3, HEADS, HDIM)
    queries = split[:, :, 0]
    key_part = split[:, :, 1]
    values = split[:, :, 2]
    scores = jnp.einsum('gqhd,gkhd->ghqk', queries, key_part, precision=HIGHEST) * HDIM ** (-0.5) + bias[None]
    scores = low_back(scores)
    scores = jnp.where(keep_block[:, None, None, :] > 0, scores, -jnp.inf)
    top = lax.optimization_barrier(jnp.max(scores, axis=-1, keepdims=True))
    expo = jnp.exp(scores - top)
    probs = expo / lax.optimization_barrier(jnp.sum(expo, axis=-1, keepdims=True))
    mixed = jnp.einsum('ghqk,gkhd->gqhd', low(probs), values, precision=HIGHEST)
    return mixed.reshape(count, WIN, D)

def forward(inputs, keep, ln1_gain, ln1_shift, qkv_weight, query_bias, value_bias, bias_table, proj_weight, proj_shift, ln2_gain, ln2_shift, fc1_weight, fc1_shift, fc2_weight, fc2_shift):
    rows = inputs.reshape(-1, D)
    normed_one = low(layer_norm(rows, ln1_gain, ln1_shift))
    qkv_shift = jnp.concatenate([query_bias, jnp.zeros_like(query_bias), value_bias])
    qkv_rows = low(low_back(jnp.dot(normed_one, qkv_weight, precision=HIGHEST) + qkv_shift))
    bias = jnp.transpose(bias_table[relative_index()], (2, 0, 1))
    groups = qkv_rows.reshape(-1, W_DEV, WIN, 3 * D)
    keep_groups = keep.reshape(-1, W_DEV, WIN)

    def one_group(item):
        return window_attention(item[0], item[1], bias)
    mixed = lax.map(jax.checkpoint(one_group), (groups, keep_groups))
    attended = low(low_back(mixed.reshape(-1, D)))
    branch = low_back(jnp.dot(attended, proj_weight, precision=HIGHEST) + proj_shift)
    resid = rows + branch
    normed_two = low(layer_norm(resid, ln2_gain, ln2_shift))
    hidden = low_back(jnp.dot(normed_two, fc1_weight, precision=HIGHEST) + fc1_shift)
    active = low(exact_gelu(hidden))
    out_branch = low_back(jnp.dot(active, fc2_weight, precision=HIGHEST) + fc2_shift)
    return ((resid + out_branch) * keep.reshape(-1, 1)).reshape(inputs.shape)

def reference(inputs, extents, cotangent, ln1_gain, ln1_shift, qkv_weight, query_bias, value_bias, bias_table, proj_weight, proj_shift, ln2_gain, ln2_shift, fc1_weight, fc1_shift, fc2_weight, fc2_shift):
    keep = valid_mask(extents).astype(jnp.float32)
    params = (ln1_gain, ln1_shift, qkv_weight, query_bias, value_bias, bias_table, proj_weight, proj_shift, ln2_gain, ln2_shift, fc1_weight, fc1_shift, fc2_weight, fc2_shift)
    params = tuple((item.astype(jnp.float32) for item in params))

    def wrapped(source, *weights):
        return forward(source, keep, *weights)
    result, pullback = jax.vjp(wrapped, inputs.astype(jnp.float32), *params)
    grads = pullback(cotangent.astype(jnp.float32))
    return (result.astype(jnp.bfloat16), grads[0].astype(jnp.bfloat16), grads[1], grads[2], grads[3], grads[4], grads[5], grads[6], grads[7], grads[8], grads[9], grads[10], grads[11], grads[12], grads[13], grads[14])
```

```python
import functools
import math

import jax
import jax.numpy as jnp
import numpy as np
from jax import lax
from jax.experimental import pallas as pl
from jax.experimental.pallas import tpu as pltpu
from jax.sharding import PartitionSpec as P

D = 512
HEADS = 16
HDIM = 32
FF = 2048
WIN_T = 8
WIN_H = 7
WIN_W = 7
WIN = WIN_T * WIN_H * WIN_W
FLAT = WIN_H * WIN_W
OFFS_T = 2 * WIN_T - 1
OFFS_H = 2 * WIN_H - 1
OFFS_W = 2 * WIN_W - 1
SPREAD = OFFS_T * FLAT
EPS = 1e-05
LOG2E = math.log2(math.e)
LN2 = math.log(2.0)
SCALE = HDIM ** (-0.5)
AXES = ("dp", "fsdp")
BF16 = jnp.bfloat16
F32 = jnp.float32
MIB = 2**20


def dot(left, right, left_dim, right_dim):
    return lax.dot_general(
        left, right, (((left_dim,), (right_dim,)), ((), ())), preferred_element_type=F32
    )


def dot_nn(left, right):
    return dot(left, right, 1, 0)


def dot_nt(left, right):
    return dot(left, right, 1, 1)


def dot_tn(left, right):
    return dot(left, right, 0, 0)


def standardize(rows):
    average = jnp.mean(rows, axis=-1, keepdims=True)
    centered = rows - average
    variance = jnp.mean(centered * centered, axis=-1, keepdims=True)
    scale = lax.rsqrt(variance + EPS)
    return centered * scale, scale


def norm_backward(grad, unit, scale, gain):
    scaled = grad * gain
    first = jnp.mean(scaled, axis=-1, keepdims=True)
    second = jnp.mean(scaled * unit, axis=-1, keepdims=True)
    return (scaled - first - unit * second) * scale


def gelu_parts(hidden):
    reach = jnp.abs(hidden) * (0.5**0.5)
    ratio = 1.0 / (1.0 + 0.3275911 * reach)
    series = 1.061405429 * ratio - 1.453152027
    series = series * ratio + 1.421413741
    series = series * ratio - 0.284496736
    series = series * ratio + 0.254829592
    bell = jnp.exp(-0.5 * hidden * hidden)
    tail = (0.5 * series) * (ratio * bell)
    below = jnp.where(hidden < 0, tail, 1.0 - tail)
    return hidden * below, below + hidden * bell * (1.0 / math.sqrt(2 * math.pi))


def qkv_kernel(x_ref, gain_ref, shift_ref, weight_ref, bias_ref, out_ref):
    unit, _ = standardize(x_ref[...].astype(F32))
    normed = (unit * gain_ref[...] + shift_ref[...]).astype(BF16)
    for part in range(3):
        columns = slice(part * D, (part + 1) * D)
        got = dot_nn(normed, weight_ref[:, columns]) + bias_ref[:, columns]
        if part == 0:
            got = got * (SCALE * LOG2E)
        out_ref[:, columns] = got.astype(BF16)


def project_qkv(x_rows, gain, shift, weight, bias):
    rows = x_rows.shape[0]
    block = rows // 2
    whole = lambda i: (0, 0)
    return pl.pallas_call(
        qkv_kernel,
        grid=(2,),
        in_specs=[
            pl.BlockSpec((block, D), lambda i: (i, 0)),
            pl.BlockSpec((1, D), whole),
            pl.BlockSpec((1, D), whole),
            pl.BlockSpec((D, 3 * D), whole),
            pl.BlockSpec((1, 3 * D), whole),
        ],
        out_specs=pl.BlockSpec((block, 3 * D), lambda i: (i, 0)),
        out_shape=jax.ShapeDtypeStruct((rows, 3 * D), BF16),
        compiler_params=pltpu.CompilerParams(vmem_limit_bytes=48 * MIB),
        name="norm_qkv",
    )(x_rows, gain, shift, weight, bias)


def attend_kernel(
    windows, qkv_ref, spread_ref, keyrow_ref, qkvt_ref, probs_ref, att_ref, attt_ref, inv_ref, bias_ref
):
    head = pl.program_id(0)

    @pl.when(head == 0)
    def _():
        for w in range(windows):
            for part in range(12):
                rows = slice(part * 128, (part + 1) * 128)
                qkvt_ref[w, rows, :] = qkv_ref[w, :, rows].astype(F32).T.astype(BF16)

    for u in range(WIN_T):
        start = (WIN_T - 1 - u) * FLAT
        bias_ref[u * FLAT : (u + 1) * FLAT, :] = spread_ref[0, :, start : start + WIN]
    row = pl.multiple_of(head * HDIM, HDIM)
    ones = jnp.ones((16, WIN), BF16)
    for w in range(windows):
        queries = qkvt_ref[w, pl.ds(row, HDIM), :]
        keys = qkvt_ref[w, pl.ds(row + D, HDIM), :]
        values = qkvt_ref[w, pl.ds(row + 2 * D, HDIM), :]
        scores = dot_tn(
            jnp.concatenate([keys, keyrow_ref[w]], axis=0), jnp.concatenate([queries, ones], axis=0)
        )
        scores = scores + bias_ref[...]
        top = jnp.max(scores, axis=0, keepdims=True)
        expo = jnp.exp2(scores - top).astype(BF16)
        probs_ref[w, 0] = expo
        mixed = dot_nn(jnp.concatenate([values, ones], axis=0), expo)
        inverse = 1.0 / mixed[HDIM : HDIM + 1]
        inv_ref[w, pl.ds(head, 1), :] = inverse
        attt_ref[w, pl.ds(row, HDIM), :] = (mixed[:HDIM] * inverse).astype(BF16)

    @pl.when(head == HEADS - 1)
    def _():
        for w in range(windows):
            for part in range(4):
                rows = slice(part * 128, (part + 1) * 128)
                att_ref[w, :, rows] = attt_ref[w, rows, :].astype(F32).T.astype(BF16)


def attend(qkv, spread, keyrow):
    windows = qkv.shape[0]
    whole = lambda h: (0, 0, 0)
    return pl.pallas_call(
        functools.partial(attend_kernel, windows),
        grid=(HEADS,),
        in_specs=[
            pl.BlockSpec((windows, WIN, 3 * D), whole),
            pl.BlockSpec((1, FLAT, SPREAD), lambda h: (h, 0, 0)),
            pl.BlockSpec((windows, 16, WIN), whole),
        ],
        out_specs=[
            pl.BlockSpec((windows, 3 * D, WIN), whole),
            pl.BlockSpec((windows, 1, WIN, WIN), lambda h: (0, h, 0, 0)),
            pl.BlockSpec((windows, WIN, D), whole),
            pl.BlockSpec((windows, D, WIN), whole),
            pl.BlockSpec((windows, HEADS, WIN), whole),
        ],
        out_shape=[
            jax.ShapeDtypeStruct((windows, 3 * D, WIN), BF16),
            jax.ShapeDtypeStruct((windows, HEADS, WIN, WIN), BF16),
            jax.ShapeDtypeStruct((windows, WIN, D), BF16),
            jax.ShapeDtypeStruct((windows, D, WIN), BF16),
            jax.ShapeDtypeStruct((windows, HEADS, WIN), F32),
        ],
        scratch_shapes=[pltpu.VMEM((WIN, WIN), F32)],
        compiler_params=pltpu.CompilerParams(vmem_limit_bytes=60 * MIB),
        name="attend",
    )(qkv, spread, keyrow)


def mlp_kernel(
    x_ref,
    att_ref,
    cot_ref,
    keep_ref,
    proj_ref,
    pshift_ref,
    gain_ref,
    shift_ref,
    fc1_ref,
    fshift1_ref,
    fc2_ref,
    fshift2_ref,
    out_ref,
    rgrad_ref,
    agrad_ref,
    fc1g_ref,
    fc2g_ref,
    projg_ref,
    sums_ref,
    fsum_ref,
    act_ref,
    hid_ref,
    norm_ref,
    gout_ref,
    branch_ref,
):
    rows = x_ref.shape[0]
    block = rows // 2
    pieces = 4
    wide = FF // pieces
    sums_ref[...] = jnp.zeros_like(sums_ref)
    fsum_ref[...] = jnp.zeros_like(fsum_ref)

    def one_block(i, carry):
        at = pl.ds(pl.multiple_of(i * block, 16), block)
        keep = keep_ref[at, :]
        resid = x_ref[at, :].astype(F32) + dot_nn(att_ref[at, :], proj_ref[...]) + pshift_ref[...]
        unit, scale = standardize(resid)
        normed = (unit * gain_ref[...] + shift_ref[...]).astype(BF16)
        norm_ref[at, :] = normed
        gout = cot_ref[at, :].astype(F32) * keep
        gout_low = gout.astype(BF16)
        gout_ref[at, :] = gout_low
        total = resid + fshift2_ref[...]
        grad_two = None
        for part in range(pieces):
            columns = slice(part * wide, (part + 1) * wide)
            hidden = dot_nn(normed, fc1_ref[:, columns]) + fshift1_ref[:, columns]
            active, slope = gelu_parts(hidden)
            active = active.astype(BF16)
            act_ref[at, columns] = active
            total = total + dot_nn(active, fc2_ref[columns, :])
            hgrad = (dot_nt(gout_low, fc2_ref[columns, :]) * slope).astype(BF16)
            hid_ref[at, columns] = hgrad
            fsum_ref[0:1, columns] += jnp.sum(hgrad.astype(F32), axis=0, keepdims=True)
            back = dot_nt(hgrad, fc1_ref[:, columns])
            grad_two = back if grad_two is None else grad_two + back
        out_ref[at, :] = (total * keep).astype(BF16)
        rgrad = gout + norm_backward(grad_two, unit, scale, gain_ref[...])
        rgrad_ref[at, :] = rgrad
        branch = rgrad.astype(BF16)
        branch_ref[at, :] = branch
        agrad_ref[at, :] = dot_nt(branch, proj_ref[...]).astype(BF16)
        sums_ref[0:1, :] += jnp.sum(gout, axis=0, keepdims=True)
        sums_ref[1:2, :] += jnp.sum(grad_two * unit, axis=0, keepdims=True)
        sums_ref[2:3, :] += jnp.sum(grad_two, axis=0, keepdims=True)
        sums_ref[3:4, :] += jnp.sum(branch.astype(F32), axis=0, keepdims=True)
        return carry

    lax.fori_loop(0, 2, one_block, 0)
    projg_ref[...] = dot_tn(att_ref[...], branch_ref[...])
    for part in range(pieces):
        columns = slice(part * wide, (part + 1) * wide)
        fc2g_ref[columns, :] = dot_tn(act_ref[:, columns], gout_ref[...])
        fc1g_ref[:, columns] = dot_tn(norm_ref[...], hid_ref[:, columns])


def feed_forward(x_rows, att_rows, cot_rows, keep_rows, proj, pshift, gain, shift, fc1, fshift1, fc2, fshift2):
    rows = x_rows.shape[0]
    vmem = pl.BlockSpec(memory_space=pltpu.VMEM)
    return pl.pallas_call(
        mlp_kernel,
        in_specs=[vmem] * 12,
        out_specs=[vmem] * 8,
        out_shape=[
            jax.ShapeDtypeStruct((rows, D), BF16),
            jax.ShapeDtypeStruct((rows, D), F32),
            jax.ShapeDtypeStruct((rows, D), BF16),
            jax.ShapeDtypeStruct((D, FF), F32),
            jax.ShapeDtypeStruct((FF, D), F32),
            jax.ShapeDtypeStruct((D, D), F32),
            jax.ShapeDtypeStruct((8, D), F32),
            jax.ShapeDtypeStruct((8, FF), F32),
        ],
        scratch_shapes=[
            pltpu.VMEM((rows, FF), BF16),
            pltpu.VMEM((rows, FF), BF16),
            pltpu.VMEM((rows, D), BF16),
            pltpu.VMEM((rows, D), BF16),
            pltpu.VMEM((rows, D), BF16),
        ],
        compiler_params=pltpu.CompilerParams(vmem_limit_bytes=62 * MIB),
        name="feed_forward",
    )(x_rows, att_rows, cot_rows, keep_rows, proj, pshift, gain, shift, fc1, fshift1, fc2, fshift2)


def attend_back_kernel(
    windows,
    qkvt_ref,
    attt_ref,
    agrad_ref,
    inv_ref,
    probs_ref,
    dqkv_ref,
    fold_ref,
    dot_ref,
    dqkvt_ref,
    sum_ref,
    wide_ref,
):
    head = pl.program_id(0)

    @pl.when(head == 0)
    def _():
        for w in range(windows):
            for part in range(4):
                rows = slice(part * 128, (part + 1) * 128)
                dot_ref[w, rows, :] = agrad_ref[w, :, rows].astype(F32).T.astype(BF16)

    row = pl.multiple_of(head * HDIM, HDIM)
    ones = jnp.ones((16, WIN), BF16)
    place = lax.broadcasted_iota(jnp.int32, (16, WIN), 0)
    for w in range(windows):
        queries = qkvt_ref[w, pl.ds(row, HDIM), :]
        keys = qkvt_ref[w, pl.ds(row + D, HDIM), :]
        values = qkvt_ref[w, pl.ds(row + 2 * D, HDIM), :]
        expo = probs_ref[w, 0]
        grad = dot_ref[w, pl.ds(row, HDIM), :].astype(F32) * inv_ref[w, pl.ds(head, 1), :]
        inner = -jnp.sum(grad * attt_ref[w, pl.ds(row, HDIM), :].astype(F32), axis=0, keepdims=True)
        high = inner.astype(BF16).astype(F32)
        middle = (inner - high).astype(BF16).astype(F32)
        lowest = inner - high - middle
        extra = jnp.where(
            place == 0, high, jnp.where(place == 1, middle, jnp.where(place == 2, lowest, 0.0))
        ).astype(BF16)
        grad = grad.astype(BF16)
        probs_grad = dot_tn(
            jnp.concatenate([values, ones], axis=0), jnp.concatenate([grad, extra], axis=0)
        )
        scores_grad = expo.astype(F32) * probs_grad
        low = scores_grad.astype(BF16)
        if w == 0:
            sum_ref[...] = scores_grad
        else:
            sum_ref[...] += scores_grad
        dqkvt_ref[w, pl.ds(row, HDIM), :] = (dot_nn(keys, low) * SCALE).astype(BF16)
        dqkvt_ref[w, pl.ds(row + D, HDIM), :] = (dot_nt(queries, low) * LN2).astype(BF16)
        dqkvt_ref[w, pl.ds(row + 2 * D, HDIM), :] = dot_nt(grad, expo).astype(BF16)

    wide_ref[...] = jnp.zeros_like(wide_ref)
    for u in range(WIN_T):
        start = (WIN_T - 1 - u) * FLAT
        wide_ref[:, start : start + WIN] += sum_ref[u * FLAT : (u + 1) * FLAT, :]
    fold_ref[0] = wide_ref[...]

    @pl.when(head == HEADS - 1)
    def _():
        for w in range(windows):
            for part in range(12):
                rows = slice(part * 128, (part + 1) * 128)
                dqkv_ref[w, :, rows] = dqkvt_ref[w, rows, :].astype(F32).T.astype(BF16)


def attend_back(qkvt, attt, agrad, inverse, probs):
    windows = qkvt.shape[0]
    whole = lambda h: (0, 0, 0)
    return pl.pallas_call(
        functools.partial(attend_back_kernel, windows),
        grid=(HEADS,),
        in_specs=[
            pl.BlockSpec((windows, 3 * D, WIN), whole, pipeline_mode=pl.Buffered(1)),
            pl.BlockSpec((windows, D, WIN), whole, pipeline_mode=pl.Buffered(1)),
            pl.BlockSpec((windows, WIN, D), whole, pipeline_mode=pl.Buffered(1)),
            pl.BlockSpec((windows, HEADS, WIN), whole),
            pl.BlockSpec((windows, 1, WIN, WIN), lambda h: (0, h, 0, 0)),
        ],
        out_specs=[
            pl.BlockSpec((windows, WIN, 3 * D), whole),
            pl.BlockSpec((1, FLAT, SPREAD), lambda h: (h, 0, 0)),
        ],
        out_shape=[
            jax.ShapeDtypeStruct((windows, WIN, 3 * D), BF16),
            jax.ShapeDtypeStruct((HEADS, FLAT, SPREAD), F32),
        ],
        scratch_shapes=[
            pltpu.VMEM((windows, D, WIN), BF16),
            pltpu.VMEM((windows, 3 * D, WIN), BF16),
            pltpu.VMEM((WIN, WIN), F32),
            pltpu.VMEM((FLAT, SPREAD), F32),
        ],
        compiler_params=pltpu.CompilerParams(vmem_limit_bytes=62 * MIB),
        name="attend_back",
    )(qkvt, attt, agrad, inverse, probs)


def qkv_back_kernel(
    x_ref, dqkv_ref, rgrad_ref, gain_ref, shift_ref, weight_ref, igrad_ref, wgrad_ref, sums_ref, norm_ref
):
    rows = x_ref.shape[0]
    block = rows // 2
    sums_ref[...] = jnp.zeros_like(sums_ref)

    def one_block(i, carry):
        at = pl.ds(pl.multiple_of(i * block, 16), block)
        unit, scale = standardize(x_ref[at, :].astype(F32))
        norm_ref[at, :] = (unit * gain_ref[...] + shift_ref[...]).astype(BF16)
        back = dot_nt(dqkv_ref[at, :], weight_ref[...])
        igrad_ref[at, :] = (rgrad_ref[at, :] + norm_backward(back, unit, scale, gain_ref[...])).astype(BF16)
        sums_ref[0:1, :D] += jnp.sum(back * unit, axis=0, keepdims=True)
        sums_ref[1:2, :D] += jnp.sum(back, axis=0, keepdims=True)
        sums_ref[2:3, :] += jnp.sum(dqkv_ref[at, :].astype(F32), axis=0, keepdims=True)
        return carry

    lax.fori_loop(0, 2, one_block, 0)
    for part in range(3):
        columns = slice(part * D, (part + 1) * D)
        wgrad_ref[:, columns] = dot_tn(norm_ref[...], dqkv_ref[:, columns])


def qkv_back(x_rows, dqkv_rows, rgrad, gain, shift, weight):
    rows = x_rows.shape[0]
    vmem = pl.BlockSpec(memory_space=pltpu.VMEM)
    return pl.pallas_call(
        qkv_back_kernel,
        in_specs=[vmem] * 6,
        out_specs=[vmem] * 3,
        out_shape=[
            jax.ShapeDtypeStruct((rows, D), BF16),
            jax.ShapeDtypeStruct((D, 3 * D), F32),
            jax.ShapeDtypeStruct((8, 3 * D), F32),
        ],
        scratch_shapes=[pltpu.VMEM((rows, D), BF16)],
        compiler_params=pltpu.CompilerParams(vmem_limit_bytes=62 * MIB),
        name="qkv_back",
    )(x_rows, dqkv_rows, rgrad, gain, shift, weight)


def offset_choice():
    spots = np.arange(FLAT)
    rows, columns = spots // WIN_W, spots % WIN_W
    index = (rows[None, :] - rows[:, None] + WIN_H - 1) * OFFS_W + (
        columns[None, :] - columns[:, None] + WIN_W - 1
    )
    return jnp.asarray(index.reshape(1, -1)) == jnp.arange(OFFS_H * OFFS_W)[:, None]


def spread_table(bias_table):
    table = bias_table.reshape(OFFS_T, OFFS_H * OFFS_W, HEADS)
    table = jnp.transpose(table, (2, 0, 1)).reshape(HEADS * OFFS_T, OFFS_H * OFFS_W)
    wide = dot_nn(table, offset_choice().astype(BF16)) * LOG2E
    wide = wide.reshape(HEADS, OFFS_T, FLAT, FLAT)
    return jnp.transpose(wide, (0, 2, 1, 3)).reshape(HEADS, FLAT, SPREAD)


def fold_table(spread_grad):
    wide = spread_grad.reshape(HEADS, FLAT, OFFS_T, FLAT)
    wide = jnp.transpose(wide, (0, 2, 1, 3)).reshape(HEADS * OFFS_T, FLAT * FLAT)
    table = lax.dot_general(
        wide,
        offset_choice().astype(F32),
        (((1,), (1,)), ((), ())),
        precision=lax.Precision.HIGHEST,
        preferred_element_type=F32,
    )
    table = table.reshape(HEADS, OFFS_T, OFFS_H * OFFS_W)
    return jnp.transpose(table, (1, 2, 0)).reshape(-1, HEADS)


def valid_mask(extents):
    spots = np.arange(WIN)
    depth, height, across = spots // FLAT, spots // WIN_W % WIN_H, spots % WIN_W
    return (
        (depth[None, :] < extents[:, 0:1])
        & (height[None, :] < extents[:, 1:2])
        & (across[None, :] < extents[:, 2:3])
    ).astype(F32)


def gathered(value):
    return lax.all_gather(value, AXES, axis=0, tiled=True)


def scattered(value):
    return lax.psum_scatter(value, AXES, scatter_dimension=0, tiled=True)


def per_device(
    inputs,
    extents,
    cotangent,
    ln1_gain,
    ln1_shift,
    qkv_weight,
    query_bias,
    value_bias,
    bias_table,
    proj_weight,
    proj_shift,
    ln2_gain,
    ln2_shift,
    fc1_weight,
    fc1_shift,
    fc2_weight,
    fc2_shift,
):
    windows = inputs.shape[0]
    rows = windows * WIN
    qkv_full = gathered(qkv_weight)
    proj_full = gathered(proj_weight)
    fc1_full = gathered(fc1_weight)
    fc2_full = gathered(fc2_weight)
    shards = (
        ln1_gain,
        ln1_shift,
        query_bias,
        value_bias,
        proj_shift,
        ln2_gain,
        ln2_shift,
        fc2_shift,
    )
    small = ln1_gain.shape[0]
    packed = lax.all_gather(jnp.concatenate(shards + (fc1_shift,)), AXES, axis=0)
    vectors = [
        packed[:, i * small : (i + 1) * small].reshape(1, D).astype(F32) for i in range(len(shards))
    ]
    gain1, shift1, qbias, vbias, pshift, gain2, shift2, fshift2 = vectors
    fshift1 = packed[:, len(shards) * small :].reshape(1, FF).astype(F32)
    qkv_bias = jnp.concatenate([qbias, jnp.zeros_like(qbias), vbias], axis=1)

    keep = valid_mask(extents)
    keep_rows = keep.reshape(rows, 1)
    keyrow = jnp.concatenate(
        [((keep - 1.0) * 1e30)[:, None, :], jnp.zeros((windows, 15, WIN), F32)], axis=1
    ).astype(BF16)
    spread = spread_table(bias_table)

    x_rows = inputs.reshape(rows, D)
    qkv = project_qkv(x_rows, gain1, shift1, qkv_full, qkv_bias)
    qkvt, probs, att, attt, inverse = attend(qkv.reshape(windows, WIN, 3 * D), spread, keyrow)
    output, rgrad, agrad, fc1_grad, fc2_grad, proj_grad, sums, fsum = feed_forward(
        x_rows,
        att.reshape(rows, D),
        cotangent.reshape(rows, D),
        keep_rows,
        proj_full,
        pshift,
        gain2,
        shift2,
        fc1_full,
        fshift1,
        fc2_full,
        fshift2,
    )
    dqkv, spread_grad = attend_back(qkvt, attt, agrad.reshape(windows, WIN, D), inverse, probs)
    input_grad, qkv_grad, qsums = qkv_back(
        x_rows, dqkv.reshape(rows, 3 * D), rgrad, gain1, shift1, qkv_full
    )
    table_grad = lax.psum(fold_table(spread_grad), AXES)
    count = D // small
    vector_grads = jnp.concatenate(
        [
            item.reshape(count, -1)
            for item in (
                qsums[0, :D],
                qsums[1, :D],
                qsums[2, :D],
                qsums[2, 2 * D :],
                sums[3],
                sums[1],
                sums[2],
                sums[0],
                fsum[0],
            )
        ],
        axis=1,
    )
    vector_grads = scattered(vector_grads).reshape(-1)
    owned = [vector_grads[i * small : (i + 1) * small] for i in range(8)]
    return (
        output.reshape(inputs.shape),
        input_grad.reshape(inputs.shape),
        owned[0],
        owned[1],
        scattered(qkv_grad),
        owned[2],
        owned[3],
        table_grad,
        scattered(proj_grad),
        owned[4],
        owned[5],
        owned[6],
        scattered(fc1_grad),
        vector_grads[8 * small :],
        scattered(fc2_grad),
        owned[7],
    )


def solution(mesh):
    rows = P(AXES, None)
    vector = P(AXES)
    block = P(AXES, None, None)
    in_specs = (
        block,
        rows,
        block,
        vector,
        vector,
        rows,
        vector,
        vector,
        P(),
        rows,
        vector,
        vector,
        vector,
        rows,
        vector,
        rows,
        vector,
    )
    out_specs = (
        block,
        block,
        vector,
        vector,
        rows,
        vector,
        vector,
        P(),
        rows,
        vector,
        vector,
        vector,
        rows,
        vector,
        rows,
        vector,
    )
    return jax.shard_map(
        per_device, mesh=mesh, in_specs=in_specs, out_specs=out_specs, check_vma=False
    )
```

```python
import functools
import math

import jax
import jax.numpy as jnp
import numpy as np
from jax import lax
from jax.experimental import pallas as pl
from jax.experimental.pallas import tpu as pltpu
from jax.sharding import PartitionSpec as P

D = 512
HEADS = 16
HDIM = 32
FF = 2048
WIN_T = 8
WIN_H = 7
WIN_W = 7
WIN = WIN_T * WIN_H * WIN_W
FLAT = WIN_H * WIN_W
OFFS_T = 2 * WIN_T - 1
OFFS_H = 2 * WIN_H - 1
OFFS_W = 2 * WIN_W - 1
SPREAD = OFFS_T * FLAT
EPS = 1e-05
LOG2E = math.log2(math.e)
LN2 = math.log(2.0)
SCALE = HDIM ** (-0.5)
AXES = ("dp", "fsdp")
BF16 = jnp.bfloat16
F32 = jnp.float32
MIB = 2**20


def dot(left, right, left_dim, right_dim):
    return lax.dot_general(
        left, right, (((left_dim,), (right_dim,)), ((), ())), preferred_element_type=F32
    )


def dot_nn(left, right):
    return dot(left, right, 1, 0)


def dot_nt(left, right):
    return dot(left, right, 1, 1)


def dot_tn(left, right):
    return dot(left, right, 0, 0)


def standardize(rows):
    average = jnp.mean(rows, axis=-1, keepdims=True)
    centered = rows - average
    variance = jnp.mean(centered * centered, axis=-1, keepdims=True)
    scale = lax.rsqrt(variance + EPS)
    return centered * scale, scale


def norm_backward(grad, unit, scale, gain):
    scaled = grad * gain
    first = jnp.mean(scaled, axis=-1, keepdims=True)
    second = jnp.mean(scaled * unit, axis=-1, keepdims=True)
    return (scaled - first - unit * second) * scale


def gelu_parts(hidden):
    reach = jnp.abs(hidden) * (0.5**0.5)
    ratio = 1.0 / (1.0 + 0.3275911 * reach)
    series = 1.061405429 * ratio - 1.453152027
    series = series * ratio + 1.421413741
    series = series * ratio - 0.284496736
    series = series * ratio + 0.254829592
    bell = jnp.exp(-0.5 * hidden * hidden)
    tail = (0.5 * series) * (ratio * bell)
    below = jnp.where(hidden < 0, tail, 1.0 - tail)
    return hidden * below, below + hidden * bell * (1.0 / math.sqrt(2 * math.pi))


class Place:
    def __init__(self, depth):
        dp, fsdp = lax.axis_index("dp"), lax.axis_index("fsdp")
        self.depth = depth
        self.y, self.c = dp // 2, dp % 2
        self.z, self.x = fsdp // 2, fsdp % 2
        self.core = (self.y * 2 + 1 - self.c, fsdp)
        self.across_x = (dp, self.z * 2 + 1 - self.x)
        self.across_y = ((1 - self.y) * 2 + self.c, fsdp)
        self.along_z = [(dp, ((self.z + j) % depth) * 2 + self.x) for j in range(1, depth)]

    def greet(self):
        barrier = pltpu.get_barrier_semaphore()
        partners = [self.core, self.across_x, self.across_y] + self.along_z
        for partner in partners:
            pl.semaphore_signal(barrier, inc=1, device_id=partner, device_id_type=pl.DeviceIdType.MESH)
        pl.semaphore_wait(barrier, len(partners))


def send(source, target, sems, slot, device):
    return pltpu.make_async_remote_copy(
        src_ref=source,
        dst_ref=target,
        send_sem=sems[0].at[slot],
        recv_sem=sems[1].at[slot],
        device_id=device,
        device_id_type=pl.DeviceIdType.MESH,
    )


def gather_slots(depth):
    return depth + 5


def gather_stages(place, own, full, sems, base, y_first):
    y, c, z, x, depth = place.y, place.c, place.z, place.x, place.depth
    every = slice(None)
    here = full(y, c, z, x)
    local = pltpu.make_async_copy(own, here, sems[0].at[base])
    along = [send(own, here, sems, base + j, place.along_z[j - 1]) for j in range(1, depth)]
    column = full(y, c, every, x)
    if y_first:
        first = send(column, column, sems, base + depth, place.across_y)
        both = full(every, c, every, x)
        second = send(both, both, sems, base + depth + 1, place.across_x)
        one = full(1 - y, c, every, x)
        two = full(every, c, every, 1 - x)
    else:
        first = send(column, column, sems, base + depth, place.across_x)
        both = full(y, c, every, every)
        second = send(both, both, sems, base + depth + 1, place.across_y)
        one = full(y, c, every, 1 - x)
        two = full(1 - y, c, every, every)
    shares = [
        send(part, part, sems, base + depth + 2 + k, place.core) for k, part in enumerate((column, one, two))
    ]

    def begin():
        local.start()
        for copy in along:
            copy.start()

    def turn():
        local.wait()
        for copy in along:
            copy.wait_recv()
        first.start()
        shares[0].start()

    def cross():
        first.wait_recv()
        second.start()
        shares[1].start()

    def share():
        second.wait_recv()
        shares[2].start()

    def finish():
        for copy in shares:
            copy.wait()
        for copy in along + [first, second]:
            copy.wait_send()

    return [begin, turn, cross, share, finish]


def scatter_slots(depth):
    return depth + 2


def add_into(target, index, extra):
    target[index] = (target[index].astype(F32) + extra.astype(F32)).astype(target.dtype)


def scatter_stages(place, parts, held, sems, base, x_first, result):
    y, c, z, x, depth = place.y, place.c, place.z, place.x, place.depth
    every = slice(None)
    from_core, from_first, from_second, from_z = held
    share = send(parts.at[:, 1 - c], from_core, sems, base, place.core)
    if x_first:
        first = send(parts.at[:, c, :, 1 - x], from_first, sems, base + 1, place.across_x)
        second = send(parts.at[1 - y, c, :, x], from_second, sems, base + 2, place.across_y)
    else:
        first = send(parts.at[1 - y, c], from_first, sems, base + 1, place.across_y)
        second = send(parts.at[y, c, :, 1 - x], from_second, sems, base + 2, place.across_x)
    along = [
        send(
            parts.at[y, c, (z + j) % depth, x],
            from_z.at[j - 1],
            sems,
            base + 2 + j,
            place.along_z[j - 1],
        )
        for j in range(1, depth)
    ]

    def begin():
        share.start()

    def cross():
        share.wait_recv()
        for yy in range(2):
            add_into(parts, (yy, c), from_core[yy])
        first.start()

    def turn():
        first.wait_recv()
        if x_first:
            for yy in range(2):
                for zz in range(depth):
                    add_into(parts, (yy, c, zz, x), from_first[yy, zz])
        else:
            add_into(parts, (y, c), from_first[...])
        second.start()

    def spread():
        second.wait_recv()
        for zz in range(depth):
            add_into(parts, (y, c, zz, x), from_second[zz])
        for copy in along:
            copy.start()

    def finish():
        for copy in along:
            copy.wait_recv()
        total = parts[y, c, z, x].astype(F32)
        for j in range(depth - 1):
            total = total + from_z[j].astype(F32)
        result[...] = total
        for copy in along + [share, first, second]:
            copy.wait_send()

    return [begin, cross, turn, spread, finish]


def held_shapes(depth, rows, columns, dtype, x_first):
    first = (2, depth, rows, columns) if x_first else (depth, 2, rows, columns)
    return [
        pltpu.VMEM((2, depth, 2, rows, columns), dtype),
        pltpu.VMEM(first, dtype),
        pltpu.VMEM((depth, rows, columns), dtype),
        pltpu.VMEM((depth - 1, rows, columns), dtype),
    ]


def in_turn(lists):
    for stage in zip(*lists):
        for step in stage:
            step()


def gather_kernel(depth, plan, *refs):
    count = len(plan)
    shards, wholes, sems = refs[:count], refs[count : 2 * count], refs[2 * count :]
    place = Place(depth)
    place.greet()
    lists, base = [], 0
    for shard, whole, cuts in zip(shards, wholes, plan):
        for start, size, y_first in cuts:
            columns = pl.ds(start, size)
            view = lambda y, c, z, x, whole=whole, columns=columns: whole.at[y, c, z, x, :, columns]
            lists.append(gather_stages(place, shard.at[:, columns], view, sems, base, y_first))
            base += gather_slots(depth)
    in_turn(lists)


def gather_all(depth, shards, plan):
    slots = gather_slots(depth) * sum(len(cuts) for cuts in plan)
    anywhere = pl.BlockSpec(memory_space=pl.ANY)
    wholes = pl.pallas_call(
        functools.partial(gather_kernel, depth, plan),
        in_specs=[anywhere] * len(shards),
        out_specs=[anywhere] * len(shards),
        out_shape=[jax.ShapeDtypeStruct((2, 2, depth, 2) + s.shape, s.dtype) for s in shards],
        scratch_shapes=[pltpu.SemaphoreType.DMA((slots,)), pltpu.SemaphoreType.DMA((slots,))],
        compiler_params=pltpu.CompilerParams(collective_id=0, has_side_effects=True),
        name="gather_weights",
    )(*shards)
    return [whole.reshape(-1, whole.shape[-1]) for whole in wholes]


def scatter_kernel(depth, plan, *refs):
    count = len(plan)
    parts, outs, full = refs[:count], refs[count : 2 * count], refs[2 * count]
    works = refs[2 * count + 1 : 3 * count + 1]
    helds, sems = refs[3 * count + 1 : -2], refs[-2:]
    place = Place(depth)
    loads = []
    for i in range(count):
        loads.append(pltpu.make_async_copy(parts[i], works[i], sems[0].at[i]))
        loads[-1].start()
    place.greet()
    for load in loads:
        load.wait()
    lists, base, at = [], count, 0
    for work, out, cuts in zip(works, outs, plan):
        for start, size, x_first in cuts:
            columns = pl.ds(start, size)
            lists.append(
                scatter_stages(
                    place,
                    work.at[:, :, :, :, :, columns],
                    helds[at : at + 4],
                    sems,
                    base,
                    x_first,
                    out.at[:, columns],
                )
            )
            base += scatter_slots(depth)
            at += 4
    in_turn(lists)
    view = lambda y, c, z, x: full.at[y, c, z, x]
    in_turn([gather_stages(place, outs[0], view, sems, base, False)])


def scatter_all(depth, parts, plan):
    slots = len(parts) + scatter_slots(depth) * sum(len(cuts) for cuts in plan) + gather_slots(depth)
    vmem = pl.BlockSpec(memory_space=pltpu.VMEM)
    shapes = [pltpu.VMEM(part.shape, part.dtype) for part in parts]
    for part, cuts in zip(parts, plan):
        for _, size, x_first in cuts:
            shapes += held_shapes(depth, part.shape[-2], size, part.dtype, x_first)
    return pl.pallas_call(
        functools.partial(scatter_kernel, depth, plan),
        in_specs=[pl.BlockSpec(memory_space=pl.ANY)] * len(parts),
        out_specs=[vmem] * (len(parts) + 1),
        out_shape=[jax.ShapeDtypeStruct(part.shape[-2:], F32) for part in parts]
        + [jax.ShapeDtypeStruct(parts[0].shape, F32)],
        scratch_shapes=shapes + [pltpu.SemaphoreType.DMA((slots,)), pltpu.SemaphoreType.DMA((slots,))],
        compiler_params=pltpu.CompilerParams(
            collective_id=1, has_side_effects=True, vmem_limit_bytes=60 * MIB
        ),
        name="scatter_gradients",
    )(*parts)


def qkv_kernel(x_ref, gain_ref, shift_ref, weight_ref, bias_ref, out_ref):
    unit, _ = standardize(x_ref[...].astype(F32))
    normed = (unit * gain_ref[...] + shift_ref[...]).astype(BF16)
    for part in range(3):
        columns = slice(part * D, (part + 1) * D)
        got = dot_nn(normed, weight_ref[:, columns]) + bias_ref[:, columns]
        if part == 0:
            got = got * (SCALE * LOG2E)
        out_ref[:, columns] = got.astype(BF16)


def project_qkv(x_rows, gain, shift, weight, bias):
    rows = x_rows.shape[0]
    block = rows // 2
    whole = lambda i: (0, 0)
    return pl.pallas_call(
        qkv_kernel,
        grid=(2,),
        in_specs=[
            pl.BlockSpec((block, D), lambda i: (i, 0)),
            pl.BlockSpec((1, D), whole),
            pl.BlockSpec((1, D), whole),
            pl.BlockSpec((D, 3 * D), whole),
            pl.BlockSpec((1, 3 * D), whole),
        ],
        out_specs=pl.BlockSpec((block, 3 * D), lambda i: (i, 0)),
        out_shape=jax.ShapeDtypeStruct((rows, 3 * D), BF16),
        compiler_params=pltpu.CompilerParams(vmem_limit_bytes=48 * MIB),
        name="norm_qkv",
    )(x_rows, gain, shift, weight, bias)


def attend_kernel(
    windows, qkv_ref, spread_ref, keyrow_ref, qkvt_ref, probs_ref, att_ref, attt_ref, inv_ref, bias_ref
):
    head = pl.program_id(0)

    @pl.when(head == 0)
    def _():
        for w in range(windows):
            for part in range(12):
                rows = slice(part * 128, (part + 1) * 128)
                qkvt_ref[w, rows, :] = qkv_ref[w, :, rows].astype(F32).T.astype(BF16)

    for u in range(WIN_T):
        start = (WIN_T - 1 - u) * FLAT
        bias_ref[u * FLAT : (u + 1) * FLAT, :] = spread_ref[0, :, start : start + WIN]
    row = pl.multiple_of(head * HDIM, HDIM)
    ones = jnp.ones((16, WIN), BF16)
    for w in range(windows):
        queries = qkvt_ref[w, pl.ds(row, HDIM), :]
        keys = qkvt_ref[w, pl.ds(row + D, HDIM), :]
        values = qkvt_ref[w, pl.ds(row + 2 * D, HDIM), :]
        scores = dot_tn(
            jnp.concatenate([keys, keyrow_ref[w]], axis=0), jnp.concatenate([queries, ones], axis=0)
        )
        scores = scores + bias_ref[...]
        top = jnp.max(scores, axis=0, keepdims=True)
        expo = jnp.exp2(scores - top).astype(BF16)
        probs_ref[w, 0] = expo
        mixed = dot_nn(jnp.concatenate([values, ones], axis=0), expo)
        inverse = 1.0 / mixed[HDIM : HDIM + 1]
        inv_ref[w, pl.ds(head, 1), :] = inverse
        attt_ref[w, pl.ds(row, HDIM), :] = (mixed[:HDIM] * inverse).astype(BF16)

    @pl.when(head == HEADS - 1)
    def _():
        for w in range(windows):
            for part in range(4):
                rows = slice(part * 128, (part + 1) * 128)
                att_ref[w, :, rows] = attt_ref[w, rows, :].astype(F32).T.astype(BF16)


def attend(qkv, spread, keyrow):
    windows = qkv.shape[0]
    whole = lambda h: (0, 0, 0)
    return pl.pallas_call(
        functools.partial(attend_kernel, windows),
        grid=(HEADS,),
        in_specs=[
            pl.BlockSpec((windows, WIN, 3 * D), whole),
            pl.BlockSpec((1, FLAT, SPREAD), lambda h: (h, 0, 0)),
            pl.BlockSpec((windows, 16, WIN), whole),
        ],
        out_specs=[
            pl.BlockSpec((windows, 3 * D, WIN), whole),
            pl.BlockSpec((windows, 1, WIN, WIN), lambda h: (0, h, 0, 0)),
            pl.BlockSpec((windows, WIN, D), whole),
            pl.BlockSpec((windows, D, WIN), whole),
            pl.BlockSpec((windows, HEADS, WIN), whole),
        ],
        out_shape=[
            jax.ShapeDtypeStruct((windows, 3 * D, WIN), BF16),
            jax.ShapeDtypeStruct((windows, HEADS, WIN, WIN), BF16),
            jax.ShapeDtypeStruct((windows, WIN, D), BF16),
            jax.ShapeDtypeStruct((windows, D, WIN), BF16),
            jax.ShapeDtypeStruct((windows, HEADS, WIN), F32),
        ],
        scratch_shapes=[pltpu.VMEM((WIN, WIN), F32)],
        compiler_params=pltpu.CompilerParams(vmem_limit_bytes=60 * MIB),
        name="attend",
    )(qkv, spread, keyrow)


def mlp_kernel(
    x_ref,
    att_ref,
    cot_ref,
    keep_ref,
    proj_ref,
    pshift_ref,
    gain_ref,
    shift_ref,
    fc1_ref,
    fshift1_ref,
    fc2_ref,
    fshift2_ref,
    out_ref,
    rgrad_ref,
    agrad_ref,
    fc1g_ref,
    fc2g_ref,
    projg_ref,
    sums_ref,
    fsum_ref,
    act_ref,
    hid_ref,
    norm_ref,
    gout_ref,
    branch_ref,
):
    rows = x_ref.shape[0]
    block = rows // 2
    pieces = 4
    wide = FF // pieces
    sums_ref[...] = jnp.zeros_like(sums_ref)
    fsum_ref[...] = jnp.zeros_like(fsum_ref)

    def one_block(i, carry):
        at = pl.ds(pl.multiple_of(i * block, 16), block)
        keep = keep_ref[at, :]
        resid = x_ref[at, :].astype(F32) + dot_nn(att_ref[at, :], proj_ref[...]) + pshift_ref[...]
        unit, scale = standardize(resid)
        normed = (unit * gain_ref[...] + shift_ref[...]).astype(BF16)
        norm_ref[at, :] = normed
        gout = cot_ref[at, :].astype(F32) * keep
        gout_low = gout.astype(BF16)
        gout_ref[at, :] = gout_low
        total = resid + fshift2_ref[...]
        grad_two = None
        for part in range(pieces):
            columns = slice(part * wide, (part + 1) * wide)
            hidden = dot_nn(normed, fc1_ref[:, columns]) + fshift1_ref[:, columns]
            active, slope = gelu_parts(hidden)
            active = active.astype(BF16)
            act_ref[at, columns] = active
            total = total + dot_nn(active, fc2_ref[columns, :])
            hgrad = (dot_nt(gout_low, fc2_ref[columns, :]) * slope).astype(BF16)
            hid_ref[at, columns] = hgrad
            fsum_ref[0:1, columns] += jnp.sum(hgrad.astype(F32), axis=0, keepdims=True)
            back = dot_nt(hgrad, fc1_ref[:, columns])
            grad_two = back if grad_two is None else grad_two + back
        out_ref[at, :] = (total * keep).astype(BF16)
        rgrad = gout + norm_backward(grad_two, unit, scale, gain_ref[...])
        rgrad_ref[at, :] = rgrad
        branch = rgrad.astype(BF16)
        branch_ref[at, :] = branch
        agrad_ref[at, :] = dot_nt(branch, proj_ref[...]).astype(BF16)
        sums_ref[0:1, :] += jnp.sum(gout, axis=0, keepdims=True)
        sums_ref[1:2, :] += jnp.sum(grad_two * unit, axis=0, keepdims=True)
        sums_ref[2:3, :] += jnp.sum(grad_two, axis=0, keepdims=True)
        sums_ref[3:4, :] += jnp.sum(branch.astype(F32), axis=0, keepdims=True)
        return carry

    lax.fori_loop(0, 2, one_block, 0)
    projg_ref[...] = dot_tn(att_ref[...], branch_ref[...]).astype(BF16)
    for part in range(pieces):
        columns = slice(part * wide, (part + 1) * wide)
        fc2g_ref[columns, :] = dot_tn(act_ref[:, columns], gout_ref[...]).astype(BF16)
        fc1g_ref[:, columns] = dot_tn(norm_ref[...], hid_ref[:, columns]).astype(BF16)


def feed_forward(x_rows, att_rows, cot_rows, keep_rows, proj, pshift, gain, shift, fc1, fshift1, fc2, fshift2):
    rows = x_rows.shape[0]
    vmem = pl.BlockSpec(memory_space=pltpu.VMEM)
    return pl.pallas_call(
        mlp_kernel,
        in_specs=[vmem] * 12,
        out_specs=[vmem] * 8,
        out_shape=[
            jax.ShapeDtypeStruct((rows, D), BF16),
            jax.ShapeDtypeStruct((rows, D), F32),
            jax.ShapeDtypeStruct((rows, D), BF16),
            jax.ShapeDtypeStruct((D, FF), BF16),
            jax.ShapeDtypeStruct((FF, D), BF16),
            jax.ShapeDtypeStruct((D, D), BF16),
            jax.ShapeDtypeStruct((8, D), F32),
            jax.ShapeDtypeStruct((8, FF), F32),
        ],
        scratch_shapes=[
            pltpu.VMEM((rows, FF), BF16),
            pltpu.VMEM((rows, FF), BF16),
            pltpu.VMEM((rows, D), BF16),
            pltpu.VMEM((rows, D), BF16),
            pltpu.VMEM((rows, D), BF16),
        ],
        compiler_params=pltpu.CompilerParams(vmem_limit_bytes=62 * MIB),
        name="feed_forward",
    )(x_rows, att_rows, cot_rows, keep_rows, proj, pshift, gain, shift, fc1, fshift1, fc2, fshift2)


def attend_back_kernel(
    windows,
    qkvt_ref,
    attt_ref,
    agrad_ref,
    inv_ref,
    probs_ref,
    dqkv_ref,
    fold_ref,
    dot_ref,
    dqkvt_ref,
    sum_ref,
    wide_ref,
):
    head = pl.program_id(0)

    @pl.when(head == 0)
    def _():
        for w in range(windows):
            for part in range(4):
                rows = slice(part * 128, (part + 1) * 128)
                dot_ref[w, rows, :] = agrad_ref[w, :, rows].astype(F32).T.astype(BF16)

    row = pl.multiple_of(head * HDIM, HDIM)
    ones = jnp.ones((16, WIN), BF16)
    place = lax.broadcasted_iota(jnp.int32, (16, WIN), 0)
    for w in range(windows):
        queries = qkvt_ref[w, pl.ds(row, HDIM), :]
        keys = qkvt_ref[w, pl.ds(row + D, HDIM), :]
        values = qkvt_ref[w, pl.ds(row + 2 * D, HDIM), :]
        expo = probs_ref[w, 0]
        grad = dot_ref[w, pl.ds(row, HDIM), :].astype(F32) * inv_ref[w, pl.ds(head, 1), :]
        inner = -jnp.sum(grad * attt_ref[w, pl.ds(row, HDIM), :].astype(F32), axis=0, keepdims=True)
        high = inner.astype(BF16).astype(F32)
        middle = (inner - high).astype(BF16).astype(F32)
        lowest = inner - high - middle
        extra = jnp.where(
            place == 0, high, jnp.where(place == 1, middle, jnp.where(place == 2, lowest, 0.0))
        ).astype(BF16)
        grad = grad.astype(BF16)
        probs_grad = dot_tn(
            jnp.concatenate([values, ones], axis=0), jnp.concatenate([grad, extra], axis=0)
        )
        scores_grad = expo.astype(F32) * probs_grad
        low = scores_grad.astype(BF16)
        if w == 0:
            sum_ref[...] = scores_grad
        else:
            sum_ref[...] += scores_grad
        dqkvt_ref[w, pl.ds(row, HDIM), :] = (dot_nn(keys, low) * SCALE).astype(BF16)
        dqkvt_ref[w, pl.ds(row + D, HDIM), :] = (dot_nt(queries, low) * LN2).astype(BF16)
        dqkvt_ref[w, pl.ds(row + 2 * D, HDIM), :] = dot_nt(grad, expo).astype(BF16)

    wide_ref[...] = jnp.zeros_like(wide_ref)
    for u in range(WIN_T):
        start = (WIN_T - 1 - u) * FLAT
        wide_ref[:, start : start + WIN] += sum_ref[u * FLAT : (u + 1) * FLAT, :]
    fold_ref[0] = wide_ref[...]

    @pl.when(head == HEADS - 1)
    def _():
        for w in range(windows):
            for part in range(12):
                rows = slice(part * 128, (part + 1) * 128)
                dqkv_ref[w, :, rows] = dqkvt_ref[w, rows, :].astype(F32).T.astype(BF16)


def attend_back(qkvt, attt, agrad, inverse, probs):
    windows = qkvt.shape[0]
    whole = lambda h: (0, 0, 0)
    return pl.pallas_call(
        functools.partial(attend_back_kernel, windows),
        grid=(HEADS,),
        in_specs=[
            pl.BlockSpec((windows, 3 * D, WIN), whole, pipeline_mode=pl.Buffered(1)),
            pl.BlockSpec((windows, D, WIN), whole, pipeline_mode=pl.Buffered(1)),
            pl.BlockSpec((windows, WIN, D), whole, pipeline_mode=pl.Buffered(1)),
            pl.BlockSpec((windows, HEADS, WIN), whole),
            pl.BlockSpec((windows, 1, WIN, WIN), lambda h: (0, h, 0, 0)),
        ],
        out_specs=[
            pl.BlockSpec((windows, WIN, 3 * D), whole),
            pl.BlockSpec((1, FLAT, SPREAD), lambda h: (h, 0, 0)),
        ],
        out_shape=[
            jax.ShapeDtypeStruct((windows, WIN, 3 * D), BF16),
            jax.ShapeDtypeStruct((HEADS, FLAT, SPREAD), F32),
        ],
        scratch_shapes=[
            pltpu.VMEM((windows, D, WIN), BF16),
            pltpu.VMEM((windows, 3 * D, WIN), BF16),
            pltpu.VMEM((WIN, WIN), F32),
            pltpu.VMEM((FLAT, SPREAD), F32),
        ],
        compiler_params=pltpu.CompilerParams(vmem_limit_bytes=62 * MIB),
        name="attend_back",
    )(qkvt, attt, agrad, inverse, probs)


def qkv_back_kernel(
    x_ref, dqkv_ref, rgrad_ref, gain_ref, shift_ref, weight_ref, igrad_ref, wgrad_ref, sums_ref, norm_ref
):
    rows = x_ref.shape[0]
    block = rows // 2
    sums_ref[...] = jnp.zeros_like(sums_ref)

    def one_block(i, carry):
        at = pl.ds(pl.multiple_of(i * block, 16), block)
        unit, scale = standardize(x_ref[at, :].astype(F32))
        norm_ref[at, :] = (unit * gain_ref[...] + shift_ref[...]).astype(BF16)
        back = dot_nt(dqkv_ref[at, :], weight_ref[...])
        igrad_ref[at, :] = (rgrad_ref[at, :] + norm_backward(back, unit, scale, gain_ref[...])).astype(BF16)
        sums_ref[0:1, :D] += jnp.sum(back * unit, axis=0, keepdims=True)
        sums_ref[1:2, :D] += jnp.sum(back, axis=0, keepdims=True)
        sums_ref[2:3, :] += jnp.sum(dqkv_ref[at, :].astype(F32), axis=0, keepdims=True)
        return carry

    lax.fori_loop(0, 2, one_block, 0)
    for part in range(3):
        columns = slice(part * D, (part + 1) * D)
        wgrad_ref[:, columns] = dot_tn(norm_ref[...], dqkv_ref[:, columns]).astype(BF16)


def qkv_back(x_rows, dqkv_rows, rgrad, gain, shift, weight):
    rows = x_rows.shape[0]
    vmem = pl.BlockSpec(memory_space=pltpu.VMEM)
    return pl.pallas_call(
        qkv_back_kernel,
        in_specs=[vmem] * 6,
        out_specs=[vmem] * 3,
        out_shape=[
            jax.ShapeDtypeStruct((rows, D), BF16),
            jax.ShapeDtypeStruct((D, 3 * D), BF16),
            jax.ShapeDtypeStruct((8, 3 * D), F32),
        ],
        scratch_shapes=[pltpu.VMEM((rows, D), BF16)],
        compiler_params=pltpu.CompilerParams(vmem_limit_bytes=62 * MIB),
        name="qkv_back",
    )(x_rows, dqkv_rows, rgrad, gain, shift, weight)


def offset_choice():
    spots = np.arange(FLAT)
    rows, columns = spots // WIN_W, spots % WIN_W
    index = (rows[None, :] - rows[:, None] + WIN_H - 1) * OFFS_W + (
        columns[None, :] - columns[:, None] + WIN_W - 1
    )
    return jnp.asarray(index.reshape(1, -1)) == jnp.arange(OFFS_H * OFFS_W)[:, None]


def spread_table(bias_table):
    table = bias_table.reshape(OFFS_T, OFFS_H * OFFS_W, HEADS)
    table = jnp.transpose(table, (2, 0, 1)).reshape(HEADS * OFFS_T, OFFS_H * OFFS_W)
    wide = dot_nn(table, offset_choice().astype(BF16)) * LOG2E
    wide = wide.reshape(HEADS, OFFS_T, FLAT, FLAT)
    return jnp.transpose(wide, (0, 2, 1, 3)).reshape(HEADS, FLAT, SPREAD)


def fold_table(spread_grad):
    wide = spread_grad.reshape(HEADS, FLAT, OFFS_T, FLAT)
    wide = jnp.transpose(wide, (0, 2, 1, 3)).reshape(HEADS * OFFS_T, FLAT * FLAT)
    table = lax.dot_general(
        wide,
        offset_choice().astype(F32),
        (((1,), (1,)), ((), ())),
        precision=lax.Precision.HIGHEST,
        preferred_element_type=F32,
    )
    table = table.reshape(HEADS, OFFS_T, OFFS_H * OFFS_W)
    return jnp.transpose(table, (1, 2, 0)).reshape(-1, HEADS)


def valid_mask(extents):
    spots = np.arange(WIN)
    depth, height, across = spots // FLAT, spots // WIN_W % WIN_H, spots % WIN_W
    return (
        (depth[None, :] < extents[:, 0:1])
        & (height[None, :] < extents[:, 1:2])
        & (across[None, :] < extents[:, 2:3])
    ).astype(F32)


def gathered(value):
    return lax.all_gather(value, AXES, axis=0, tiled=True)


def scattered(value):
    return lax.psum_scatter(value, AXES, scatter_dimension=0, tiled=True)


def per_device(
    inputs,
    extents,
    cotangent,
    ln1_gain,
    ln1_shift,
    qkv_weight,
    query_bias,
    value_bias,
    bias_table,
    proj_weight,
    proj_shift,
    ln2_gain,
    ln2_shift,
    fc1_weight,
    fc1_shift,
    fc2_weight,
    fc2_shift,
):
    windows = inputs.shape[0]
    rows = windows * WIN
    small = ln1_gain.shape[0]
    count = D // small
    depth = lax.axis_size("fsdp") // 2
    direct = small % 16 == 0 and lax.axis_size("dp") == 4
    vectors = jnp.concatenate(
        (ln1_gain, ln1_shift, query_bias, value_bias, proj_shift, ln2_gain, ln2_shift, fc2_shift, fc1_shift)
    )
    length = vectors.shape[0]
    if direct:
        vectors = jnp.pad(vectors, (0, 16 * 128 - length)).reshape(16, 128)
        packed, qkv_full, proj_full, fc1_full, fc2_full = gather_all(
            depth,
            (vectors, qkv_weight, proj_weight, fc1_weight, fc2_weight),
            (
                ((0, 128, False),),
                ((0, 768, False), (768, 768, True)),
                ((0, 256, False), (256, 256, True)),
                ((0, 1024, False), (1024, 1024, True)),
                ((0, 256, False), (256, 256, True)),
            ),
        )
        packed = packed.reshape(count, 16 * 128)[:, :length]
    else:
        packed = lax.all_gather(vectors, AXES, axis=0)
        qkv_full, proj_full, fc1_full, fc2_full = [
            gathered(item) for item in (qkv_weight, proj_weight, fc1_weight, fc2_weight)
        ]
    pieces = [packed[:, i * small : (i + 1) * small].reshape(1, D).astype(F32) for i in range(8)]
    gain1, shift1, qbias, vbias, pshift, gain2, shift2, fshift2 = pieces
    fshift1 = packed[:, 8 * small :].reshape(1, FF).astype(F32)
    qkv_bias = jnp.concatenate([qbias, jnp.zeros_like(qbias), vbias], axis=1)

    keep = valid_mask(extents)
    keep_rows = keep.reshape(rows, 1)
    keyrow = jnp.concatenate(
        [((keep - 1.0) * 1e30)[:, None, :], jnp.zeros((windows, 15, WIN), F32)], axis=1
    ).astype(BF16)
    spread = spread_table(bias_table)

    x_rows = inputs.reshape(rows, D)
    qkv = project_qkv(x_rows, gain1, shift1, qkv_full, qkv_bias)
    qkvt, probs, att, attt, inverse = attend(qkv.reshape(windows, WIN, 3 * D), spread, keyrow)
    output, rgrad, agrad, fc1_grad, fc2_grad, proj_grad, sums, fsum = feed_forward(
        x_rows,
        att.reshape(rows, D),
        cotangent.reshape(rows, D),
        keep_rows,
        proj_full,
        pshift,
        gain2,
        shift2,
        fc1_full,
        fshift1,
        fc2_full,
        fshift2,
    )
    dqkv, spread_grad = attend_back(qkvt, attt, agrad.reshape(windows, WIN, D), inverse, probs)
    input_grad, qkv_grad, qsums = qkv_back(
        x_rows, dqkv.reshape(rows, 3 * D), rgrad, gain1, shift1, qkv_full
    )
    table_part = fold_table(spread_grad)
    vector_parts = jnp.concatenate(
        [
            item.reshape(count, -1)
            for item in (
                qsums[0, :D],
                qsums[1, :D],
                qsums[2, :D],
                qsums[2, 2 * D :],
                sums[3],
                sums[1],
                sums[2],
                sums[0],
                fsum[0],
            )
        ],
        axis=1,
    )
    matrices = (qkv_grad, proj_grad, fc1_grad, fc2_grad)
    if direct:
        table_rows = -(-table_part.size // (count * 128))
        table_flat = jnp.pad(table_part.reshape(-1), (0, count * table_rows * 128 - table_part.size))
        block = jnp.concatenate(
            [
                table_flat.reshape(count, table_rows * 128),
                vector_parts,
                jnp.zeros((count, 16 * 128 - table_rows * 128 - length), F32),
            ],
            axis=1,
        ).reshape(2, 2, depth, 2, 16, 128)
        views = [item.reshape(2, 2, depth, 2, -1, item.shape[1]) for item in matrices]
        block, qkv_own, proj_own, fc1_own, fc2_own, table_all = scatter_all(
            depth,
            (block, *views),
            (
                ((0, 128, False),),
                ((0, 768, False), (768, 768, True)),
                ((0, 256, False), (256, 256, True)),
                ((0, 1024, False), (1024, 1024, True)),
                ((0, 256, False), (256, 256, True)),
            ),
        )
        owned_vectors = block.reshape(-1)[table_rows * 128 : table_rows * 128 + length]
        table_all = table_all.reshape(count, 16, 128)[:, :table_rows].reshape(-1)
        table_grad = table_all[: table_part.size].reshape(table_part.shape)
    else:
        qkv_own, proj_own, fc1_own, fc2_own = [scattered(item.astype(F32)) for item in matrices]
        owned_vectors = scattered(vector_parts).reshape(-1)
        table_grad = lax.psum(table_part, AXES)
    owned = [owned_vectors[i * small : (i + 1) * small] for i in range(8)]
    return (
        output.reshape(inputs.shape),
        input_grad.reshape(inputs.shape),
        owned[0],
        owned[1],
        qkv_own,
        owned[2],
        owned[3],
        table_grad,
        proj_own,
        owned[4],
        owned[5],
        owned[6],
        fc1_own,
        owned_vectors[8 * small :],
        fc2_own,
        owned[7],
    )


def solution(mesh):
    rows = P(AXES, None)
    vector = P(AXES)
    block = P(AXES, None, None)
    in_specs = (
        block,
        rows,
        block,
        vector,
        vector,
        rows,
        vector,
        vector,
        P(),
        rows,
        vector,
        vector,
        vector,
        rows,
        vector,
        rows,
        vector,
    )
    out_specs = (
        block,
        block,
        vector,
        vector,
        rows,
        vector,
        vector,
        P(),
        rows,
        vector,
        vector,
        vector,
        rows,
        vector,
        rows,
        vector,
    )
    return jax.shard_map(
        per_device, mesh=mesh, in_specs=in_specs, out_specs=out_specs, check_vma=False
    )
```

```python
import functools
import math

import jax
import jax.numpy as jnp
import numpy as np
from jax import lax
from jax.experimental import pallas as pl
from jax.experimental.pallas import tpu as pltpu
from jax.sharding import PartitionSpec as P

D = 512
HEADS = 16
HDIM = 32
FF = 2048
WIN_T = 8
WIN_H = 7
WIN_W = 7
WIN = WIN_T * WIN_H * WIN_W
FLAT = WIN_H * WIN_W
OFFS_T = 2 * WIN_T - 1
OFFS_H = 2 * WIN_H - 1
OFFS_W = 2 * WIN_W - 1
SPREAD = OFFS_T * FLAT
EPS = 1e-05
LOG2E = math.log2(math.e)
LN2 = math.log(2.0)
SCALE = HDIM ** (-0.5)
AXES = ("dp", "fsdp")
BF16 = jnp.bfloat16
F32 = jnp.float32
MIB = 2**20


def dot(left, right, left_dim, right_dim):
    return lax.dot_general(
        left, right, (((left_dim,), (right_dim,)), ((), ())), preferred_element_type=F32
    )


def dot_nn(left, right):
    return dot(left, right, 1, 0)


def dot_nt(left, right):
    return dot(left, right, 1, 1)


def dot_tn(left, right):
    return dot(left, right, 0, 0)


def standardize(rows):
    average = jnp.mean(rows, axis=-1, keepdims=True)
    centered = rows - average
    variance = jnp.mean(centered * centered, axis=-1, keepdims=True)
    scale = lax.rsqrt(variance + EPS)
    return centered * scale, scale


def norm_backward(grad, unit, scale, gain):
    scaled = grad * gain
    first = jnp.mean(scaled, axis=-1, keepdims=True)
    second = jnp.mean(scaled * unit, axis=-1, keepdims=True)
    return (scaled - first - unit * second) * scale


def gelu_parts(hidden):
    reach = jnp.abs(hidden) * (0.5**0.5)
    ratio = 1.0 / (1.0 + 0.3275911 * reach)
    series = 1.061405429 * ratio - 1.453152027
    series = series * ratio + 1.421413741
    series = series * ratio - 0.284496736
    series = series * ratio + 0.254829592
    bell = jnp.exp(-0.5 * hidden * hidden)
    tail = (0.5 * series) * (ratio * bell)
    below = jnp.where(hidden < 0, tail, 1.0 - tail)
    return hidden * below, below + hidden * bell * (1.0 / math.sqrt(2 * math.pi))


class Place:
    def __init__(self, depth):
        dp, fsdp = lax.axis_index("dp"), lax.axis_index("fsdp")
        self.depth = depth
        self.y, self.c = dp // 2, dp % 2
        self.z, self.x = fsdp // 2, fsdp % 2
        self.core = (self.y * 2 + 1 - self.c, fsdp)
        self.across_x = (dp, self.z * 2 + 1 - self.x)
        self.across_y = ((1 - self.y) * 2 + self.c, fsdp)
        self.along_z = [(dp, ((self.z + j) % depth) * 2 + self.x) for j in range(1, depth)]

    def greet(self):
        barrier = pltpu.get_barrier_semaphore()
        partners = [self.core, self.across_x, self.across_y] + self.along_z
        for partner in partners:
            pl.semaphore_signal(barrier, inc=1, device_id=partner, device_id_type=pl.DeviceIdType.MESH)
        pl.semaphore_wait(barrier, len(partners))


def send(source, target, sems, slot, device):
    return pltpu.make_async_remote_copy(
        src_ref=source,
        dst_ref=target,
        send_sem=sems[0].at[slot],
        recv_sem=sems[1].at[slot],
        device_id=device,
        device_id_type=pl.DeviceIdType.MESH,
    )


def gather_slots(depth):
    return depth + 5


def gather_stages(place, own, full, sems, base, y_first):
    y, c, z, x, depth = place.y, place.c, place.z, place.x, place.depth
    every = slice(None)
    here = full(y, c, z, x)
    local = pltpu.make_async_copy(own, here, sems[0].at[base])
    along = [send(own, here, sems, base + j, place.along_z[j - 1]) for j in range(1, depth)]
    column = full(y, c, every, x)
    if y_first:
        first = send(column, column, sems, base + depth, place.across_y)
        both = full(every, c, every, x)
        second = send(both, both, sems, base + depth + 1, place.across_x)
        one = full(1 - y, c, every, x)
        two = full(every, c, every, 1 - x)
    else:
        first = send(column, column, sems, base + depth, place.across_x)
        both = full(y, c, every, every)
        second = send(both, both, sems, base + depth + 1, place.across_y)
        one = full(y, c, every, 1 - x)
        two = full(1 - y, c, every, every)
    shares = [
        send(part, part, sems, base + depth + 2 + k, place.core) for k, part in enumerate((column, one, two))
    ]

    def begin():
        local.start()
        for copy in along:
            copy.start()

    def turn():
        local.wait()
        for copy in along:
            copy.wait_recv()
        first.start()
        shares[0].start()

    def cross():
        first.wait_recv()
        second.start()
        shares[1].start()

    def share():
        second.wait_recv()
        shares[2].start()

    def finish():
        for copy in shares:
            copy.wait()
        for copy in along + [first, second]:
            copy.wait_send()

    return [begin, turn, cross, share, finish]


def scatter_slots(depth):
    return depth + 2


def add_into(target, index, extra):
    target[index] = (target[index].astype(F32) + extra.astype(F32)).astype(target.dtype)


def scatter_stages(place, parts, held, sems, base, x_first, result):
    y, c, z, x, depth = place.y, place.c, place.z, place.x, place.depth
    every = slice(None)
    from_core, from_first, from_second, from_z = held
    share = send(parts.at[:, 1 - c], from_core, sems, base, place.core)
    if x_first:
        first = send(parts.at[:, c, :, 1 - x], from_first, sems, base + 1, place.across_x)
        second = send(parts.at[1 - y, c, :, x], from_second, sems, base + 2, place.across_y)
    else:
        first = send(parts.at[1 - y, c], from_first, sems, base + 1, place.across_y)
        second = send(parts.at[y, c, :, 1 - x], from_second, sems, base + 2, place.across_x)
    along = [
        send(
            parts.at[y, c, (z + j) % depth, x],
            from_z.at[j - 1],
            sems,
            base + 2 + j,
            place.along_z[j - 1],
        )
        for j in range(1, depth)
    ]

    def begin():
        share.start()

    def cross():
        share.wait_recv()
        for yy in range(2):
            add_into(parts, (yy, c), from_core[yy])
        first.start()

    def turn():
        first.wait_recv()
        if x_first:
            for yy in range(2):
                for zz in range(depth):
                    add_into(parts, (yy, c, zz, x), from_first[yy, zz])
        else:
            add_into(parts, (y, c), from_first[...])
        second.start()

    def spread():
        second.wait_recv()
        for zz in range(depth):
            add_into(parts, (y, c, zz, x), from_second[zz])
        for copy in along:
            copy.start()

    def finish():
        for copy in along:
            copy.wait_recv()
        total = parts[y, c, z, x].astype(F32)
        for j in range(depth - 1):
            total = total + from_z[j].astype(F32)
        result[...] = total
        for copy in along + [share, first, second]:
            copy.wait_send()

    return [begin, cross, turn, spread, finish]


def held_shapes(depth, rows, columns, dtype, x_first):
    first = (2, depth, rows, columns) if x_first else (depth, 2, rows, columns)
    return [
        pltpu.VMEM((2, depth, 2, rows, columns), dtype),
        pltpu.VMEM(first, dtype),
        pltpu.VMEM((depth, rows, columns), dtype),
        pltpu.VMEM((depth - 1, rows, columns), dtype),
    ]


def in_turn(lists):
    for stage in zip(*lists):
        for step in stage:
            step()


def skewed(groups):
    stages = len(groups[0][0])
    ticks = []
    for t in range(len(groups) + stages - 1):
        tick = []
        for g, lists in enumerate(groups):
            if 0 <= t - g < stages:
                tick += [stage[t - g] for stage in lists]
        ticks.append(tick)
    return ticks


def scatter_kernel(depth, plan, *refs):
    count = len(plan)
    parts, outs, full = refs[:count], refs[count : 2 * count], refs[2 * count]
    works = refs[2 * count + 1 : 3 * count + 1]
    helds, sems = refs[3 * count + 1 : -2], refs[-2:]
    place = Place(depth)
    loads = []
    for i in range(count):
        loads.append(pltpu.make_async_copy(parts[i], works[i], sems[0].at[i]))
        loads[-1].start()
    place.greet()
    for load in loads:
        load.wait()
    lists, base, at = [], count, 0
    for work, out, cuts in zip(works, outs, plan):
        for start, size, x_first in cuts:
            columns = pl.ds(start, size)
            lists.append(
                scatter_stages(
                    place,
                    work.at[:, :, :, :, :, columns],
                    helds[at : at + 4],
                    sems,
                    base,
                    x_first,
                    out.at[:, columns],
                )
            )
            base += scatter_slots(depth)
            at += 4
    in_turn(lists)
    view = lambda y, c, z, x: full.at[y, c, z, x]
    in_turn([gather_stages(place, outs[0], view, sems, base, False)])


def scatter_all(depth, parts, plan):
    slots = len(parts) + scatter_slots(depth) * sum(len(cuts) for cuts in plan) + gather_slots(depth)
    vmem = pl.BlockSpec(memory_space=pltpu.VMEM)
    shapes = [pltpu.VMEM(part.shape, part.dtype) for part in parts]
    for part, cuts in zip(parts, plan):
        for _, size, x_first in cuts:
            shapes += held_shapes(depth, part.shape[-2], size, part.dtype, x_first)
    return pl.pallas_call(
        functools.partial(scatter_kernel, depth, plan),
        in_specs=[pl.BlockSpec(memory_space=pl.ANY)] * len(parts),
        out_specs=[vmem] * (len(parts) + 1),
        out_shape=[jax.ShapeDtypeStruct(part.shape[-2:], F32) for part in parts]
        + [jax.ShapeDtypeStruct(parts[0].shape, F32)],
        scratch_shapes=shapes + [pltpu.SemaphoreType.DMA((slots,)), pltpu.SemaphoreType.DMA((slots,))],
        compiler_params=pltpu.CompilerParams(
            collective_id=1, has_side_effects=True, vmem_limit_bytes=60 * MIB
        ),
        name="scatter_gradients",
    )(*parts)


def spots_of(shape, axis):
    return lax.broadcasted_iota(jnp.int32, shape, axis)


def pack_vectors(vectors):
    rows = spots_of((16, 128), 0)
    block = jnp.zeros((16, 128), F32)
    for i, vector in enumerate(vectors):
        vector = vector.astype(F32)
        if vector.shape[1] < 128:
            vector = jnp.concatenate([vector, jnp.zeros((1, 128 - vector.shape[1]), F32)], axis=1)
        block = jnp.where(rows == i, vector, block)
    return block


def unpack_vectors(blocks, count, small):
    width = count * small
    lanes, columns = spots_of((128, width), 0), spots_of((128, width), 1)
    choice = ((columns & (small - 1)) == lanes).astype(BF16)
    wide = dot_nn(blocks, choice).reshape(count, 16, width)
    owner = spots_of((count, 16, width), 0)
    column = spots_of((count, 16, width), 2)
    low = owner * small
    return jnp.sum(jnp.where((column >= low) & (column < low + small), wide, 0.0), axis=0)


def frame_spots(shape, axis):
    spot = spots_of(shape, axis)
    row = jnp.zeros(shape, jnp.int32)
    for i in range(1, WIN_H):
        row += (spot >= i * WIN_W).astype(jnp.int32)
    return (row + WIN_H - 1) * OFFS_W + spot - row * WIN_W + WIN_W - 1


def spread_bias(table_ref, spread_ref, line_ref):
    span = OFFS_H * OFFS_W
    table = table_ref[...].astype(F32)
    table = jnp.concatenate([table[k * span : (k + 1) * span] for k in range(OFFS_T)], axis=1)
    table = table.T.astype(BF16)
    base = frame_spots((span, FLAT), 1) - spots_of((span, FLAT), 0)

    def one(spot, carry):
        shift = spot // WIN_W * OFFS_W + spot % WIN_W
        choice = jnp.where(base == shift, 1.0, 0.0).astype(BF16)
        wide = dot_nn(table, choice) * LOG2E
        for k in range(OFFS_T):
            line_ref[:, k * FLAT : (k + 1) * FLAT] = wide[k * HEADS : (k + 1) * HEADS]
        for h in range(HEADS):
            spread_ref[h, pl.ds(spot, 1), :] = line_ref[h : h + 1, :]
        return carry

    lax.fori_loop(0, FLAT, one, 0)


def front_kernel(setup, *refs):
    windows, depth, direct, plan_one, plan_two, small = setup
    refs = list(refs)
    take = lambda count: [refs.pop(0) for _ in range(count)]
    x_ref, table_ref, keyrow_ref = take(3)
    if direct:
        vector_refs, shards = take(9), take(4)
    else:
        packed_ref, weight_in = take(2)
    qkvt_ref, probs_ref, att_ref, attt_ref, inv_ref, vec_ref, fvec_ref = take(7)
    if direct:
        wholes = take(4)
    spread_ref, line_ref, bias_ref, unit_ref = take(4)
    if direct:
        pack_ref, packed_ref, weight_ref, *sems = take(5)
    head = pl.program_id(0)
    count = D // small

    if direct:
        place = Place(depth)
        base = 0
        first, groups = [], []
        views = [packed_ref, weight_ref] + wholes[1:]
        sources = [pack_ref] + shards
        for plan, into in ((plan_one, None), (plan_two, groups)):
            for index, start, size, y_first in plan:
                columns = pl.ds(start, size)
                view = lambda y, c, z, x, whole=views[index], columns=columns: whole.at[y, c, z, x, :, columns]
                stages = gather_stages(place, sources[index].at[:, columns], view, sems, base, y_first)
                base += gather_slots(depth)
                if into is None:
                    first.append(stages)
                elif into and len(into[-1]) < 2:
                    into[-1].append(stages)
                else:
                    into.append([stages])
        ticks = skewed(groups)
        keep_weight = pltpu.make_async_copy(weight_ref, wholes[0], sems[0].at[base])

    def normalize():
        for w in range(windows):
            unit_ref[w], _ = standardize(x_ref[w].astype(F32))

    @pl.when(head == 0)
    def _():
        if direct:
            pack_ref[...] = pack_vectors([ref[...] for ref in vector_refs]).astype(BF16)
            place.greet()
            for stages in first:
                stages[0]()
            spread_bias(table_ref, spread_ref, line_ref)
            normalize()
            for k in range(1, 5):
                for stages in first:
                    stages[k]()
            keep_weight.start()
            weight = weight_ref[...].reshape(D, 3 * D)
            blocks = packed_ref[...].reshape(count * 16, 128)
        else:
            spread_bias(table_ref, spread_ref, line_ref)
            normalize()
            weight = weight_in[...]
            blocks = packed_ref[...]
        vectors = unpack_vectors(blocks, count, small)
        vec_ref[...] = vectors
        fvec_ref[...] = unpack_vectors(blocks, count, FF // count)[8:9]
        for w in range(windows):
            normed = (unit_ref[w] * vectors[0:1] + vectors[1:2]).astype(BF16)
            for part in range(3):
                got = dot_nn(normed, weight[:, part * D : (part + 1) * D])
                if part == 0:
                    got = (got + vectors[2:3]) * (SCALE * LOG2E)
                if part == 2:
                    got = got + vectors[3:4]
                for piece in range(4):
                    at = part * D + piece * 128
                    qkvt_ref[w, at : at + 128, :] = got[:, piece * 128 : (piece + 1) * 128].T.astype(BF16)

    if direct:
        for t, tick in enumerate(ticks):

            @pl.when(head == 2 * t)
            def _(tick=tick):
                for step in tick:
                    step()

    for u in range(WIN_T):
        start = (WIN_T - 1 - u) * FLAT
        bias_ref[u * FLAT : (u + 1) * FLAT, :] = spread_ref[head, :, start : start + WIN]
    row = pl.multiple_of(head * HDIM, HDIM)
    ones = jnp.ones((16, WIN), BF16)
    for w in range(windows):
        queries = qkvt_ref[w, pl.ds(row, HDIM), :]
        keys = qkvt_ref[w, pl.ds(row + D, HDIM), :]
        values = qkvt_ref[w, pl.ds(row + 2 * D, HDIM), :]
        scores = dot_tn(
            jnp.concatenate([keys, keyrow_ref[w]], axis=0), jnp.concatenate([queries, ones], axis=0)
        )
        scores = scores + bias_ref[...]
        top = jnp.max(scores, axis=0, keepdims=True)
        expo = jnp.exp2(scores - top).astype(BF16)
        probs_ref[w, 0] = expo
        mixed = dot_nn(jnp.concatenate([values, ones], axis=0), expo)
        inverse = 1.0 / mixed[HDIM : HDIM + 1]
        inv_ref[w, pl.ds(head, 1), :] = inverse
        attt_ref[w, pl.ds(row, HDIM), :] = (mixed[:HDIM] * inverse).astype(BF16)

    @pl.when(head == HEADS - 1)
    def _():
        for w in range(windows):
            for part in range(4):
                rows = slice(part * 128, (part + 1) * 128)
                att_ref[w, :, rows] = attt_ref[w, rows, :].astype(F32).T.astype(BF16)
        if direct:
            keep_weight.wait()


def front(inputs, table, keyrow, vectors, weights, packed, depth, direct):
    windows = inputs.shape[0]
    once = lambda shape: pl.BlockSpec(shape, lambda h: (0,) * len(shape), pipeline_mode=pl.Buffered(1))
    anywhere = pl.BlockSpec(memory_space=pl.ANY)
    outs = [
        (once((windows, 3 * D, WIN)), jax.ShapeDtypeStruct((windows, 3 * D, WIN), BF16)),
        (
            pl.BlockSpec((windows, 1, WIN, WIN), lambda h: (0, h, 0, 0)),
            jax.ShapeDtypeStruct((windows, HEADS, WIN, WIN), BF16),
        ),
        (once((windows, WIN, D)), jax.ShapeDtypeStruct((windows, WIN, D), BF16)),
        (once((windows, D, WIN)), jax.ShapeDtypeStruct((windows, D, WIN), BF16)),
        (once((windows, HEADS, WIN)), jax.ShapeDtypeStruct((windows, HEADS, WIN), F32)),
        (once((16, D)), jax.ShapeDtypeStruct((16, D), F32)),
        (once((1, FF)), jax.ShapeDtypeStruct((1, FF), F32)),
    ]
    scratch = [
        pltpu.VMEM((HEADS, FLAT, SPREAD), F32),
        pltpu.VMEM((HEADS, SPREAD), F32),
        pltpu.VMEM((WIN, WIN), F32),
        pltpu.VMEM((windows, WIN, D), F32),
    ]
    args = [inputs, table, keyrow]
    small = vectors[0].shape[1]
    plan_one = ((0, 0, 128, False), (1, 0, 768, False), (1, 768, 768, True))
    plan_two = (
        (2, 0, 256, False),
        (2, 256, 256, True),
        (3, 0, 1024, False),
        (3, 1024, 1024, True),
        (4, 0, 256, False),
        (4, 256, 256, True),
    )
    extra = {}
    if direct:
        args += list(vectors) + list(weights)
        specs = [once(item.shape) for item in args[:-4]] + [anywhere] * 4
        wholes = [jax.ShapeDtypeStruct((2, 2, depth, 2) + item.shape, BF16) for item in weights]
        outs += [(anywhere, whole) for whole in wholes]
        slots = gather_slots(depth) * (len(plan_one) + len(plan_two)) + 1
        scratch += [
            pltpu.VMEM((16, 128), BF16),
            pltpu.VMEM((2, 2, depth, 2, 16, 128), BF16),
            pltpu.VMEM(wholes[0].shape, BF16),
            pltpu.SemaphoreType.DMA((slots,)),
            pltpu.SemaphoreType.DMA((slots,)),
        ]
        extra = dict(collective_id=0, has_side_effects=True)
    else:
        args += [packed, weights[0]]
        specs = [once(item.shape) for item in args]
    return pl.pallas_call(
        functools.partial(front_kernel, (windows, depth, direct, plan_one, plan_two, small)),
        grid=(HEADS,),
        in_specs=specs,
        out_specs=[spec for spec, _ in outs],
        out_shape=[shape for _, shape in outs],
        scratch_shapes=scratch,
        compiler_params=pltpu.CompilerParams(vmem_limit_bytes=60 * MIB, **extra),
        name="front",
    )(*args)


def mlp_kernel(
    x_ref,
    att_ref,
    cot_ref,
    keep_ref,
    proj_ref,
    pshift_ref,
    gain_ref,
    shift_ref,
    fc1_ref,
    fshift1_ref,
    fc2_ref,
    fshift2_ref,
    out_ref,
    rgrad_ref,
    agrad_ref,
    fc1g_ref,
    fc2g_ref,
    projg_ref,
    sums_ref,
    fsum_ref,
    act_ref,
    hid_ref,
    norm_ref,
    gout_ref,
    branch_ref,
):
    rows = x_ref.shape[0]
    block = rows // 2
    pieces = 4
    wide = FF // pieces
    sums_ref[...] = jnp.zeros_like(sums_ref)
    fsum_ref[...] = jnp.zeros_like(fsum_ref)

    def one_block(i, carry):
        at = pl.ds(pl.multiple_of(i * block, 16), block)
        keep = keep_ref[at, :]
        resid = x_ref[at, :].astype(F32) + dot_nn(att_ref[at, :], proj_ref[...]) + pshift_ref[...]
        unit, scale = standardize(resid)
        normed = (unit * gain_ref[...] + shift_ref[...]).astype(BF16)
        norm_ref[at, :] = normed
        gout = cot_ref[at, :].astype(F32) * keep
        gout_low = gout.astype(BF16)
        gout_ref[at, :] = gout_low
        total = resid + fshift2_ref[...]
        grad_two = None
        for part in range(pieces):
            columns = slice(part * wide, (part + 1) * wide)
            hidden = dot_nn(normed, fc1_ref[:, columns]) + fshift1_ref[:, columns]
            active, slope = gelu_parts(hidden)
            active = active.astype(BF16)
            act_ref[at, columns] = active
            total = total + dot_nn(active, fc2_ref[columns, :])
            hgrad = (dot_nt(gout_low, fc2_ref[columns, :]) * slope).astype(BF16)
            hid_ref[at, columns] = hgrad
            fsum_ref[0:1, columns] += jnp.sum(hgrad.astype(F32), axis=0, keepdims=True)
            back = dot_nt(hgrad, fc1_ref[:, columns])
            grad_two = back if grad_two is None else grad_two + back
        out_ref[at, :] = (total * keep).astype(BF16)
        rgrad = gout + norm_backward(grad_two, unit, scale, gain_ref[...])
        rgrad_ref[at, :] = rgrad
        branch = rgrad.astype(BF16)
        branch_ref[at, :] = branch
        agrad_ref[at, :] = dot_nt(branch, proj_ref[...]).astype(BF16)
        sums_ref[0:1, :] += jnp.sum(gout, axis=0, keepdims=True)
        sums_ref[1:2, :] += jnp.sum(grad_two * unit, axis=0, keepdims=True)
        sums_ref[2:3, :] += jnp.sum(grad_two, axis=0, keepdims=True)
        sums_ref[3:4, :] += jnp.sum(branch.astype(F32), axis=0, keepdims=True)
        return carry

    lax.fori_loop(0, 2, one_block, 0)
    projg_ref[...] = dot_tn(att_ref[...], branch_ref[...]).astype(BF16)
    for part in range(pieces):
        columns = slice(part * wide, (part + 1) * wide)
        fc2g_ref[columns, :] = dot_tn(act_ref[:, columns], gout_ref[...]).astype(BF16)
        fc1g_ref[:, columns] = dot_tn(norm_ref[...], hid_ref[:, columns]).astype(BF16)


def feed_forward(x_rows, att_rows, cot_rows, keep_rows, proj, pshift, gain, shift, fc1, fshift1, fc2, fshift2):
    rows = x_rows.shape[0]
    vmem = pl.BlockSpec(memory_space=pltpu.VMEM)
    return pl.pallas_call(
        mlp_kernel,
        in_specs=[vmem] * 12,
        out_specs=[vmem] * 8,
        out_shape=[
            jax.ShapeDtypeStruct((rows, D), BF16),
            jax.ShapeDtypeStruct((rows, D), F32),
            jax.ShapeDtypeStruct((rows, D), BF16),
            jax.ShapeDtypeStruct((D, FF), BF16),
            jax.ShapeDtypeStruct((FF, D), BF16),
            jax.ShapeDtypeStruct((D, D), BF16),
            jax.ShapeDtypeStruct((8, D), F32),
            jax.ShapeDtypeStruct((8, FF), F32),
        ],
        scratch_shapes=[
            pltpu.VMEM((rows, FF), BF16),
            pltpu.VMEM((rows, FF), BF16),
            pltpu.VMEM((rows, D), BF16),
            pltpu.VMEM((rows, D), BF16),
            pltpu.VMEM((rows, D), BF16),
        ],
        compiler_params=pltpu.CompilerParams(vmem_limit_bytes=62 * MIB),
        name="feed_forward",
    )(x_rows, att_rows, cot_rows, keep_rows, proj, pshift, gain, shift, fc1, fshift1, fc2, fshift2)


def attend_back_kernel(
    windows,
    qkvt_ref,
    attt_ref,
    agrad_ref,
    inv_ref,
    probs_ref,
    dqkv_ref,
    fold_ref,
    dot_ref,
    dqkvt_ref,
    sum_ref,
    wide_ref,
):
    head = pl.program_id(0)

    @pl.when(head == 0)
    def _():
        for w in range(windows):
            for part in range(4):
                rows = slice(part * 128, (part + 1) * 128)
                dot_ref[w, rows, :] = agrad_ref[w, :, rows].astype(F32).T.astype(BF16)

    row = pl.multiple_of(head * HDIM, HDIM)
    ones = jnp.ones((16, WIN), BF16)
    place = lax.broadcasted_iota(jnp.int32, (16, WIN), 0)
    for w in range(windows):
        queries = qkvt_ref[w, pl.ds(row, HDIM), :]
        keys = qkvt_ref[w, pl.ds(row + D, HDIM), :]
        values = qkvt_ref[w, pl.ds(row + 2 * D, HDIM), :]
        expo = probs_ref[w, 0]
        grad = dot_ref[w, pl.ds(row, HDIM), :].astype(F32) * inv_ref[w, pl.ds(head, 1), :]
        inner = -jnp.sum(grad * attt_ref[w, pl.ds(row, HDIM), :].astype(F32), axis=0, keepdims=True)
        high = inner.astype(BF16).astype(F32)
        middle = (inner - high).astype(BF16).astype(F32)
        lowest = inner - high - middle
        extra = jnp.where(
            place == 0, high, jnp.where(place == 1, middle, jnp.where(place == 2, lowest, 0.0))
        ).astype(BF16)
        grad = grad.astype(BF16)
        probs_grad = dot_tn(
            jnp.concatenate([values, ones], axis=0), jnp.concatenate([grad, extra], axis=0)
        )
        scores_grad = expo.astype(F32) * probs_grad
        low = scores_grad.astype(BF16)
        if w == 0:
            sum_ref[...] = scores_grad
        else:
            sum_ref[...] += scores_grad
        dqkvt_ref[w, pl.ds(row, HDIM), :] = (dot_nn(keys, low) * SCALE).astype(BF16)
        dqkvt_ref[w, pl.ds(row + D, HDIM), :] = (dot_nt(queries, low) * LN2).astype(BF16)
        dqkvt_ref[w, pl.ds(row + 2 * D, HDIM), :] = dot_nt(grad, expo).astype(BF16)

    wide_ref[...] = jnp.zeros_like(wide_ref)
    for u in range(WIN_T):
        start = (WIN_T - 1 - u) * FLAT
        wide_ref[:, start : start + WIN] += sum_ref[u * FLAT : (u + 1) * FLAT, :]
    fold_ref[0] = wide_ref[...]

    @pl.when(head == HEADS - 1)
    def _():
        for w in range(windows):
            for part in range(12):
                rows = slice(part * 128, (part + 1) * 128)
                dqkv_ref[w, :, rows] = dqkvt_ref[w, rows, :].astype(F32).T.astype(BF16)


def attend_back(qkvt, attt, agrad, inverse, probs):
    windows = qkvt.shape[0]
    whole = lambda h: (0, 0, 0)
    return pl.pallas_call(
        functools.partial(attend_back_kernel, windows),
        grid=(HEADS,),
        in_specs=[
            pl.BlockSpec((windows, 3 * D, WIN), whole, pipeline_mode=pl.Buffered(1)),
            pl.BlockSpec((windows, D, WIN), whole, pipeline_mode=pl.Buffered(1)),
            pl.BlockSpec((windows, WIN, D), whole, pipeline_mode=pl.Buffered(1)),
            pl.BlockSpec((windows, HEADS, WIN), whole),
            pl.BlockSpec((windows, 1, WIN, WIN), lambda h: (0, h, 0, 0)),
        ],
        out_specs=[
            pl.BlockSpec((windows, WIN, 3 * D), whole),
            pl.BlockSpec((1, FLAT, SPREAD), lambda h: (h, 0, 0)),
        ],
        out_shape=[
            jax.ShapeDtypeStruct((windows, WIN, 3 * D), BF16),
            jax.ShapeDtypeStruct((HEADS, FLAT, SPREAD), F32),
        ],
        scratch_shapes=[
            pltpu.VMEM((windows, D, WIN), BF16),
            pltpu.VMEM((windows, 3 * D, WIN), BF16),
            pltpu.VMEM((WIN, WIN), F32),
            pltpu.VMEM((FLAT, SPREAD), F32),
        ],
        compiler_params=pltpu.CompilerParams(vmem_limit_bytes=62 * MIB),
        name="attend_back",
    )(qkvt, attt, agrad, inverse, probs)


def qkv_back_kernel(
    x_ref, dqkv_ref, rgrad_ref, gain_ref, shift_ref, weight_ref, igrad_ref, wgrad_ref, sums_ref, norm_ref
):
    rows = x_ref.shape[0]
    block = rows // 2
    sums_ref[...] = jnp.zeros_like(sums_ref)

    def one_block(i, carry):
        at = pl.ds(pl.multiple_of(i * block, 16), block)
        unit, scale = standardize(x_ref[at, :].astype(F32))
        norm_ref[at, :] = (unit * gain_ref[...] + shift_ref[...]).astype(BF16)
        back = dot_nt(dqkv_ref[at, :], weight_ref[...])
        igrad_ref[at, :] = (rgrad_ref[at, :] + norm_backward(back, unit, scale, gain_ref[...])).astype(BF16)
        sums_ref[0:1, :D] += jnp.sum(back * unit, axis=0, keepdims=True)
        sums_ref[1:2, :D] += jnp.sum(back, axis=0, keepdims=True)
        sums_ref[2:3, :] += jnp.sum(dqkv_ref[at, :].astype(F32), axis=0, keepdims=True)
        return carry

    lax.fori_loop(0, 2, one_block, 0)
    for part in range(3):
        columns = slice(part * D, (part + 1) * D)
        wgrad_ref[:, columns] = dot_tn(norm_ref[...], dqkv_ref[:, columns]).astype(BF16)


def qkv_back(x_rows, dqkv_rows, rgrad, gain, shift, weight):
    rows = x_rows.shape[0]
    vmem = pl.BlockSpec(memory_space=pltpu.VMEM)
    return pl.pallas_call(
        qkv_back_kernel,
        in_specs=[vmem] * 6,
        out_specs=[vmem] * 3,
        out_shape=[
            jax.ShapeDtypeStruct((rows, D), BF16),
            jax.ShapeDtypeStruct((D, 3 * D), BF16),
            jax.ShapeDtypeStruct((8, 3 * D), F32),
        ],
        scratch_shapes=[pltpu.VMEM((rows, D), BF16)],
        compiler_params=pltpu.CompilerParams(vmem_limit_bytes=62 * MIB),
        name="qkv_back",
    )(x_rows, dqkv_rows, rgrad, gain, shift, weight)


def offset_choice():
    spots = np.arange(FLAT)
    rows, columns = spots // WIN_W, spots % WIN_W
    index = (rows[None, :] - rows[:, None] + WIN_H - 1) * OFFS_W + (
        columns[None, :] - columns[:, None] + WIN_W - 1
    )
    return jnp.asarray(index.reshape(1, -1)) == jnp.arange(OFFS_H * OFFS_W)[:, None]


def fold_table(spread_grad):
    wide = spread_grad.reshape(HEADS, FLAT, OFFS_T, FLAT)
    wide = jnp.transpose(wide, (0, 2, 1, 3)).reshape(HEADS * OFFS_T, FLAT * FLAT)
    table = lax.dot_general(
        wide,
        offset_choice().astype(F32),
        (((1,), (1,)), ((), ())),
        precision=lax.Precision.HIGHEST,
        preferred_element_type=F32,
    )
    table = table.reshape(HEADS, OFFS_T, OFFS_H * OFFS_W)
    return jnp.transpose(table, (1, 2, 0)).reshape(-1, HEADS)


def valid_mask(extents):
    spots = np.arange(WIN)
    depth, height, across = spots // FLAT, spots // WIN_W % WIN_H, spots % WIN_W
    return (
        (depth[None, :] < extents[:, 0:1])
        & (height[None, :] < extents[:, 1:2])
        & (across[None, :] < extents[:, 2:3])
    ).astype(F32)


def gathered(value):
    return lax.all_gather(value, AXES, axis=0, tiled=True)


def scattered(value):
    return lax.psum_scatter(value, AXES, scatter_dimension=0, tiled=True)


def per_device(
    inputs,
    extents,
    cotangent,
    ln1_gain,
    ln1_shift,
    qkv_weight,
    query_bias,
    value_bias,
    bias_table,
    proj_weight,
    proj_shift,
    ln2_gain,
    ln2_shift,
    fc1_weight,
    fc1_shift,
    fc2_weight,
    fc2_shift,
):
    windows = inputs.shape[0]
    rows = windows * WIN
    small = ln1_gain.shape[0]
    count = D // small
    depth = lax.axis_size("fsdp") // 2
    direct = small % 16 == 0 and lax.axis_size("dp") == 4
    vectors = [
        item[None]
        for item in (
            ln1_gain,
            ln1_shift,
            query_bias,
            value_bias,
            proj_shift,
            ln2_gain,
            ln2_shift,
            fc2_shift,
            fc1_shift,
        )
    ]
    length = 8 * small + FF // count
    weights = (qkv_weight, proj_weight, fc1_weight, fc2_weight)
    packed = None
    if not direct:
        packed = jnp.concatenate([jnp.pad(item, ((0, 0), (0, 128 - item.shape[1]))) for item in vectors])
        packed = gathered(jnp.pad(packed, ((0, 16 - len(vectors)), (0, 0))))
        weights = [gathered(item) for item in weights]
    keep = valid_mask(extents)
    keep_rows = keep.reshape(rows, 1)
    keyrow = jnp.concatenate(
        [((keep - 1.0) * 1e30)[:, None, :], jnp.zeros((windows, 15, WIN), F32)], axis=1
    ).astype(BF16)
    x_rows = inputs.reshape(rows, D)
    qkvt, probs, att, attt, inverse, full_vectors, fshift1, *wholes = front(
        inputs, bias_table, keyrow, vectors, weights, packed, depth, direct
    )
    if direct:
        weights = [item.reshape(-1, item.shape[-1]) for item in wholes]
    qkv_full, proj_full, fc1_full, fc2_full = weights
    gain1, shift1, _, _, pshift, gain2, shift2, fshift2 = [full_vectors[i : i + 1] for i in range(8)]
    output, rgrad, agrad, fc1_grad, fc2_grad, proj_grad, sums, fsum = feed_forward(
        x_rows,
        att.reshape(rows, D),
        cotangent.reshape(rows, D),
        keep_rows,
        proj_full,
        pshift,
        gain2,
        shift2,
        fc1_full,
        fshift1,
        fc2_full,
        fshift2,
    )
    dqkv, spread_grad = attend_back(qkvt, attt, agrad.reshape(windows, WIN, D), inverse, probs)
    input_grad, qkv_grad, qsums = qkv_back(
        x_rows, dqkv.reshape(rows, 3 * D), rgrad, gain1, shift1, qkv_full
    )
    table_part = fold_table(spread_grad)
    vector_parts = jnp.concatenate(
        [
            item.reshape(count, -1)
            for item in (
                qsums[0, :D],
                qsums[1, :D],
                qsums[2, :D],
                qsums[2, 2 * D :],
                sums[3],
                sums[1],
                sums[2],
                sums[0],
                fsum[0],
            )
        ],
        axis=1,
    )
    matrices = (qkv_grad, proj_grad, fc1_grad, fc2_grad)
    if direct:
        table_rows = -(-table_part.size // (count * 128))
        table_flat = jnp.pad(table_part.reshape(-1), (0, count * table_rows * 128 - table_part.size))
        block = jnp.concatenate(
            [
                table_flat.reshape(count, table_rows * 128),
                vector_parts,
                jnp.zeros((count, 16 * 128 - table_rows * 128 - length), F32),
            ],
            axis=1,
        ).reshape(2, 2, depth, 2, 16, 128)
        views = [item.reshape(2, 2, depth, 2, -1, item.shape[1]) for item in matrices]
        block, qkv_own, proj_own, fc1_own, fc2_own, table_all = scatter_all(
            depth,
            (block, *views),
            (
                ((0, 128, False),),
                ((0, 768, False), (768, 768, True)),
                ((0, 256, False), (256, 256, True)),
                ((0, 1024, False), (1024, 1024, True)),
                ((0, 256, False), (256, 256, True)),
            ),
        )
        owned_vectors = block.reshape(-1)[table_rows * 128 : table_rows * 128 + length]
        table_all = table_all.reshape(count, 16, 128)[:, :table_rows].reshape(-1)
        table_grad = table_all[: table_part.size].reshape(table_part.shape)
    else:
        qkv_own, proj_own, fc1_own, fc2_own = [scattered(item.astype(F32)) for item in matrices]
        owned_vectors = scattered(vector_parts).reshape(-1)
        table_grad = lax.psum(table_part, AXES)
    owned = [owned_vectors[i * small : (i + 1) * small] for i in range(8)]
    return (
        output.reshape(inputs.shape),
        input_grad.reshape(inputs.shape),
        owned[0],
        owned[1],
        qkv_own,
        owned[2],
        owned[3],
        table_grad,
        proj_own,
        owned[4],
        owned[5],
        owned[6],
        fc1_own,
        owned_vectors[8 * small :],
        fc2_own,
        owned[7],
    )


def solution(mesh):
    rows = P(AXES, None)
    vector = P(AXES)
    block = P(AXES, None, None)
    in_specs = (
        block,
        rows,
        block,
        vector,
        vector,
        rows,
        vector,
        vector,
        P(),
        rows,
        vector,
        vector,
        vector,
        rows,
        vector,
        rows,
        vector,
    )
    out_specs = (
        block,
        block,
        vector,
        vector,
        rows,
        vector,
        vector,
        P(),
        rows,
        vector,
        vector,
        vector,
        rows,
        vector,
        rows,
        vector,
    )
    return jax.shard_map(
        per_device, mesh=mesh, in_specs=in_specs, out_specs=out_specs, check_vma=False
    )
```

```python
import functools
import math

import jax
import jax.numpy as jnp
import numpy as np
from jax import lax
from jax.experimental import pallas as pl
from jax.experimental.pallas import tpu as pltpu
from jax.sharding import PartitionSpec as P

D = 512
HEADS = 16
HDIM = 32
FF = 2048
WIN_T = 8
WIN_H = 7
WIN_W = 7
WIN = WIN_T * WIN_H * WIN_W
FLAT = WIN_H * WIN_W
OFFS_T = 2 * WIN_T - 1
OFFS_H = 2 * WIN_H - 1
OFFS_W = 2 * WIN_W - 1
SPREAD = OFFS_T * FLAT
EPS = 1e-05
LOG2E = math.log2(math.e)
LN2 = math.log(2.0)
SCALE = HDIM ** (-0.5)
AXES = ("dp", "fsdp")
BF16 = jnp.bfloat16
F32 = jnp.float32
MIB = 2**20


def dot(left, right, left_dim, right_dim):
    return lax.dot_general(
        left, right, (((left_dim,), (right_dim,)), ((), ())), preferred_element_type=F32
    )


def dot_nn(left, right):
    return dot(left, right, 1, 0)


def dot_nt(left, right):
    return dot(left, right, 1, 1)


def dot_tn(left, right):
    return dot(left, right, 0, 0)


def standardize(rows):
    average = jnp.mean(rows, axis=-1, keepdims=True)
    centered = rows - average
    variance = jnp.mean(centered * centered, axis=-1, keepdims=True)
    scale = lax.rsqrt(variance + EPS)
    return centered * scale, scale


def norm_backward(grad, unit, scale, gain):
    scaled = grad * gain
    first = jnp.mean(scaled, axis=-1, keepdims=True)
    second = jnp.mean(scaled * unit, axis=-1, keepdims=True)
    return (scaled - first - unit * second) * scale


def gelu_parts(hidden):
    reach = jnp.abs(hidden) * (0.5**0.5)
    ratio = 1.0 / (1.0 + 0.3275911 * reach)
    series = 1.061405429 * ratio - 1.453152027
    series = series * ratio + 1.421413741
    series = series * ratio - 0.284496736
    series = series * ratio + 0.254829592
    bell = jnp.exp(-0.5 * hidden * hidden)
    tail = (0.5 * series) * (ratio * bell)
    below = jnp.where(hidden < 0, tail, 1.0 - tail)
    return hidden * below, below + hidden * bell * (1.0 / math.sqrt(2 * math.pi))


class Place:
    def __init__(self, depth):
        dp, fsdp = lax.axis_index("dp"), lax.axis_index("fsdp")
        self.depth = depth
        self.y, self.c = dp // 2, dp % 2
        self.z, self.x = fsdp // 2, fsdp % 2
        self.core = (self.y * 2 + 1 - self.c, fsdp)
        self.across_x = (dp, self.z * 2 + 1 - self.x)
        self.across_y = ((1 - self.y) * 2 + self.c, fsdp)
        self.along_z = [(dp, ((self.z + j) % depth) * 2 + self.x) for j in range(1, depth)]

    def greet(self):
        barrier = pltpu.get_barrier_semaphore()
        partners = [self.core, self.across_x, self.across_y] + self.along_z
        for partner in partners:
            pl.semaphore_signal(barrier, inc=1, device_id=partner, device_id_type=pl.DeviceIdType.MESH)
        pl.semaphore_wait(barrier, len(partners))


def send(source, target, sems, slot, device):
    return pltpu.make_async_remote_copy(
        src_ref=source,
        dst_ref=target,
        send_sem=sems[0].at[slot],
        recv_sem=sems[1].at[slot],
        device_id=device,
        device_id_type=pl.DeviceIdType.MESH,
    )


def gather_slots(depth):
    return depth + 5


def gather_stages(place, own, full, sems, base, y_first):
    y, c, z, x, depth = place.y, place.c, place.z, place.x, place.depth
    every = slice(None)
    here = full(y, c, z, x)
    local = pltpu.make_async_copy(own, here, sems[0].at[base])
    along = [send(own, here, sems, base + j, place.along_z[j - 1]) for j in range(1, depth)]
    column = full(y, c, every, x)
    if y_first:
        first = send(column, column, sems, base + depth, place.across_y)
        both = full(every, c, every, x)
        second = send(both, both, sems, base + depth + 1, place.across_x)
        one = full(1 - y, c, every, x)
        two = full(every, c, every, 1 - x)
    else:
        first = send(column, column, sems, base + depth, place.across_x)
        both = full(y, c, every, every)
        second = send(both, both, sems, base + depth + 1, place.across_y)
        one = full(y, c, every, 1 - x)
        two = full(1 - y, c, every, every)
    shares = [
        send(part, part, sems, base + depth + 2 + k, place.core) for k, part in enumerate((column, one, two))
    ]

    def begin():
        local.start()
        for copy in along:
            copy.start()

    def turn():
        local.wait()
        for copy in along:
            copy.wait_recv()
        first.start()
        shares[0].start()

    def cross():
        first.wait_recv()
        second.start()
        shares[1].start()

    def share():
        second.wait_recv()
        shares[2].start()

    def finish():
        for copy in shares:
            copy.wait()
        for copy in along + [first, second]:
            copy.wait_send()

    return [begin, turn, cross, share, finish]


def scatter_slots(depth):
    return depth + 2


def add_into(target, index, extra):
    target[index] = (target[index].astype(F32) + extra.astype(F32)).astype(target.dtype)


def scatter_stages(place, parts, held, sems, base, x_first, result):
    y, c, z, x, depth = place.y, place.c, place.z, place.x, place.depth
    every = slice(None)
    from_core, from_first, from_second, from_z = held
    share = send(parts.at[:, 1 - c], from_core, sems, base, place.core)
    if x_first:
        first = send(parts.at[:, c, :, 1 - x], from_first, sems, base + 1, place.across_x)
        second = send(parts.at[1 - y, c, :, x], from_second, sems, base + 2, place.across_y)
    else:
        first = send(parts.at[1 - y, c], from_first, sems, base + 1, place.across_y)
        second = send(parts.at[y, c, :, 1 - x], from_second, sems, base + 2, place.across_x)
    along = [
        send(
            parts.at[y, c, (z + j) % depth, x],
            from_z.at[j - 1],
            sems,
            base + 2 + j,
            place.along_z[j - 1],
        )
        for j in range(1, depth)
    ]

    def begin():
        share.start()

    def cross():
        share.wait_recv()
        for yy in range(2):
            add_into(parts, (yy, c), from_core[yy])
        first.start()

    def turn():
        first.wait_recv()
        if x_first:
            for yy in range(2):
                for zz in range(depth):
                    add_into(parts, (yy, c, zz, x), from_first[yy, zz])
        else:
            add_into(parts, (y, c), from_first[...])
        second.start()

    def spread():
        second.wait_recv()
        for zz in range(depth):
            add_into(parts, (y, c, zz, x), from_second[zz])
        for copy in along:
            copy.start()

    def finish():
        for copy in along:
            copy.wait_recv()
        total = parts[y, c, z, x].astype(F32)
        for j in range(depth - 1):
            total = total + from_z[j].astype(F32)
        result[...] = total
        for copy in along + [share, first, second]:
            copy.wait_send()

    return [begin, cross, turn, spread, finish]


def held_shapes(depth, rows, columns, dtype, x_first):
    first = (2, depth, rows, columns) if x_first else (depth, 2, rows, columns)
    return [
        pltpu.VMEM((2, depth, 2, rows, columns), dtype),
        pltpu.VMEM(first, dtype),
        pltpu.VMEM((depth, rows, columns), dtype),
        pltpu.VMEM((depth - 1, rows, columns), dtype),
    ]


def in_turn(lists):
    for stage in zip(*lists):
        for step in stage:
            step()


def skewed(groups):
    stages = len(groups[0][0])
    ticks = []
    for t in range(len(groups) + stages - 1):
        tick = []
        for g, lists in enumerate(groups):
            if 0 <= t - g < stages:
                tick += [stage[t - g] for stage in lists]
        ticks.append(tick)
    return ticks


def spots_of(shape, axis):
    return lax.broadcasted_iota(jnp.int32, shape, axis)


def pack_vectors(vectors):
    rows = spots_of((16, 128), 0)
    block = jnp.zeros((16, 128), F32)
    for i, vector in enumerate(vectors):
        vector = vector.astype(F32)
        if vector.shape[1] < 128:
            vector = jnp.concatenate([vector, jnp.zeros((1, 128 - vector.shape[1]), F32)], axis=1)
        block = jnp.where(rows == i, vector, block)
    return block


def unpack_vectors(blocks, count, small):
    width = count * small
    lanes, columns = spots_of((128, width), 0), spots_of((128, width), 1)
    choice = ((columns & (small - 1)) == lanes).astype(BF16)
    wide = dot_nn(blocks, choice).reshape(count, 16, width)
    owner = spots_of((count, 16, width), 0)
    column = spots_of((count, 16, width), 2)
    low = owner * small
    return jnp.sum(jnp.where((column >= low) & (column < low + small), wide, 0.0), axis=0)


def frame_spots(shape, axis):
    spot = spots_of(shape, axis)
    row = jnp.zeros(shape, jnp.int32)
    for i in range(1, WIN_H):
        row += (spot >= i * WIN_W).astype(jnp.int32)
    return (row + WIN_H - 1) * OFFS_W + spot - row * WIN_W + WIN_W - 1


def table_columns(table):
    span = OFFS_H * OFFS_W
    table = jnp.concatenate([table[k * span : (k + 1) * span] for k in range(OFFS_T)], axis=1)
    return table.T


def spread_bias(table, spread_ref, line_ref, begin, end):
    span = OFFS_H * OFFS_W
    base = frame_spots((span, FLAT), 1) - spots_of((span, FLAT), 0)

    def one(v, carry):
        for e in range(WIN_W):
            choice = jnp.where(base == v * OFFS_W + e, 1.0, 0.0).astype(BF16)
            wide = dot_nn(table, choice) * LOG2E
            for k in range(OFFS_T):
                line_ref[e, :, k * FLAT : (k + 1) * FLAT] = wide[k * HEADS : (k + 1) * HEADS]
            for h in range(HEADS):
                spread_ref[h, pl.ds(v * WIN_W + e, 1), :] = line_ref[e, h : h + 1, :]
        return carry

    lax.fori_loop(begin, end, one, 0)


def fold_bias(folded_ref, total_ref, line_ref, begin, end):
    base = frame_spots((FLAT, 256), 0) - spots_of((FLAT, 256), 1)

    def one(v, carry):
        total = total_ref[...]
        for e in range(WIN_W):
            choice = jnp.where(base == v * OFFS_W + e, 1.0, 0.0).astype(BF16)
            for h in range(HEADS):
                line_ref[e, h : h + 1, :] = folded_ref[h, pl.ds(v * WIN_W + e, 1), :]
            wide = jnp.concatenate(
                [line_ref[e, :, k * FLAT : (k + 1) * FLAT] for k in range(OFFS_T)], axis=0
            )
            high = wide.astype(BF16)
            total = total + dot_nn(high, choice) + dot_nn((wide - high.astype(F32)).astype(BF16), choice)
        total_ref[...] = total
        return carry

    lax.fori_loop(begin, end, one, 0)


def share_vectors(rows, count, small):
    kinds, width = rows.shape
    lanes, columns = spots_of((128, width), 0), spots_of((128, width), 1)
    choice = ((columns & (small - 1)) == lanes).astype(BF16)
    low = spots_of((count, kinds, width), 0) * small
    column = spots_of((count, kinds, width), 2)
    wide = jnp.where((column >= low) & (column < low + small), rows[None], 0.0)
    wide = wide.reshape(count * kinds, width)
    blocks = 0.0
    for _ in range(3):
        part = wide.astype(BF16)
        blocks = blocks + dot_nt(part, choice)
        wide = wide - part.astype(F32)
    return blocks.reshape(count, kinds, 128)


def front_kernel(setup, *refs):
    windows, depth, direct, plan_one, plan_two, small = setup
    refs = list(refs)
    take = lambda count: [refs.pop(0) for _ in range(count)]
    x_ref, table_ref, keyrow_ref = take(3)
    if direct:
        vector_refs, shards = take(9), take(4)
    else:
        packed_ref, weight_in = take(2)
    qkvt_ref, probs_ref, att_ref, attt_ref, inv_ref, vec_ref, fvec_ref = take(7)
    if direct:
        wholes = take(4)
    spread_ref, line_ref, bias_ref, unit_ref = take(4)
    if direct:
        pack_ref, packed_ref, weight_ref, *sems = take(5)
    head = pl.program_id(0)
    count = D // small

    if direct:
        place = Place(depth)
        base = 0
        first, groups = [], []
        views = [packed_ref, weight_ref] + wholes[1:]
        sources = [pack_ref] + shards
        for plan, into in ((plan_one, None), (plan_two, groups)):
            for index, start, size, y_first in plan:
                columns = pl.ds(start, size)
                view = lambda y, c, z, x, whole=views[index], columns=columns: whole.at[y, c, z, x, :, columns]
                stages = gather_stages(place, sources[index].at[:, columns], view, sems, base, y_first)
                base += gather_slots(depth)
                if into is None:
                    first.append(stages)
                elif into and len(into[-1]) < 2:
                    into[-1].append(stages)
                else:
                    into.append([stages])
        ticks = skewed(groups)
        keep_weight = pltpu.make_async_copy(weight_ref, wholes[0], sems[0].at[base])

    def normalize():
        for w in range(windows):
            unit_ref[w], _ = standardize(x_ref[w].astype(F32))

    @pl.when(head == 0)
    def _():
        if direct:
            pack_ref[...] = pack_vectors([ref[...] for ref in vector_refs]).astype(BF16)
            place.greet()
            run = lambda steps: [step() for step in steps]
            run([stages[0] for stages in first])
            normalize()
            table = table_columns(table_ref[...].astype(F32)).astype(BF16)
            spread_bias(table, spread_ref, line_ref, 0, 1)
            run([stages[1] for stages in first])
            spread_bias(table, spread_ref, line_ref, 1, 3)
            run([stages[2] for stages in first])
            spread_bias(table, spread_ref, line_ref, 3, 6)
            run([stages[3] for stages in first])
            run(ticks[0])
            spread_bias(table, spread_ref, line_ref, 6, 7)
            run([stages[4] for stages in first])
            run(ticks[1])
            keep_weight.start()
            weight = weight_ref[...].reshape(D, 3 * D)
            blocks = packed_ref[...].reshape(count * 16, 128)
        else:
            table = table_columns(table_ref[...].astype(F32)).astype(BF16)
            spread_bias(table, spread_ref, line_ref, 0, WIN_H)
            normalize()
            weight = weight_in[...]
            blocks = packed_ref[...]
        vectors = unpack_vectors(blocks, count, small)
        vec_ref[...] = vectors
        fvec_ref[...] = unpack_vectors(blocks, count, FF // count)[8:9]
        for w in range(windows):
            normed = (unit_ref[w] * vectors[0:1] + vectors[1:2]).astype(BF16)
            for part in range(3):
                got = dot_nn(normed, weight[:, part * D : (part + 1) * D])
                if part == 0:
                    got = (got + vectors[2:3]) * (SCALE * LOG2E)
                if part == 2:
                    got = got + vectors[3:4]
                for piece in range(4):
                    at = part * D + piece * 128
                    qkvt_ref[w, at : at + 128, :] = got[:, piece * 128 : (piece + 1) * 128].T.astype(BF16)

    if direct:
        for at, tick in zip((1, 3, 7, 11, 14), ticks[2:]):

            @pl.when(head == at)
            def _(tick=tick):
                for step in tick:
                    step()

    for u in range(WIN_T):
        start = (WIN_T - 1 - u) * FLAT
        bias_ref[u * FLAT : (u + 1) * FLAT, :] = spread_ref[head, :, start : start + WIN]
    row = pl.multiple_of(head * HDIM, HDIM)
    ones = jnp.ones((16, WIN), BF16)
    for w in range(windows):
        queries = qkvt_ref[w, pl.ds(row, HDIM), :]
        keys = qkvt_ref[w, pl.ds(row + D, HDIM), :]
        values = qkvt_ref[w, pl.ds(row + 2 * D, HDIM), :]
        scores = dot_tn(
            jnp.concatenate([keys, keyrow_ref[w]], axis=0), jnp.concatenate([queries, ones], axis=0)
        )
        scores = scores + bias_ref[...]
        top = jnp.max(scores, axis=0, keepdims=True)
        expo = jnp.exp2(scores - top).astype(BF16)
        probs_ref[w, 0] = expo
        mixed = dot_nn(jnp.concatenate([values, ones], axis=0), expo)
        inverse = 1.0 / mixed[HDIM : HDIM + 1]
        inv_ref[w, pl.ds(head, 1), :] = inverse
        attt_ref[w, pl.ds(row, HDIM), :] = (mixed[:HDIM] * inverse).astype(BF16)

    @pl.when(head == HEADS - 1)
    def _():
        for w in range(windows):
            for part in range(4):
                rows = slice(part * 128, (part + 1) * 128)
                att_ref[w, :, rows] = attt_ref[w, rows, :].astype(F32).T.astype(BF16)
        if direct:
            keep_weight.wait()


def front(inputs, table, keyrow, vectors, weights, packed, depth, direct):
    windows = inputs.shape[0]
    once = lambda shape: pl.BlockSpec(shape, lambda h: (0,) * len(shape), pipeline_mode=pl.Buffered(1))
    anywhere = pl.BlockSpec(memory_space=pl.ANY)
    outs = [
        (once((windows, 3 * D, WIN)), jax.ShapeDtypeStruct((windows, 3 * D, WIN), BF16)),
        (
            pl.BlockSpec((windows, 1, WIN, WIN), lambda h: (0, h, 0, 0)),
            jax.ShapeDtypeStruct((windows, HEADS, WIN, WIN), BF16),
        ),
        (once((windows, WIN, D)), jax.ShapeDtypeStruct((windows, WIN, D), BF16)),
        (once((windows, D, WIN)), jax.ShapeDtypeStruct((windows, D, WIN), BF16)),
        (once((windows, HEADS, WIN)), jax.ShapeDtypeStruct((windows, HEADS, WIN), F32)),
        (once((16, D)), jax.ShapeDtypeStruct((16, D), F32)),
        (once((1, FF)), jax.ShapeDtypeStruct((1, FF), F32)),
    ]
    scratch = [
        pltpu.VMEM((HEADS, FLAT, SPREAD), F32),
        pltpu.VMEM((WIN_W, HEADS, SPREAD), F32),
        pltpu.VMEM((WIN, WIN), F32),
        pltpu.VMEM((windows, WIN, D), F32),
    ]
    args = [inputs, table, keyrow]
    small = vectors[0].shape[1]
    plan_one = ((0, 0, 128, False), (1, 0, 768, False), (1, 768, 768, True))
    plan_two = (
        (2, 0, 256, False),
        (2, 256, 256, True),
        (3, 0, 1024, False),
        (3, 1024, 1024, True),
        (4, 0, 256, False),
        (4, 256, 256, True),
    )
    extra = {}
    if direct:
        args += list(vectors) + list(weights)
        specs = [once(item.shape) for item in args[:-4]] + [anywhere] * 4
        wholes = [jax.ShapeDtypeStruct((2, 2, depth, 2) + item.shape, BF16) for item in weights]
        outs += [(anywhere, whole) for whole in wholes]
        slots = gather_slots(depth) * (len(plan_one) + len(plan_two)) + 1
        scratch += [
            pltpu.VMEM((16, 128), BF16),
            pltpu.VMEM((2, 2, depth, 2, 16, 128), BF16),
            pltpu.VMEM(wholes[0].shape, BF16),
            pltpu.SemaphoreType.DMA((slots,)),
            pltpu.SemaphoreType.DMA((slots,)),
        ]
        extra = dict(collective_id=0, has_side_effects=True)
    else:
        args += [packed, weights[0]]
        specs = [once(item.shape) for item in args]
    return pl.pallas_call(
        functools.partial(front_kernel, (windows, depth, direct, plan_one, plan_two, small)),
        grid=(HEADS,),
        in_specs=specs,
        out_specs=[spec for spec, _ in outs],
        out_shape=[shape for _, shape in outs],
        scratch_shapes=scratch,
        compiler_params=pltpu.CompilerParams(vmem_limit_bytes=60 * MIB, **extra),
        name="front",
    )(*args)


def mlp_kernel(
    x_ref,
    att_ref,
    cot_ref,
    keep_ref,
    proj_ref,
    pshift_ref,
    gain_ref,
    shift_ref,
    fc1_ref,
    fshift1_ref,
    fc2_ref,
    fshift2_ref,
    out_ref,
    rgrad_ref,
    agrad_ref,
    fc1g_ref,
    fc2g_ref,
    projg_ref,
    sums_ref,
    fsum_ref,
    act_ref,
    hid_ref,
    norm_ref,
    gout_ref,
    branch_ref,
):
    rows = x_ref.shape[0]
    block = rows // 2
    pieces = 4
    wide = FF // pieces
    sums_ref[...] = jnp.zeros_like(sums_ref)
    fsum_ref[...] = jnp.zeros_like(fsum_ref)

    def one_block(i, carry):
        at = pl.ds(pl.multiple_of(i * block, 16), block)
        keep = keep_ref[at, :]
        resid = x_ref[at, :].astype(F32) + dot_nn(att_ref[at, :], proj_ref[...]) + pshift_ref[...]
        unit, scale = standardize(resid)
        normed = (unit * gain_ref[...] + shift_ref[...]).astype(BF16)
        norm_ref[at, :] = normed
        gout = cot_ref[at, :].astype(F32) * keep
        gout_low = gout.astype(BF16)
        gout_ref[at, :] = gout_low
        total = resid + fshift2_ref[...]
        grad_two = None
        for part in range(pieces):
            columns = slice(part * wide, (part + 1) * wide)
            hidden = dot_nn(normed, fc1_ref[:, columns]) + fshift1_ref[:, columns]
            active, slope = gelu_parts(hidden)
            active = active.astype(BF16)
            act_ref[at, columns] = active
            total = total + dot_nn(active, fc2_ref[columns, :])
            hgrad = (dot_nt(gout_low, fc2_ref[columns, :]) * slope).astype(BF16)
            hid_ref[at, columns] = hgrad
            fsum_ref[0:1, columns] += jnp.sum(hgrad.astype(F32), axis=0, keepdims=True)
            back = dot_nt(hgrad, fc1_ref[:, columns])
            grad_two = back if grad_two is None else grad_two + back
        out_ref[at, :] = (total * keep).astype(BF16)
        rgrad = gout + norm_backward(grad_two, unit, scale, gain_ref[...])
        rgrad_ref[at, :] = rgrad
        branch = rgrad.astype(BF16)
        branch_ref[at, :] = branch
        agrad_ref[at, :] = dot_nt(branch, proj_ref[...]).astype(BF16)
        sums_ref[0:1, :] += jnp.sum(gout, axis=0, keepdims=True)
        sums_ref[1:2, :] += jnp.sum(grad_two * unit, axis=0, keepdims=True)
        sums_ref[2:3, :] += jnp.sum(grad_two, axis=0, keepdims=True)
        sums_ref[3:4, :] += jnp.sum(branch.astype(F32), axis=0, keepdims=True)
        return carry

    lax.fori_loop(0, 2, one_block, 0)
    projg_ref[...] = dot_tn(att_ref[...], branch_ref[...]).astype(BF16)
    for part in range(pieces):
        columns = slice(part * wide, (part + 1) * wide)
        fc2g_ref[columns, :] = dot_tn(act_ref[:, columns], gout_ref[...]).astype(BF16)
        fc1g_ref[:, columns] = dot_tn(norm_ref[...], hid_ref[:, columns]).astype(BF16)


def feed_forward(x_rows, att_rows, cot_rows, keep_rows, proj, pshift, gain, shift, fc1, fshift1, fc2, fshift2):
    rows = x_rows.shape[0]
    vmem = pl.BlockSpec(memory_space=pltpu.VMEM)
    return pl.pallas_call(
        mlp_kernel,
        in_specs=[vmem] * 12,
        out_specs=[vmem] * 8,
        out_shape=[
            jax.ShapeDtypeStruct((rows, D), BF16),
            jax.ShapeDtypeStruct((rows, D), F32),
            jax.ShapeDtypeStruct((rows, D), BF16),
            jax.ShapeDtypeStruct((D, FF), BF16),
            jax.ShapeDtypeStruct((FF, D), BF16),
            jax.ShapeDtypeStruct((D, D), BF16),
            jax.ShapeDtypeStruct((8, D), F32),
            jax.ShapeDtypeStruct((8, FF), F32),
        ],
        scratch_shapes=[
            pltpu.VMEM((rows, FF), BF16),
            pltpu.VMEM((rows, FF), BF16),
            pltpu.VMEM((rows, D), BF16),
            pltpu.VMEM((rows, D), BF16),
            pltpu.VMEM((rows, D), BF16),
        ],
        compiler_params=pltpu.CompilerParams(vmem_limit_bytes=62 * MIB),
        name="feed_forward",
    )(x_rows, att_rows, cot_rows, keep_rows, proj, pshift, gain, shift, fc1, fshift1, fc2, fshift2)


LATE = ((0, 768, False), (768, 768, True))
EARLY = (
    (2, 0, 256, False),
    (2, 256, 256, True),
    (1, 0, 1024, False),
    (1, 1024, 1024, True),
    (0, 0, 256, False),
    (0, 256, 256, True),
)


def back_kernel(setup, *refs):
    windows, depth, direct, small = setup
    refs = list(refs)
    take = lambda count: [refs.pop(0) for _ in range(count)]
    qkvt_ref, attt_ref, agrad_ref, inv_ref, probs_ref, x_ref, rgrad_ref, weight_ref = take(8)
    vec_ref, sums_ref, fsum_ref = take(3)
    if direct:
        grads = take(3)
    igrad_ref, table_ref = take(2)
    if direct:
        vec_own, qkv_own, *owns = take(5)
    else:
        qkv_work, vec_work = take(2)
    dot_ref, dqkvt_ref, sum_ref, folded_ref, line_ref, total_ref, dq_ref, norm_ref, acc_ref = take(9)
    if direct:
        qkv_work, vec_work, table_work, table_own, table_full, *works = take(8)
        sems = (refs[-2], refs[-1])
        helds = refs[:-2]
    head = pl.program_id(0)
    count = D // small

    if direct:
        place = Place(depth)
        base, spot = len(works) + 1, 0

        def pieces(work, own, columns, x_first):
            nonlocal base, spot
            view = work if columns is None else work.at[:, :, :, :, :, columns]
            stages = scatter_stages(
                place,
                view,
                helds[spot : spot + 4],
                sems,
                base,
                x_first,
                own if columns is None else own.at[:, columns],
            )
            base += scatter_slots(depth)
            spot += 4
            return stages

        early = [pieces(works[i], owns[i], pl.ds(start, size), x_first) for i, start, size, x_first in EARLY]
        ticks = skewed([early[i : i + 2] for i in range(0, len(early), 2)])
        late = [pieces(qkv_work, qkv_own, pl.ds(start, size), x_first) for start, size, x_first in LATE]
        table_stages = pieces(table_work, table_own, None, False)
        vec_stages = pieces(vec_work, vec_own, None, True)
        collect = gather_stages(
            place, table_own, lambda y, c, z, x: table_full.at[y, c, z, x], sems, base, True
        )
        loads = [pltpu.make_async_copy(grads[i], works[i], sems[0].at[i]) for i in range(len(works))]
    run = lambda steps: [step() for step in steps]

    @pl.when(head == 0)
    def _():
        if direct:
            place.greet()
            for load in loads:
                load.start()
        for w in range(windows):
            for part in range(4):
                rows = slice(part * 128, (part + 1) * 128)
                dot_ref[w, rows, :] = agrad_ref[w, :, rows].astype(F32).T.astype(BF16)

    if direct:
        for at, tick in zip((1, 2, 4, 7, 9, 11, 14), ticks):

            @pl.when(head == at)
            def _(at=at, tick=tick):
                if at == 1:
                    for load in loads:
                        load.wait()
                run(tick)

    row = pl.multiple_of(head * HDIM, HDIM)
    ones = jnp.ones((16, WIN), BF16)
    order = spots_of((16, WIN), 0)
    for w in range(windows):
        queries = qkvt_ref[w, pl.ds(row, HDIM), :]
        keys = qkvt_ref[w, pl.ds(row + D, HDIM), :]
        values = qkvt_ref[w, pl.ds(row + 2 * D, HDIM), :]
        expo = probs_ref[w, 0]
        grad = dot_ref[w, pl.ds(row, HDIM), :].astype(F32) * inv_ref[w, pl.ds(head, 1), :]
        inner = -jnp.sum(grad * attt_ref[w, pl.ds(row, HDIM), :].astype(F32), axis=0, keepdims=True)
        high = inner.astype(BF16).astype(F32)
        middle = (inner - high).astype(BF16).astype(F32)
        lowest = inner - high - middle
        extra = jnp.where(
            order == 0, high, jnp.where(order == 1, middle, jnp.where(order == 2, lowest, 0.0))
        ).astype(BF16)
        grad = grad.astype(BF16)
        probs_grad = dot_tn(
            jnp.concatenate([values, ones], axis=0), jnp.concatenate([grad, extra], axis=0)
        )
        scores_grad = expo.astype(F32) * probs_grad
        low = scores_grad.astype(BF16)
        if w == 0:
            sum_ref[...] = scores_grad
        else:
            sum_ref[...] += scores_grad
        dqkvt_ref[w, pl.ds(row, HDIM), :] = (dot_nn(keys, low) * SCALE).astype(BF16)
        dqkvt_ref[w, pl.ds(row + D, HDIM), :] = (dot_nt(queries, low) * LN2).astype(BF16)
        dqkvt_ref[w, pl.ds(row + 2 * D, HDIM), :] = dot_nt(grad, expo).astype(BF16)

    folded_ref[head] = jnp.zeros((FLAT, SPREAD), F32)
    for u in range(WIN_T):
        start = (WIN_T - 1 - u) * FLAT
        folded_ref[head, :, start : start + WIN] += sum_ref[u * FLAT : (u + 1) * FLAT, :]

    @pl.when(head == HEADS - 1)
    def _():
        gain, shift = vec_ref[0:1], vec_ref[1:2]
        column_sums = [0.0] * 12
        for w in range(windows):
            unit, _ = standardize(x_ref[w].astype(F32))
            norm_ref[w] = (unit * gain + shift).astype(BF16)
            for part in range(12):
                rows = slice(part * 128, (part + 1) * 128)
                low = dqkvt_ref[w, rows, :].astype(F32).T
                dq_ref[w, :, rows] = low.astype(BF16)
                column_sums[part] = column_sums[part] + jnp.sum(low, axis=0, keepdims=True)
        total_ref[...] = jnp.zeros_like(total_ref)

        def weight_grad(start, size):
            columns = slice(start, start + size)
            for w in range(windows):
                got = dot_tn(norm_ref[w], dq_ref[w, :, columns])
                if w == 0:
                    acc_ref[:, :size] = got
                else:
                    acc_ref[:, :size] += got
            got = acc_ref[:, :size].astype(BF16)
            if direct:
                qkv_work[:, :, :, :, :, columns] = got.reshape(2, 2, depth, 2, small, size)
            else:
                qkv_work[:, columns] = got

        gain_sum, shift_sum = 0.0, 0.0

        def input_grad(w):
            nonlocal gain_sum, shift_sum
            unit, scale = standardize(x_ref[w].astype(F32))
            grad = dot_nt(dq_ref[w], weight_ref[...])
            igrad_ref[w] = (rgrad_ref[w] + norm_backward(grad, unit, scale, gain)).astype(BF16)
            gain_sum = gain_sum + jnp.sum(grad * unit, axis=0, keepdims=True)
            shift_sum = shift_sum + jnp.sum(grad, axis=0, keepdims=True)

        def vector_block():
            rows = [
                gain_sum,
                shift_sum,
                jnp.concatenate(column_sums[:4], axis=1),
                jnp.concatenate(column_sums[8:], axis=1),
                sums_ref[3:4],
                sums_ref[1:2],
                sums_ref[2:3],
                sums_ref[0:1],
                jnp.zeros((8, D), F32),
            ]
            block = share_vectors(jnp.concatenate(rows, axis=0), count, small)
            last = share_vectors(fsum_ref[0:1], count, FF // count)
            return jnp.where(spots_of((count, 16, 128), 1) == 8, last, block)

        fold = lambda begin, end: fold_bias(folded_ref, total_ref, line_ref, begin, end)
        if direct:
            weight_grad(0, 768)
            late[0][0]()
            weight_grad(768, 768)
            late[1][0]()
            late[0][1]()
            fold(0, 1)
            late[1][1]()
            fold(1, 3)
            late[0][2]()
            late[1][2]()
            fold(3, 7)
            total = jnp.concatenate([total_ref[...], jnp.zeros((256 - OFFS_T * HEADS, 256), F32)], axis=0)
            table_work[...] = total.reshape(table_work.shape)
            table_stages[0]()
            late[0][3]()
            late[1][3]()
            input_grad(0)
            table_stages[1]()
            input_grad(1)
            table_stages[2]()
            late[0][4]()
            late[1][4]()
            input_grad(2)
            table_stages[3]()
            input_grad(3)
            vec_work[...] = vector_block().reshape(vec_work.shape)
            vec_stages[0]()
            table_stages[4]()
            collect[0]()
            for k in range(1, 5):
                vec_stages[k]()
                collect[k]()
            total = table_full[...].reshape(256, 256)
        else:
            weight_grad(0, 768)
            weight_grad(768, 768)
            fold(0, WIN_H)
            for w in range(windows):
                input_grad(w)
            vec_work[...] = vector_block()
            total = total_ref[...]
        span = OFFS_H * OFFS_W
        for k in range(OFFS_T):
            table_ref[k * span : (k + 1) * span, :] = total[k * HEADS : (k + 1) * HEADS].T[:span]


def back(qkvt, attt, agrad, inverse, probs, inputs, rgrad, weight, vectors, sums, fsum, grads, depth, direct):
    windows = qkvt.shape[0]
    count = 4 * depth if direct else lax.axis_size("dp") * lax.axis_size("fsdp")
    count = 8 * depth if direct else count
    small = D // count
    once = lambda shape: pl.BlockSpec(shape, lambda h: (0,) * len(shape), pipeline_mode=pl.Buffered(1))
    anywhere = pl.BlockSpec(memory_space=pl.ANY)
    args = [qkvt, attt, agrad, inverse, probs, inputs, rgrad, weight, vectors, sums, fsum]
    specs = [once(item.shape) for item in args]
    specs[4] = pl.BlockSpec((windows, 1, WIN, WIN), lambda h: (0, h, 0, 0))
    shapes = [
        jax.ShapeDtypeStruct(inputs.shape, BF16),
        jax.ShapeDtypeStruct((OFFS_T * OFFS_H * OFFS_W, HEADS), F32),
    ]
    scratch = [
        pltpu.VMEM((windows, D, WIN), BF16),
        pltpu.VMEM((windows, 3 * D, WIN), BF16),
        pltpu.VMEM((WIN, WIN), F32),
        pltpu.VMEM((HEADS, FLAT, SPREAD), F32),
        pltpu.VMEM((WIN_W, HEADS, SPREAD), F32),
        pltpu.VMEM((OFFS_T * HEADS, 256), F32),
        pltpu.VMEM((windows, WIN, 3 * D), BF16),
        pltpu.VMEM((windows, WIN, D), BF16),
        pltpu.VMEM((D, 768), F32),
    ]
    extra = {}
    if direct:
        lead = (2, 2, depth, 2)
        rows = 256 // count
        views = [item.reshape(lead + (-1, item.shape[1])) for item in grads]
        args += views
        specs += [anywhere] * len(views)
        shapes += [
            jax.ShapeDtypeStruct((16, 128), F32),
            jax.ShapeDtypeStruct((small, 3 * D), F32),
        ] + [jax.ShapeDtypeStruct(item.shape[-2:], F32) for item in views]
        scratch += [
            pltpu.VMEM(lead + (small, 3 * D), BF16),
            pltpu.VMEM(lead + (16, 128), F32),
            pltpu.VMEM(lead + (rows, 256), F32),
            pltpu.VMEM((rows, 256), F32),
            pltpu.VMEM(lead + (rows, 256), F32),
        ] + [pltpu.VMEM(item.shape, BF16) for item in views]
        for i, _, size, x_first in EARLY:
            scratch += held_shapes(depth, views[i].shape[-2], size, BF16, x_first)
        for _, size, x_first in LATE:
            scratch += held_shapes(depth, small, size, BF16, x_first)
        scratch += held_shapes(depth, rows, 256, F32, False) + held_shapes(depth, 16, 128, F32, True)
        slots = len(views) + 1 + scatter_slots(depth) * (len(EARLY) + len(LATE) + 2) + gather_slots(depth)
        scratch += [pltpu.SemaphoreType.DMA((slots,)), pltpu.SemaphoreType.DMA((slots,))]
        extra = dict(collective_id=1, has_side_effects=True)
    else:
        shapes += [
            jax.ShapeDtypeStruct((D, 3 * D), BF16),
            jax.ShapeDtypeStruct((count, 16, 128), F32),
        ]
    return pl.pallas_call(
        functools.partial(back_kernel, (windows, depth, direct, small)),
        grid=(HEADS,),
        in_specs=specs,
        out_specs=[once(item.shape) for item in shapes],
        out_shape=shapes,
        scratch_shapes=scratch,
        compiler_params=pltpu.CompilerParams(vmem_limit_bytes=63 * MIB, **extra),
        name="back",
    )(*args)


def valid_mask(extents):
    spots = np.arange(WIN)
    depth, height, across = spots // FLAT, spots // WIN_W % WIN_H, spots % WIN_W
    return (
        (depth[None, :] < extents[:, 0:1])
        & (height[None, :] < extents[:, 1:2])
        & (across[None, :] < extents[:, 2:3])
    ).astype(F32)


def gathered(value):
    return lax.all_gather(value, AXES, axis=0, tiled=True)


def scattered(value):
    return lax.psum_scatter(value, AXES, scatter_dimension=0, tiled=True)


def per_device(
    inputs,
    extents,
    cotangent,
    ln1_gain,
    ln1_shift,
    qkv_weight,
    query_bias,
    value_bias,
    bias_table,
    proj_weight,
    proj_shift,
    ln2_gain,
    ln2_shift,
    fc1_weight,
    fc1_shift,
    fc2_weight,
    fc2_shift,
):
    windows = inputs.shape[0]
    rows = windows * WIN
    small = ln1_gain.shape[0]
    count = D // small
    depth = lax.axis_size("fsdp") // 2
    direct = small % 16 == 0 and lax.axis_size("dp") == 4
    vectors = [
        item[None]
        for item in (
            ln1_gain,
            ln1_shift,
            query_bias,
            value_bias,
            proj_shift,
            ln2_gain,
            ln2_shift,
            fc2_shift,
            fc1_shift,
        )
    ]
    weights = (qkv_weight, proj_weight, fc1_weight, fc2_weight)
    packed = None
    if not direct:
        packed = jnp.concatenate([jnp.pad(item, ((0, 0), (0, 128 - item.shape[1]))) for item in vectors])
        packed = gathered(jnp.pad(packed, ((0, 16 - len(vectors)), (0, 0))))
        weights = [gathered(item) for item in weights]
    keep = valid_mask(extents)
    keep_rows = keep.reshape(rows, 1)
    keyrow = jnp.concatenate(
        [((keep - 1.0) * 1e30)[:, None, :], jnp.zeros((windows, 15, WIN), F32)], axis=1
    ).astype(BF16)
    x_rows = inputs.reshape(rows, D)
    qkvt, probs, att, attt, inverse, full_vectors, fshift1, *wholes = front(
        inputs, bias_table, keyrow, vectors, weights, packed, depth, direct
    )
    if direct:
        weights = [item.reshape(-1, item.shape[-1]) for item in wholes]
    qkv_full, proj_full, fc1_full, fc2_full = weights
    gain1, shift1, _, _, pshift, gain2, shift2, fshift2 = [full_vectors[i : i + 1] for i in range(8)]
    output, rgrad, agrad, fc1_grad, fc2_grad, proj_grad, sums, fsum = feed_forward(
        x_rows,
        att.reshape(rows, D),
        cotangent.reshape(rows, D),
        keep_rows,
        proj_full,
        pshift,
        gain2,
        shift2,
        fc1_full,
        fshift1,
        fc2_full,
        fshift2,
    )
    matrices = (proj_grad, fc1_grad, fc2_grad)
    input_grad, table_grad, *rest = back(
        qkvt,
        attt,
        agrad.reshape(windows, WIN, D),
        inverse,
        probs,
        inputs,
        rgrad.reshape(windows, WIN, D),
        qkv_full,
        full_vectors,
        sums,
        fsum,
        matrices,
        depth,
        direct,
    )
    if direct:
        vector_own, qkv_own, proj_own, fc1_own, fc2_own = rest
    else:
        qkv_own, proj_own, fc1_own, fc2_own = [
            scattered(item.astype(F32)) for item in (rest[0],) + matrices
        ]
        vector_own = scattered(rest[1])[0]
        table_grad = lax.psum(table_grad, AXES)
    owned_vectors = jnp.concatenate([vector_own[i, :small] for i in range(8)] + [vector_own[8, : FF // count]])
    owned = [owned_vectors[i * small : (i + 1) * small] for i in range(8)]
    return (
        output.reshape(inputs.shape),
        input_grad.reshape(inputs.shape),
        owned[0],
        owned[1],
        qkv_own,
        owned[2],
        owned[3],
        table_grad,
        proj_own,
        owned[4],
        owned[5],
        owned[6],
        fc1_own,
        owned_vectors[8 * small :],
        fc2_own,
        owned[7],
    )


def solution(mesh):
    rows = P(AXES, None)
    vector = P(AXES)
    block = P(AXES, None, None)
    in_specs = (
        block,
        rows,
        block,
        vector,
        vector,
        rows,
        vector,
        vector,
        P(),
        rows,
        vector,
        vector,
        vector,
        rows,
        vector,
        rows,
        vector,
    )
    out_specs = (
        block,
        block,
        vector,
        vector,
        rows,
        vector,
        vector,
        P(),
        rows,
        vector,
        vector,
        vector,
        rows,
        vector,
        rows,
        vector,
    )
    return jax.shard_map(
        per_device, mesh=mesh, in_specs=in_specs, out_specs=out_specs, check_vma=False
    )
```

```python
import functools
import math

import jax
import jax.numpy as jnp
import numpy as np
from jax import lax
from jax.experimental import pallas as pl
from jax.experimental.pallas import tpu as pltpu
from jax.sharding import PartitionSpec as P

D = 512
HEADS = 16
HDIM = 32
FF = 2048
WIN_T = 8
WIN_H = 7
WIN_W = 7
WIN = WIN_T * WIN_H * WIN_W
FLAT = WIN_H * WIN_W
OFFS_T = 2 * WIN_T - 1
OFFS_H = 2 * WIN_H - 1
OFFS_W = 2 * WIN_W - 1
SPREAD = OFFS_T * FLAT
LANES = 512
HALF = HEADS // 2
HCOLS = HALF * HDIM
HWIDE = 3 * HCOLS
EPS = 1e-05
LOG2E = math.log2(math.e)
LN2 = math.log(2.0)
SCALE = HDIM ** (-0.5)
AXES = ("dp", "fsdp")
BF16 = jnp.bfloat16
F32 = jnp.float32
MIB = 2**20


def dot(left, right, left_dim, right_dim):
    return lax.dot_general(
        left, right, (((left_dim,), (right_dim,)), ((), ())), preferred_element_type=F32
    )


def dot_nn(left, right):
    return dot(left, right, 1, 0)


def dot_nt(left, right):
    return dot(left, right, 1, 1)


def dot_tn(left, right):
    return dot(left, right, 0, 0)


def standardize(rows):
    average = jnp.mean(rows, axis=-1, keepdims=True)
    centered = rows - average
    variance = jnp.mean(centered * centered, axis=-1, keepdims=True)
    scale = lax.rsqrt(variance + EPS)
    return centered * scale, scale


def norm_backward(grad, unit, scale, gain):
    scaled = grad * gain
    first = jnp.mean(scaled, axis=-1, keepdims=True)
    second = jnp.mean(scaled * unit, axis=-1, keepdims=True)
    return (scaled - first - unit * second) * scale


def gelu_parts(hidden):
    below = 0.5 * lax.erf(hidden * (0.5**0.5)) + 0.5
    bell = jnp.exp2(hidden * hidden * (-0.5 * LOG2E)) * (1.0 / math.sqrt(2 * math.pi))
    return hidden * below, below + hidden * bell


class Place:
    def __init__(self, depth):
        dp, fsdp = lax.axis_index("dp"), lax.axis_index("fsdp")
        self.depth = depth
        self.y, self.c = dp // 2, dp % 2
        self.z, self.x = fsdp // 2, fsdp % 2
        self.core = (self.y * 2 + 1 - self.c, fsdp)
        self.across_x = (dp, self.z * 2 + 1 - self.x)
        self.across_y = ((1 - self.y) * 2 + self.c, fsdp)
        self.along_z = [(dp, ((self.z + j) % depth) * 2 + self.x) for j in range(1, depth)]

    def greet(self):
        barrier = pltpu.get_barrier_semaphore()
        partners = [self.core, self.across_x, self.across_y] + self.along_z
        for partner in partners:
            pl.semaphore_signal(barrier, inc=1, device_id=partner, device_id_type=pl.DeviceIdType.MESH)
        pl.semaphore_wait(barrier, len(partners))


def send(source, target, sems, slot, device):
    return pltpu.make_async_remote_copy(
        src_ref=source,
        dst_ref=target,
        send_sem=sems[0].at[slot],
        recv_sem=sems[1].at[slot],
        device_id=device,
        device_id_type=pl.DeviceIdType.MESH,
    )


def gather_slots(depth):
    return depth + 5


def gather_stages(place, own, full, sems, base, y_first):
    y, c, z, x, depth = place.y, place.c, place.z, place.x, place.depth
    every = slice(None)
    here = full(y, c, z, x)
    local = pltpu.make_async_copy(own, here, sems[0].at[base])
    along = [send(own, here, sems, base + j, place.along_z[j - 1]) for j in range(1, depth)]
    column = full(y, c, every, x)
    if y_first:
        first = send(column, column, sems, base + depth, place.across_y)
        both = full(every, c, every, x)
        second = send(both, both, sems, base + depth + 1, place.across_x)
        one = full(1 - y, c, every, x)
        two = full(every, c, every, 1 - x)
    else:
        first = send(column, column, sems, base + depth, place.across_x)
        both = full(y, c, every, every)
        second = send(both, both, sems, base + depth + 1, place.across_y)
        one = full(y, c, every, 1 - x)
        two = full(1 - y, c, every, every)
    shares = [
        send(part, part, sems, base + depth + 2 + k, place.core) for k, part in enumerate((column, one, two))
    ]

    def begin():
        local.start()
        for copy in along:
            copy.start()

    def turn():
        local.wait()
        for copy in along:
            copy.wait_recv()
        first.start()
        shares[0].start()

    def cross():
        first.wait_recv()
        second.start()
        shares[1].start()

    def share():
        second.wait_recv()
        shares[2].start()

    def finish():
        for copy in shares:
            copy.wait()
        for copy in along + [first, second]:
            copy.wait_send()

    return [begin, turn, cross, share, finish]


def scatter_slots(depth):
    return depth + 2


def add_into(target, index, extra):
    target[index] = (target[index].astype(F32) + extra.astype(F32)).astype(target.dtype)


def scatter_stages(place, parts, held, sems, base, x_first, write):
    y, c, z, x, depth = place.y, place.c, place.z, place.x, place.depth
    every = slice(None)
    from_core, from_first, from_second, from_z = held
    share = send(parts.at[:, 1 - c], from_core, sems, base, place.core)
    if x_first:
        first = send(parts.at[:, c, :, 1 - x], from_first, sems, base + 1, place.across_x)
        second = send(parts.at[1 - y, c, :, x], from_second, sems, base + 2, place.across_y)
    else:
        first = send(parts.at[1 - y, c], from_first, sems, base + 1, place.across_y)
        second = send(parts.at[y, c, :, 1 - x], from_second, sems, base + 2, place.across_x)
    along = [
        send(
            parts.at[y, c, (z + j) % depth, x],
            from_z.at[j - 1],
            sems,
            base + 2 + j,
            place.along_z[j - 1],
        )
        for j in range(1, depth)
    ]

    def begin():
        share.start()

    def cross():
        share.wait_recv()
        for yy in range(2):
            add_into(parts, (yy, c), from_core[yy])
        first.start()

    def turn():
        first.wait_recv()
        if x_first:
            for yy in range(2):
                for zz in range(depth):
                    add_into(parts, (yy, c, zz, x), from_first[yy, zz])
        else:
            add_into(parts, (y, c), from_first[...])
        second.start()

    def spread():
        second.wait_recv()
        for zz in range(depth):
            add_into(parts, (y, c, zz, x), from_second[zz])
        for copy in along:
            copy.start()

    def finish():
        for copy in along:
            copy.wait_recv()
        total = parts[y, c, z, x].astype(F32)
        for j in range(depth - 1):
            total = total + from_z[j].astype(F32)
        write(total)
        for copy in along + [share, first, second]:
            copy.wait_send()

    return [begin, cross, turn, spread, finish]


def held_shapes(depth, rows, columns, dtype, x_first):
    first = (2, depth, rows, columns) if x_first else (depth, 2, rows, columns)
    return [
        pltpu.VMEM((2, depth, 2, rows, columns), dtype),
        pltpu.VMEM(first, dtype),
        pltpu.VMEM((depth, rows, columns), dtype),
        pltpu.VMEM((depth - 1, rows, columns), dtype),
    ]


def spots_of(shape, axis):
    return lax.broadcasted_iota(jnp.int32, shape, axis)


def pack_vectors(vectors):
    rows = spots_of((16, 128), 0)
    block = jnp.zeros((16, 128), F32)
    for i, vector in enumerate(vectors):
        vector = vector.astype(F32)
        if vector.shape[1] < 128:
            vector = jnp.concatenate([vector, jnp.zeros((1, 128 - vector.shape[1]), F32)], axis=1)
        block = jnp.where(rows == i, vector, block)
    return block


def unpack_vectors(blocks, count, small):
    width = count * small
    lanes, columns = spots_of((128, width), 0), spots_of((128, width), 1)
    choice = ((columns & (small - 1)) == lanes).astype(BF16)
    wide = dot_nn(blocks, choice).reshape(count, 16, width)
    owner = spots_of((count, 16, width), 0)
    column = spots_of((count, 16, width), 2)
    low = owner * small
    return jnp.sum(jnp.where((column >= low) & (column < low + small), wide, 0.0), axis=0)


def frame_spots(shape, axis):
    spot = spots_of(shape, axis)
    row = jnp.zeros(shape, jnp.int32)
    for i in range(1, WIN_H):
        row += (spot >= i * WIN_W).astype(jnp.int32)
    return (row + WIN_H - 1) * OFFS_W + spot - row * WIN_W + WIN_W - 1


def table_columns(table):
    span = OFFS_H * OFFS_W
    table = jnp.concatenate([table[k * span : (k + 1) * span] for k in range(OFFS_T)], axis=1)
    return table.T


def spread_bias(table, spread_ref, line_ref, begin, end):
    span = OFFS_H * OFFS_W
    base = frame_spots((span, FLAT), 1) - spots_of((span, FLAT), 0)

    def one(v, carry):
        for e in range(WIN_W):
            choice = jnp.where(base == v * OFFS_W + e, 1.0, 0.0).astype(BF16)
            wide = dot_nn(table, choice) * LOG2E
            for k in range(OFFS_T):
                line_ref[e, :, k * FLAT : (k + 1) * FLAT] = wide[k * HEADS : (k + 1) * HEADS]
            for h in range(HEADS):
                spread_ref[h, pl.ds(v * WIN_W + e, 1), :] = line_ref[e, h : h + 1, :]
        return carry

    lax.fori_loop(begin, end, one, 0)


def fold_bias(folded_ref, total_ref, line_ref, half):
    base = frame_spots((FLAT, 256), 0) - spots_of((FLAT, 256), 1)

    def one(v, total):
        for e in range(WIN_W):
            choice = jnp.where(base == v * OFFS_W + e, 1.0, 0.0).astype(BF16)
            for h in range(HALF):
                line_ref[e, h : h + 1, :] = folded_ref[half * HALF + h, pl.ds(v * WIN_W + e, 1), :]
            wide = jnp.concatenate(
                [line_ref[e, :, k * FLAT : (k + 1) * FLAT] for k in range(OFFS_T)], axis=0
            )
            high = wide.astype(BF16)
            total = total + dot_nn(high, choice) + dot_nn((wide - high.astype(F32)).astype(BF16), choice)
        return total

    total = lax.fori_loop(0, WIN_H, one, jnp.zeros((OFFS_T * HALF, 256), F32))
    total_ref[half, : OFFS_T * HALF] = total


def share_vectors(rows, count, small):
    kinds, width = rows.shape
    lanes, columns = spots_of((128, width), 0), spots_of((128, width), 1)
    choice = ((columns & (small - 1)) == lanes).astype(BF16)
    low = spots_of((count, kinds, width), 0) * small
    column = spots_of((count, kinds, width), 2)
    wide = jnp.where((column >= low) & (column < low + small), rows[None], 0.0)
    wide = wide.reshape(count * kinds, width)
    blocks = 0.0
    for _ in range(3):
        part = wide.astype(BF16)
        blocks = blocks + dot_nt(part, choice)
        wide = wide - part.astype(F32)
    return blocks.reshape(count, kinds, 128)


QKV_PIECES = ((1, 0, 384, False), (1, 384, 384, True), (1, 768, 384, False), (1, 1152, 384, True))
OTHER_PIECES = (
    (2, 0, 256, False),
    (2, 256, 256, True),
    (3, 0, 1024, False),
    (3, 1024, 1024, True),
    (4, 0, 256, False),
    (4, 256, 256, True),
)


def head_row(head):
    return pl.multiple_of(head // HALF * HWIDE + head % HALF * HDIM, HDIM)


def front_kernel(setup, *refs):
    windows, depth, direct, small = setup
    refs = list(refs)
    take = lambda count: [refs.pop(0) for _ in range(count)]
    x_ref, table_ref, keyrow_ref = take(3)
    if direct:
        vector_refs, shards = take(9), take(4)
    else:
        packed_ref, weight_in = take(2)
    qkvt_ref, probs_ref, att_ref, attt_ref, inv_ref, vec_ref, fvec_ref = take(7)
    if direct:
        wholes = take(4)
    spread_ref, line_ref, bias_ref, norm_ref = take(4)
    if direct:
        pack_ref, own_ref, packed_ref, weight_ref, *sems = take(6)
    head = pl.program_id(0)
    count = D // small
    run = lambda stage, *lists: [stages[stage]() for stages in lists]

    if direct:
        place = Place(depth)
        views = [packed_ref, weight_ref] + wholes[1:]
        sources = [pack_ref, own_ref] + shards[1:]
        lists = []
        for index, start, size, y_first in ((0, 0, 128, False),) + QKV_PIECES + OTHER_PIECES:
            columns = pl.ds(start, size)
            view = lambda y, c, z, x, whole=views[index], columns=columns: whole.at[y, c, z, x, :, columns]
            base = gather_slots(depth) * len(lists)
            lists.append(gather_stages(place, sources[index].at[:, columns], view, sems, base, y_first))
        one, two, proj, fc1, fc2 = lists[:3], lists[3:5], lists[5:7], lists[7:9], lists[9:]
        keep_weight = pltpu.make_async_copy(weight_ref, wholes[0], sems[0].at[gather_slots(depth) * len(lists)])

    def project(half, weight, vectors):
        for w in range(windows):
            for part in range(3):
                start = half * HWIDE + part * HCOLS
                got = dot_nn(norm_ref[w], weight[:, start : start + HCOLS])
                if part == 0:
                    got = (got + vectors[2:3, half * HCOLS : (half + 1) * HCOLS]) * (SCALE * LOG2E)
                if part == 2:
                    got = got + vectors[3:4, half * HCOLS : (half + 1) * HCOLS]
                for piece in range(HCOLS // 128):
                    at = start + piece * 128
                    qkvt_ref[w, at : at + 128, :WIN] = got[:, piece * 128 : (piece + 1) * 128].T.astype(BF16)

    def normalize(vectors):
        for w in range(windows):
            unit, _ = standardize(x_ref[w].astype(F32))
            norm_ref[w] = (unit * vectors[0:1] + vectors[1:2]).astype(BF16)

    @pl.when(head == 0)
    def _():
        spread = lambda begin, end: spread_bias(table, spread_ref, line_ref, begin, end)
        if direct:
            pack_ref[...] = pack_vectors([ref[...] for ref in vector_refs]).astype(BF16)
            for half in range(2):
                for part in range(3):
                    start = half * HWIDE + part * HCOLS
                    source = part * D + half * HCOLS
                    own_ref[:, start : start + HCOLS] = shards[0][:, source : source + HCOLS]
            place.greet()
            run(0, *one)
            table = table_columns(table_ref[...].astype(F32)).astype(BF16)
            run(0, *two)
            spread(0, 3)
            run(1, *one)
            spread(3, 6)
            run(2, *one)
            run(1, *two)
            run(0, *proj, *fc1)
            spread(6, 7)
            run(3, *one)
            run(2, *two)
            run(0, *fc2)
            run(4, *one)
            blocks = packed_ref[...].reshape(count * 16, 128)
            vectors = unpack_vectors(blocks, count, small)
            normalize(vectors)
            project(0, weight_ref[:, :, :, :, :, :HWIDE].reshape(D, HWIDE), vectors)
            run(3, *two)
            run(1, *proj, *fc1)
            run(4, *two)
            weight = weight_ref[...].reshape(D, 3 * D)
            keep_weight.start()
            project(1, weight, vectors)
            run(1, *fc2)
        else:
            table = table_columns(table_ref[...].astype(F32)).astype(BF16)
            spread(0, WIN_H)
            blocks = packed_ref[...]
            vectors = unpack_vectors(blocks, count, small)
            normalize(vectors)
            for half in range(2):
                project(half, weight_in[...], vectors)
        vec_ref[...] = vectors
        fvec_ref[...] = unpack_vectors(blocks, count, FF // count)[8:9]

    if direct:
        steps = (
            (2, (2, proj + fc1)),
            (4, (2, fc2)),
            (11, (3, proj + fc1)),
            (15, (3, fc2)),
        )
        for at, (stage, group) in steps:

            @pl.when(head == at)
            def _(stage=stage, group=group):
                run(stage, *group)

    for u in range(WIN_T):
        start = (WIN_T - 1 - u) * FLAT
        bias_ref[u * FLAT : (u + 1) * FLAT, :] = spread_ref[head, :, start : start + WIN]
    row = head_row(head)
    ones = jnp.ones((16, WIN), BF16)
    scores = []
    for w in range(windows):
        queries = qkvt_ref[w, pl.ds(row, HDIM), :WIN]
        keys = qkvt_ref[w, pl.ds(row + HCOLS, HDIM), :WIN]
        scores.append(
            dot_tn(
                jnp.concatenate([keys, keyrow_ref[w]], axis=0), jnp.concatenate([queries, ones], axis=0)
            )
        )
    expos = []
    for w in range(windows):
        score = scores[w] + bias_ref[...]
        top = jnp.max(score, axis=0, keepdims=True)
        expos.append(jnp.exp2(score - top).astype(BF16))
        probs_ref[w, 0, :, :WIN] = expos[w]
    for w in range(windows):
        values = qkvt_ref[w, pl.ds(row + 2 * HCOLS, HDIM), :WIN]
        mixed = dot_nn(jnp.concatenate([values, ones], axis=0), expos[w])
        inverse = 1.0 / mixed[HDIM : HDIM + 1]
        inv_ref[w, pl.ds(head, 1), :WIN] = inverse
        attt_ref[w, pl.ds(pl.multiple_of(head * HDIM, HDIM), HDIM), :WIN] = (mixed[:HDIM] * inverse).astype(BF16)

    @pl.when(head == HEADS - 1)
    def _():
        for w in range(windows):
            for part in range(4):
                rows = slice(part * 128, (part + 1) * 128)
                att_ref[w, :, rows] = attt_ref[w, rows, :WIN].astype(F32).T.astype(BF16)
        if direct:
            keep_weight.wait()
            run(4, *proj, *fc1, *fc2)


def front(inputs, table, keyrow, vectors, weights, packed, depth, direct):
    windows = inputs.shape[0]
    once = lambda shape: pl.BlockSpec(shape, lambda h: (0,) * len(shape), pipeline_mode=pl.Buffered(1))
    anywhere = pl.BlockSpec(memory_space=pl.ANY)
    outs = [
        (once((windows, 3 * D, LANES)), jax.ShapeDtypeStruct((windows, 3 * D, LANES), BF16)),
        (
            pl.BlockSpec((windows, 1, WIN, LANES), lambda h: (0, h, 0, 0)),
            jax.ShapeDtypeStruct((windows, HEADS, WIN, LANES), BF16),
        ),
        (once((windows, WIN, D)), jax.ShapeDtypeStruct((windows, WIN, D), BF16)),
        (once((windows, D, LANES)), jax.ShapeDtypeStruct((windows, D, LANES), BF16)),
        (once((windows, HEADS, LANES)), jax.ShapeDtypeStruct((windows, HEADS, LANES), F32)),
        (once((16, D)), jax.ShapeDtypeStruct((16, D), F32)),
        (once((1, FF)), jax.ShapeDtypeStruct((1, FF), F32)),
    ]
    scratch = [
        pltpu.VMEM((HEADS, FLAT, SPREAD), F32),
        pltpu.VMEM((WIN_W, HEADS, SPREAD), F32),
        pltpu.VMEM((WIN, WIN), F32),
        pltpu.VMEM((windows, WIN, D), BF16),
    ]
    args = [inputs, table, keyrow]
    small = vectors[0].shape[1]
    extra = {}
    if direct:
        args += list(vectors) + list(weights)
        specs = [once(item.shape) for item in args[:-3]] + [anywhere] * 3
        wholes = [jax.ShapeDtypeStruct((2, 2, depth, 2) + item.shape, BF16) for item in weights]
        outs += [(anywhere, whole) for whole in wholes]
        slots = gather_slots(depth) * (1 + len(QKV_PIECES) + len(OTHER_PIECES)) + 1
        scratch += [
            pltpu.VMEM((16, 128), BF16),
            pltpu.VMEM(weights[0].shape, BF16),
            pltpu.VMEM((2, 2, depth, 2, 16, 128), BF16),
            pltpu.VMEM(wholes[0].shape, BF16),
            pltpu.SemaphoreType.DMA((slots,)),
            pltpu.SemaphoreType.DMA((slots,)),
        ]
        extra = dict(collective_id=0, has_side_effects=True)
    else:
        args += [packed, weights[0]]
        specs = [once(item.shape) for item in args]
    return pl.pallas_call(
        functools.partial(front_kernel, (windows, depth, direct, small)),
        grid=(HEADS,),
        in_specs=specs,
        out_specs=[spec for spec, _ in outs],
        out_shape=[shape for _, shape in outs],
        scratch_shapes=scratch,
        compiler_params=pltpu.CompilerParams(vmem_limit_bytes=60 * MIB, **extra),
        name="front",
    )(*args)


def mlp_kernel(*refs):
    refs = list(refs)
    take = lambda count: [refs.pop(0) for _ in range(count)]
    x_in, att_in, cot_in, proj_in, fc1_in, fc2_in = take(6)
    keep_ref, vec_ref, fshift1_ref = take(3)
    out_out, rgrad_out, agrad_out, fc1g_out, fc2g_out, projg_out = take(6)
    sums_ref, fsum_ref = take(2)
    x_ref, att_ref, gout_ref, proj_ref, fc1_ref, fc2_ref = take(6)
    out_ref, rgrad_ref, agrad_ref, fc1g_ref, fc2g_ref, projg_ref = take(6)
    act_ref, hid_ref, norm_ref, branch_ref, in_sems, out_sems = take(6)
    rows = x_ref.shape[0]
    block = rows // 2
    pieces = 4
    wide = FF // pieces
    halves = [slice(i * block, (i + 1) * block) for i in range(2)]
    loads, stores = {}, []

    def load(name, source, target):
        copy = pltpu.make_async_copy(source, target, in_sems.at[len(loads)])
        copy.start()
        loads[name] = copy

    def store(source, target):
        copy = pltpu.make_async_copy(source, target, out_sems.at[len(stores)])
        copy.start()
        stores.append(copy)

    load("proj", proj_in, proj_ref)
    load("att0", att_in.at[halves[0]], att_ref.at[halves[0]])
    load("x0", x_in.at[halves[0]], x_ref.at[halves[0]])
    load("fc1", fc1_in, fc1_ref)
    load("cot0", cot_in.at[halves[0]], gout_ref.at[halves[0]])
    load("fc2", fc2_in, fc2_ref)
    load("att1", att_in.at[halves[1]], att_ref.at[halves[1]])
    load("x1", x_in.at[halves[1]], x_ref.at[halves[1]])
    load("cot1", cot_in.at[halves[1]], gout_ref.at[halves[1]])
    pshift, gain, shift, fshift2 = [vec_ref[i : i + 1] for i in range(4, 8)]
    sums_ref[...] = jnp.zeros_like(sums_ref)
    fsum_ref[...] = jnp.zeros_like(fsum_ref)

    for i, at in enumerate(halves):
        keep = keep_ref[at, :]
        if i == 0:
            loads["proj"].wait()
        loads[f"att{i}"].wait()
        loads[f"x{i}"].wait()
        resid = x_ref[at, :].astype(F32) + dot_nn(att_ref[at, :], proj_ref[...]) + pshift
        unit, scale = standardize(resid)
        normed = (unit * gain + shift).astype(BF16)
        norm_ref[at, :] = normed
        loads[f"cot{i}"].wait()
        gout = gout_ref[at, :].astype(F32) * keep
        gout_low = gout.astype(BF16)
        gout_ref[at, :] = gout_low
        if i == 0:
            loads["fc1"].wait()
            loads["fc2"].wait()
        total = resid + fshift2
        grad_two = None
        for part in range(pieces):
            columns = slice(part * wide, (part + 1) * wide)
            hidden = dot_nn(normed, fc1_ref[:, columns]) + fshift1_ref[:, columns]
            active, slope = gelu_parts(hidden)
            active = active.astype(BF16)
            act_ref[at, columns] = active
            total = total + dot_nn(active, fc2_ref[columns, :])
            hgrad = (dot_nt(gout_low, fc2_ref[columns, :]) * slope).astype(BF16)
            hid_ref[at, columns] = hgrad
            fsum_ref[0:1, columns] += jnp.sum(hgrad.astype(F32), axis=0, keepdims=True)
            back = dot_nt(hgrad, fc1_ref[:, columns])
            grad_two = back if grad_two is None else grad_two + back
        out_ref[at, :] = (total * keep).astype(BF16)
        store(out_ref.at[at], out_out.at[at])
        rgrad = gout + norm_backward(grad_two, unit, scale, gain)
        rgrad_ref[at, :] = rgrad
        store(rgrad_ref.at[at], rgrad_out.at[at])
        branch = rgrad.astype(BF16)
        branch_ref[at, :] = branch
        agrad_ref[at, :] = dot_nt(branch, proj_ref[...]).astype(BF16)
        store(agrad_ref.at[at], agrad_out.at[at])
        sums_ref[0:1, :] += jnp.sum(gout, axis=0, keepdims=True)
        sums_ref[1:2, :] += jnp.sum(grad_two * unit, axis=0, keepdims=True)
        sums_ref[2:3, :] += jnp.sum(grad_two, axis=0, keepdims=True)
        sums_ref[3:4, :] += jnp.sum(branch.astype(F32), axis=0, keepdims=True)
    for part in range(pieces):
        columns = slice(part * wide, (part + 1) * wide)
        fc2g_ref[columns, :] = dot_tn(act_ref[:, columns], gout_ref[...]).astype(BF16)
        store(fc2g_ref.at[columns], fc2g_out.at[columns])
    for part in range(pieces):
        columns = slice(part * wide, (part + 1) * wide)
        fc1g_ref[:, columns] = dot_tn(norm_ref[...], hid_ref[:, columns]).astype(BF16)
        store(fc1g_ref.at[:, columns], fc1g_out.at[:, columns])
    projg_ref[...] = dot_tn(att_ref[...], branch_ref[...]).astype(BF16)
    store(projg_ref, projg_out)
    for copy in stores:
        copy.wait()


def feed_forward(x_rows, att_rows, cot_rows, proj, fc1, fc2, keep_rows, vectors, fshift1):
    rows = x_rows.shape[0]
    vmem = pl.BlockSpec(memory_space=pltpu.VMEM)
    anywhere = pl.BlockSpec(memory_space=pl.ANY)
    streamed = [
        jax.ShapeDtypeStruct((rows, D), BF16),
        jax.ShapeDtypeStruct((rows, D), F32),
        jax.ShapeDtypeStruct((rows, D), BF16),
        jax.ShapeDtypeStruct((D, FF), BF16),
        jax.ShapeDtypeStruct((FF, D), BF16),
        jax.ShapeDtypeStruct((D, D), BF16),
    ]
    return pl.pallas_call(
        mlp_kernel,
        in_specs=[anywhere] * 6 + [vmem] * 3,
        out_specs=[anywhere] * 6 + [vmem] * 2,
        out_shape=streamed + [jax.ShapeDtypeStruct((8, D), F32), jax.ShapeDtypeStruct((8, FF), F32)],
        scratch_shapes=[
            pltpu.VMEM((rows, D), BF16),
            pltpu.VMEM((rows, D), BF16),
            pltpu.VMEM((rows, D), BF16),
            pltpu.VMEM((D, D), BF16),
            pltpu.VMEM((D, FF), BF16),
            pltpu.VMEM((FF, D), BF16),
        ]
        + [pltpu.VMEM(item.shape, item.dtype) for item in streamed]
        + [
            pltpu.VMEM((rows, FF), BF16),
            pltpu.VMEM((rows, FF), BF16),
            pltpu.VMEM((rows, D), BF16),
            pltpu.VMEM((rows, D), BF16),
            pltpu.SemaphoreType.DMA((9,)),
            pltpu.SemaphoreType.DMA((15,)),
        ],
        compiler_params=pltpu.CompilerParams(vmem_limit_bytes=62 * MIB),
        name="feed_forward",
    )(x_rows, att_rows, cot_rows, proj, fc1, fc2, keep_rows, vectors, fshift1)


FEED_PIECES = (
    (2, 0, 256, False),
    (2, 256, 256, True),
    (1, 0, 1024, False),
    (1, 1024, 1024, True),
    (0, 0, 256, False),
    (0, 256, 256, True),
)


def back_kernel(setup, *refs):
    windows, depth, direct, small = setup
    refs = list(refs)
    take = lambda count: [refs.pop(0) for _ in range(count)]
    qkvt_ref, attt_ref, agrad_ref, inv_ref, probs_ref, x_ref, rgrad_ref, weight_ref = take(8)
    vec_ref, sums_ref, fsum_ref = take(3)
    if direct:
        grads = take(3)
    igrad_ref, table_ref = take(2)
    if direct:
        vec_own, qkv_own, *owns = take(5)
    else:
        qkv_work, vec_work = take(2)
    dot_ref, dqkvt_ref, sum_ref, folded_ref, line_ref, total_ref, dq_ref, norm_ref, grad_ref, csum_ref = take(10)
    if direct:
        qkv_work, vec_work, table_work, table_own, table_full, *works = take(8)
        sems = (refs[-2], refs[-1])
        helds = refs[:-2]
    head = pl.program_id(0)
    count = D // small
    gain, shift = vec_ref[0:1], vec_ref[1:2]
    run = lambda stage, *lists: [stages[stage]() for stages in lists]

    if direct:
        place = Place(depth)
        base, spot = len(works) + 1, 0

        def piece(work, write, x_first):
            nonlocal base, spot
            stages = scatter_stages(place, work, helds[spot : spot + 4], sems, base, x_first, write)
            base += scatter_slots(depth)
            spot += 4
            return stages

        def whole(own, columns):
            def write(total):
                own[:, columns] = total

            return write

        def unpermuted(start, size):
            def write(total):
                for at in range(start, start + size, 128):
                    half, part, rest = at // HWIDE, at % HWIDE // HCOLS, at % HCOLS
                    to = part * D + half * HCOLS + rest
                    qkv_own[:, to : to + 128] = total[:, at - start : at - start + 128]

            return write

        feed = []
        for i, start, size, x_first in FEED_PIECES:
            columns = pl.ds(start, size)
            feed.append(piece(works[i].at[:, :, :, :, :, columns], whole(owns[i], columns), x_first))
        fc2, fc1 = feed[:2], feed[2:]
        qkv = []
        for _, start, size, x_first in QKV_PIECES:
            view = qkv_work.at[:, :, :, :, :, pl.ds(start, size)]
            qkv.append(piece(view, unpermuted(start, size), x_first))
        table = piece(table_work, whole(table_own, slice(None)), False)
        vector = piece(vec_work, whole(vec_own, slice(None)), True)
        collect = gather_stages(
            place, table_own, lambda y, c, z, x: table_full.at[y, c, z, x], sems, base, True
        )
        loads = [pltpu.make_async_copy(grads[i], works[i], sems[0].at[i]) for i in range(len(works))]

    def turn_over(half):
        for part in range(HWIDE // 128):
            rows = slice(half * HWIDE + part * 128, half * HWIDE + (part + 1) * 128)
            columns = slice(part * 128, (part + 1) * 128)
            total = 0.0
            for w in range(windows):
                low = dqkvt_ref[w, rows, :WIN].astype(F32).T
                dq_ref[w, :, columns] = low.astype(BF16)
                total = total + jnp.sum(low, axis=0, keepdims=True)
            csum_ref[0:1, rows] = total

    def weight_grad(half, start, size):
        total = 0.0
        for w in range(windows):
            total = total + dot_tn(norm_ref[w], dq_ref[w, :, start : start + size])
        columns = slice(half * HWIDE + start, half * HWIDE + start + size)
        if direct:
            qkv_work[:, :, :, :, :, columns] = total.astype(BF16).reshape(2, 2, depth, 2, small, size)
        else:
            qkv_work[:, columns] = total.astype(BF16)

    def norm_grad(half, w):
        return dot_nt(dq_ref[w], weight_ref[:, half * HWIDE : (half + 1) * HWIDE])

    @pl.when(head == 0)
    def _():
        if direct:
            place.greet()
            for load in loads:
                load.start()
        for w in range(windows):
            for part in range(4):
                rows = slice(part * 128, (part + 1) * 128)
                dot_ref[w, rows, :] = agrad_ref[w, :, rows].astype(F32).T.astype(BF16)
            unit, _ = standardize(x_ref[w].astype(F32))
            norm_ref[w] = (unit * gain + shift).astype(BF16)
        if direct:
            for load in loads:
                load.wait()
            run(0, *fc2, *fc1)

    @pl.when(head == HALF)
    def _():
        turn_over(0)
        weight_grad(0, 0, 384)
        if direct:
            run(0, qkv[0])
        weight_grad(0, 384, 384)
        if direct:
            run(0, qkv[1])
            run(2, *fc2)
        fold_bias(folded_ref, total_ref, line_ref, 0)
        for w in range(windows):
            grad_ref[w] = norm_grad(0, w)
        if direct:
            run(1, *qkv[:2])
            run(2, *fc1)

    if direct:
        steps = (
            (2, ((1, fc2),)),
            (4, ((1, fc1),)),
            (10, ((3, fc2),)),
            (12, ((2, qkv[:2]),)),
            (13, ((3, fc1), (4, fc2))),
            (15, ((3, qkv[:2]),)),
        )
        for at, group in steps:

            @pl.when(head == at)
            def _(group=group):
                for stage, lists in group:
                    run(stage, *lists)

    row = head_row(head)
    own_row = pl.multiple_of(head * HDIM, HDIM)
    ones = jnp.ones((16, WIN), BF16)
    order = spots_of((16, WIN), 0)

    def prepare(w):
        grad = dot_ref[w, pl.ds(own_row, HDIM), :].astype(F32) * inv_ref[w, pl.ds(head, 1), :WIN]
        mixed = attt_ref[w, pl.ds(own_row, HDIM), :WIN].astype(F32)
        inner = -jnp.sum(grad * mixed, axis=0, keepdims=True)
        high = inner.astype(BF16).astype(F32)
        middle = (inner - high).astype(BF16).astype(F32)
        lowest = inner - high - middle
        extra = jnp.where(
            order == 0, high, jnp.where(order == 1, middle, jnp.where(order == 2, lowest, 0.0))
        ).astype(BF16)
        grad = grad.astype(BF16)
        values = qkvt_ref[w, pl.ds(row + 2 * HCOLS, HDIM), :WIN]
        probs_grad = dot_tn(
            jnp.concatenate([values, ones], axis=0), jnp.concatenate([grad, extra], axis=0)
        )
        return grad, probs_grad

    for first in range(0, windows, 2):
        pair = range(first, min(first + 2, windows))
        prepared = [prepare(w) for w in pair]
        expos = [probs_ref[w, 0, :, :WIN] for w in pair]
        grads_s = [expo.astype(F32) * item[1] for expo, item in zip(expos, prepared)]
        total = sum(grads_s[1:], grads_s[0])
        if first == 0:
            sum_ref[...] = total
        else:
            sum_ref[...] += total
        for w, expo, (grad, _), scores_grad in zip(pair, expos, prepared, grads_s):
            low = scores_grad.astype(BF16)
            queries = qkvt_ref[w, pl.ds(row, HDIM), :WIN]
            keys = qkvt_ref[w, pl.ds(row + HCOLS, HDIM), :WIN]
            dqkvt_ref[w, pl.ds(row, HDIM), :WIN] = (dot_nn(keys, low) * SCALE).astype(BF16)
            dqkvt_ref[w, pl.ds(row + HCOLS, HDIM), :WIN] = (dot_nt(queries, low) * LN2).astype(BF16)
            dqkvt_ref[w, pl.ds(row + 2 * HCOLS, HDIM), :WIN] = dot_nt(grad, expo).astype(BF16)

    folded_ref[head] = jnp.zeros((FLAT, SPREAD), F32)
    for u in range(WIN_T):
        start = (WIN_T - 1 - u) * FLAT
        folded_ref[head, :, start : start + WIN] += sum_ref[u * FLAT : (u + 1) * FLAT, :]

    @pl.when(head == HEADS - 1)
    def _():
        gain_sum, shift_sum = 0.0, 0.0

        def input_grad(w):
            nonlocal gain_sum, shift_sum
            unit, scale = standardize(x_ref[w].astype(F32))
            grad = grad_ref[w] + norm_grad(1, w)
            igrad_ref[w] = (rgrad_ref[w] + norm_backward(grad, unit, scale, gain)).astype(BF16)
            gain_sum = gain_sum + jnp.sum(grad * unit, axis=0, keepdims=True)
            shift_sum = shift_sum + jnp.sum(grad, axis=0, keepdims=True)

        def vector_block():
            halves = [csum_ref[0:1, half * HWIDE : (half + 1) * HWIDE] for half in range(2)]
            rows = [
                gain_sum,
                shift_sum,
                jnp.concatenate([item[:, :HCOLS] for item in halves], axis=1),
                jnp.concatenate([item[:, 2 * HCOLS :] for item in halves], axis=1),
                sums_ref[3:4],
                sums_ref[1:2],
                sums_ref[2:3],
                sums_ref[0:1],
                jnp.zeros((8, D), F32),
            ]
            block = share_vectors(jnp.concatenate(rows, axis=0), count, small)
            last = share_vectors(fsum_ref[0:1], count, FF // count)
            return jnp.where(spots_of((count, 16, 128), 1) == 8, last, block)

        fold_bias(folded_ref, total_ref, line_ref, 1)
        if direct:
            total_ref[:, OFFS_T * HALF :] = jnp.zeros((2, 128 - OFFS_T * HALF, 256), F32)
            table_work[...] = total_ref[...].reshape(table_work.shape)
            run(0, table)
            turn_over(1)
            run(1, table)
            weight_grad(1, 0, 384)
            run(0, qkv[2])
            run(2, table)
            weight_grad(1, 384, 384)
            run(0, qkv[3])
            run(1, qkv[2])
            run(3, table)
            input_grad(0)
            run(1, qkv[3])
            run(4, *fc1)
            input_grad(1)
            run(4, table)
            run(0, collect)
            run(4, *qkv[:2])
            run(2, *qkv[2:])
            input_grad(2)
            run(1, collect)
            run(3, *qkv[2:])
            input_grad(3)
            vec_work[...] = vector_block().reshape(vec_work.shape)
            run(0, vector)
            run(2, collect)
            run(1, vector)
            run(3, collect)
            run(4, *qkv[2:])
            run(2, vector)
            run(4, collect)
            totals = table_full[...].reshape(2, 128, 256)
        else:
            turn_over(1)
            weight_grad(1, 0, 384)
            weight_grad(1, 384, 384)
            for w in range(windows):
                input_grad(w)
            vec_work[...] = vector_block()
            totals = total_ref[...]
        span = OFFS_H * OFFS_W
        for k in range(OFFS_T):
            heads = [totals[half, k * HALF : (k + 1) * HALF] for half in range(2)]
            table_ref[k * span : (k + 1) * span, :] = jnp.concatenate(heads, axis=0).T[:span]
        if direct:
            run(3, vector)
            run(4, vector)


def back(qkvt, attt, agrad, inverse, probs, inputs, rgrad, weight, vectors, sums, fsum, grads, depth, direct):
    windows = qkvt.shape[0]
    count = lax.axis_size("dp") * lax.axis_size("fsdp")
    small = D // count
    once = lambda shape: pl.BlockSpec(shape, lambda h: (0,) * len(shape), pipeline_mode=pl.Buffered(1))
    anywhere = pl.BlockSpec(memory_space=pl.ANY)
    args = [qkvt, attt, agrad, inverse, probs, inputs, rgrad, weight, vectors, sums, fsum]
    specs = [once(item.shape) for item in args]
    specs[4] = pl.BlockSpec((windows, 1, WIN, LANES), lambda h: (0, h, 0, 0))
    shapes = [
        jax.ShapeDtypeStruct(inputs.shape, BF16),
        jax.ShapeDtypeStruct((OFFS_T * OFFS_H * OFFS_W, HEADS), F32),
    ]
    scratch = [
        pltpu.VMEM((windows, D, WIN), BF16),
        pltpu.VMEM((windows, 3 * D, LANES), BF16),
        pltpu.VMEM((WIN, WIN), F32),
        pltpu.VMEM((HEADS, FLAT, SPREAD), F32),
        pltpu.VMEM((WIN_W, HALF, SPREAD), F32),
        pltpu.VMEM((2, 128, 256), F32),
        pltpu.VMEM((windows, WIN, HWIDE), BF16),
        pltpu.VMEM((windows, WIN, D), BF16),
        pltpu.VMEM((windows, WIN, D), F32),
        pltpu.VMEM((8, 3 * D), F32),
    ]
    extra = {}
    if direct:
        lead = (2, 2, depth, 2)
        rows = 256 // count
        views = [item.reshape(lead + (-1, item.shape[1])) for item in grads]
        args += views
        specs += [anywhere] * len(views)
        shapes += [
            jax.ShapeDtypeStruct((16, 128), F32),
            jax.ShapeDtypeStruct((small, 3 * D), F32),
        ] + [jax.ShapeDtypeStruct(item.shape[-2:], F32) for item in views]
        scratch += [
            pltpu.VMEM(lead + (small, 3 * D), BF16),
            pltpu.VMEM(lead + (16, 128), F32),
            pltpu.VMEM(lead + (rows, 256), F32),
            pltpu.VMEM((rows, 256), F32),
            pltpu.VMEM(lead + (rows, 256), F32),
        ] + [pltpu.VMEM(item.shape, BF16) for item in views]
        for i, _, size, x_first in FEED_PIECES:
            scratch += held_shapes(depth, views[i].shape[-2], size, BF16, x_first)
        for _, _, size, x_first in QKV_PIECES:
            scratch += held_shapes(depth, small, size, BF16, x_first)
        scratch += held_shapes(depth, rows, 256, F32, False) + held_shapes(depth, 16, 128, F32, True)
        exchanges = len(FEED_PIECES) + len(QKV_PIECES) + 2
        slots = len(views) + 1 + scatter_slots(depth) * exchanges + gather_slots(depth)
        scratch += [pltpu.SemaphoreType.DMA((slots,)), pltpu.SemaphoreType.DMA((slots,))]
        extra = dict(collective_id=1, has_side_effects=True)
    else:
        shapes += [
            jax.ShapeDtypeStruct((D, 3 * D), BF16),
            jax.ShapeDtypeStruct((count, 16, 128), F32),
        ]
    return pl.pallas_call(
        functools.partial(back_kernel, (windows, depth, direct, small)),
        grid=(HEADS,),
        in_specs=specs,
        out_specs=[once(item.shape) for item in shapes],
        out_shape=shapes,
        scratch_shapes=scratch,
        compiler_params=pltpu.CompilerParams(vmem_limit_bytes=63 * MIB, **extra),
        name="back",
    )(*args)


def valid_mask(extents):
    spots = np.arange(WIN)
    depth, height, across = spots // FLAT, spots // WIN_W % WIN_H, spots % WIN_W
    return (
        (depth[None, :] < extents[:, 0:1])
        & (height[None, :] < extents[:, 1:2])
        & (across[None, :] < extents[:, 2:3])
    ).astype(F32)


def gathered(value):
    return lax.all_gather(value, AXES, axis=0, tiled=True)


def scattered(value):
    return lax.psum_scatter(value, AXES, scatter_dimension=0, tiled=True)


def per_device(
    inputs,
    extents,
    cotangent,
    ln1_gain,
    ln1_shift,
    qkv_weight,
    query_bias,
    value_bias,
    bias_table,
    proj_weight,
    proj_shift,
    ln2_gain,
    ln2_shift,
    fc1_weight,
    fc1_shift,
    fc2_weight,
    fc2_shift,
):
    windows = inputs.shape[0]
    rows = windows * WIN
    small = ln1_gain.shape[0]
    count = D // small
    depth = lax.axis_size("fsdp") // 2
    direct = small % 16 == 0 and lax.axis_size("dp") == 4
    vectors = [
        item[None]
        for item in (
            ln1_gain,
            ln1_shift,
            query_bias,
            value_bias,
            proj_shift,
            ln2_gain,
            ln2_shift,
            fc2_shift,
            fc1_shift,
        )
    ]
    weights = (qkv_weight, proj_weight, fc1_weight, fc2_weight)
    packed = None
    if not direct:
        packed = jnp.concatenate([jnp.pad(item, ((0, 0), (0, 128 - item.shape[1]))) for item in vectors])
        packed = gathered(jnp.pad(packed, ((0, 16 - len(vectors)), (0, 0))))
        weights = [gathered(item) for item in weights]
        weights[0] = weights[0].reshape(D, 3, 2, HCOLS).swapaxes(1, 2).reshape(D, 3 * D)
    keep = valid_mask(extents)
    keep_rows = keep.reshape(rows, 1)
    keyrow = jnp.concatenate(
        [((keep - 1.0) * 1e30)[:, None, :], jnp.zeros((windows, 15, WIN), F32)], axis=1
    ).astype(BF16)
    x_rows = inputs.reshape(rows, D)
    qkvt, probs, att, attt, inverse, full_vectors, fshift1, *wholes = front(
        inputs, bias_table, keyrow, vectors, weights, packed, depth, direct
    )
    if direct:
        weights = [item.reshape(-1, item.shape[-1]) for item in wholes]
    qkv_full, proj_full, fc1_full, fc2_full = weights
    output, rgrad, agrad, fc1_grad, fc2_grad, proj_grad, sums, fsum = feed_forward(
        x_rows,
        att.reshape(rows, D),
        cotangent.reshape(rows, D),
        proj_full,
        fc1_full,
        fc2_full,
        keep_rows,
        full_vectors,
        fshift1,
    )
    matrices = (proj_grad, fc1_grad, fc2_grad)
    input_grad, table_grad, *rest = back(
        qkvt,
        attt,
        agrad.reshape(windows, WIN, D),
        inverse,
        probs,
        inputs,
        rgrad.reshape(windows, WIN, D),
        qkv_full,
        full_vectors,
        sums,
        fsum,
        matrices,
        depth,
        direct,
    )
    if direct:
        vector_own, qkv_own, proj_own, fc1_own, fc2_own = rest
    else:
        qkv_grad = rest[0].reshape(D, 2, 3, HCOLS).swapaxes(1, 2).reshape(D, 3 * D)
        qkv_own, proj_own, fc1_own, fc2_own = [
            scattered(item.astype(F32)) for item in (qkv_grad,) + matrices
        ]
        vector_own = scattered(rest[1])[0]
        table_grad = lax.psum(table_grad, AXES)
    owned_vectors = jnp.concatenate([vector_own[i, :small] for i in range(8)] + [vector_own[8, : FF // count]])
    owned = [owned_vectors[i * small : (i + 1) * small] for i in range(8)]
    return (
        output.reshape(inputs.shape),
        input_grad.reshape(inputs.shape),
        owned[0],
        owned[1],
        qkv_own,
        owned[2],
        owned[3],
        table_grad,
        proj_own,
        owned[4],
        owned[5],
        owned[6],
        fc1_own,
        owned_vectors[8 * small :],
        fc2_own,
        owned[7],
    )


def solution(mesh):
    rows = P(AXES, None)
    vector = P(AXES)
    block = P(AXES, None, None)
    in_specs = (
        block,
        rows,
        block,
        vector,
        vector,
        rows,
        vector,
        vector,
        P(),
        rows,
        vector,
        vector,
        vector,
        rows,
        vector,
        rows,
        vector,
    )
    out_specs = (
        block,
        block,
        vector,
        vector,
        rows,
        vector,
        vector,
        P(),
        rows,
        vector,
        vector,
        vector,
        rows,
        vector,
        rows,
        vector,
    )
    return jax.shard_map(
        per_device, mesh=mesh, in_specs=in_specs, out_specs=out_specs, check_vma=False
    )
```

```python
import functools
import math

import jax
import jax.numpy as jnp
import numpy as np
from jax import lax
from jax.experimental import pallas as pl
from jax.experimental.pallas import tpu as pltpu
from jax.sharding import PartitionSpec as P

D = 512
HEADS = 16
HDIM = 32
FF = 2048
WIN_T = 8
WIN_H = 7
WIN_W = 7
WIN = WIN_T * WIN_H * WIN_W
FLAT = WIN_H * WIN_W
OFFS_T = 2 * WIN_T - 1
OFFS_H = 2 * WIN_H - 1
OFFS_W = 2 * WIN_W - 1
SPREAD = OFFS_T * FLAT
LANES = 512
FEW = 4
GROUPS = ((0, FEW), (FEW, HEADS - FEW))
STARTS = (0, 3 * FEW * HDIM)
WIDE = 3 * (HEADS - FEW) * HDIM
EPS = 1e-05
LOG2E = math.log2(math.e)
LN2 = math.log(2.0)
SCALE = HDIM ** (-0.5)
AXES = ("dp", "fsdp")
BF16 = jnp.bfloat16
F32 = jnp.float32
MIB = 2**20


def dot(left, right, left_dim, right_dim):
    return lax.dot_general(
        left, right, (((left_dim,), (right_dim,)), ((), ())), preferred_element_type=F32
    )


def dot_nn(left, right):
    return dot(left, right, 1, 0)


def dot_nt(left, right):
    return dot(left, right, 1, 1)


def dot_tn(left, right):
    return dot(left, right, 0, 0)


def standardize(rows):
    average = jnp.mean(rows, axis=-1, keepdims=True)
    centered = rows - average
    variance = jnp.mean(centered * centered, axis=-1, keepdims=True)
    scale = lax.rsqrt(variance + EPS)
    return centered * scale, scale


def norm_backward(grad, unit, scale, gain):
    scaled = grad * gain
    first = jnp.mean(scaled, axis=-1, keepdims=True)
    second = jnp.mean(scaled * unit, axis=-1, keepdims=True)
    return (scaled - first - unit * second) * scale


def gelu_parts(hidden):
    below = 0.5 * lax.erf(hidden * (0.5**0.5)) + 0.5
    bell = jnp.exp2(hidden * hidden * (-0.5 * LOG2E)) * (1.0 / math.sqrt(2 * math.pi))
    return hidden * below, below + hidden * bell


class Place:
    def __init__(self, depth):
        dp, fsdp = lax.axis_index("dp"), lax.axis_index("fsdp")
        self.depth = depth
        self.y, self.c = dp // 2, dp % 2
        self.z, self.x = fsdp // 2, fsdp % 2
        self.core = (self.y * 2 + 1 - self.c, fsdp)
        self.across_x = (dp, self.z * 2 + 1 - self.x)
        self.across_y = ((1 - self.y) * 2 + self.c, fsdp)
        self.along_z = [(dp, ((self.z + j) % depth) * 2 + self.x) for j in range(1, depth)]
        self.group = []
        for j in range(1, 8):
            y = 1 - self.y if j & 4 else self.y
            c = 1 - self.c if j & 2 else self.c
            x = 1 - self.x if j & 1 else self.x
            self.group.append(((y, c, x), (y * 2 + c, self.z * 2 + x)))

    def greet(self, group=False):
        barrier = pltpu.get_barrier_semaphore()
        partners = [self.core, self.across_x, self.across_y] + self.along_z
        if group:
            partners = [device for _, device in self.group] + self.along_z
        for partner in partners:
            pl.semaphore_signal(barrier, inc=1, device_id=partner, device_id_type=pl.DeviceIdType.MESH)
        pl.semaphore_wait(barrier, len(partners))


def send(source, target, sems, slot, device):
    return pltpu.make_async_remote_copy(
        src_ref=source,
        dst_ref=target,
        send_sem=sems[0].at[slot],
        recv_sem=sems[1].at[slot],
        device_id=device,
        device_id_type=pl.DeviceIdType.MESH,
    )


def gather_slots(depth):
    return depth + 5


def gather_stages(place, own, full, sems, base, y_first):
    y, c, z, x, depth = place.y, place.c, place.z, place.x, place.depth
    every = slice(None)
    here = full(y, c, z, x)
    local = pltpu.make_async_copy(own, here, sems[0].at[base])
    along = [send(own, here, sems, base + j, place.along_z[j - 1]) for j in range(1, depth)]
    column = full(y, c, every, x)
    if y_first:
        first = send(column, column, sems, base + depth, place.across_y)
        both = full(every, c, every, x)
        second = send(both, both, sems, base + depth + 1, place.across_x)
        one = full(1 - y, c, every, x)
        two = full(every, c, every, 1 - x)
    else:
        first = send(column, column, sems, base + depth, place.across_x)
        both = full(y, c, every, every)
        second = send(both, both, sems, base + depth + 1, place.across_y)
        one = full(y, c, every, 1 - x)
        two = full(1 - y, c, every, every)
    shares = [
        send(part, part, sems, base + depth + 2 + k, place.core) for k, part in enumerate((column, one, two))
    ]

    def begin():
        local.start()
        for copy in along:
            copy.start()

    def turn():
        local.wait()
        for copy in along:
            copy.wait_recv()
        first.start()
        shares[0].start()

    def cross():
        first.wait_recv()
        second.start()
        shares[1].start()

    def share():
        second.wait_recv()
        shares[2].start()

    def finish():
        for copy in shares:
            copy.wait()
        for copy in along + [first, second]:
            copy.wait_send()

    return [begin, turn, cross, share, finish]


def scatter_slots(depth):
    return depth + 2


def add_into(target, index, extra):
    target[index] = (target[index].astype(F32) + extra.astype(F32)).astype(target.dtype)


def scatter_stages(place, parts, held, sems, base, x_first, write):
    y, c, z, x, depth = place.y, place.c, place.z, place.x, place.depth
    every = slice(None)
    from_core, from_first, from_second, from_z = held
    share = send(parts.at[:, 1 - c], from_core, sems, base, place.core)
    if x_first:
        first = send(parts.at[:, c, :, 1 - x], from_first, sems, base + 1, place.across_x)
        second = send(parts.at[1 - y, c, :, x], from_second, sems, base + 2, place.across_y)
    else:
        first = send(parts.at[1 - y, c], from_first, sems, base + 1, place.across_y)
        second = send(parts.at[y, c, :, 1 - x], from_second, sems, base + 2, place.across_x)
    along = [
        send(
            parts.at[y, c, (z + j) % depth, x],
            from_z.at[j - 1],
            sems,
            base + 2 + j,
            place.along_z[j - 1],
        )
        for j in range(1, depth)
    ]

    def begin():
        share.start()

    def cross():
        share.wait_recv()
        for yy in range(2):
            add_into(parts, (yy, c), from_core[yy])
        first.start()

    def turn():
        first.wait_recv()
        if x_first:
            for yy in range(2):
                for zz in range(depth):
                    add_into(parts, (yy, c, zz, x), from_first[yy, zz])
        else:
            add_into(parts, (y, c), from_first[...])
        second.start()

    def spread():
        second.wait_recv()
        for zz in range(depth):
            add_into(parts, (y, c, zz, x), from_second[zz])
        for copy in along:
            copy.start()

    def finish():
        for copy in along:
            copy.wait_recv()
        total = parts[y, c, z, x].astype(F32)
        for j in range(depth - 1):
            total = total + from_z[j].astype(F32)
        write(total)
        for copy in along + [share, first, second]:
            copy.wait_send()

    return [begin, cross, turn, spread, finish]


def group_slots(depth):
    return 7 + depth - 1


def sum_in_group(place, own, others):
    total = own
    for j in range(7):
        total = total + others[j]
    return total


def small_scatter_stages(place, parts, from_group, from_z, mine, sems, base, write):
    y, c, z, x, depth = place.y, place.c, place.z, place.x, place.depth
    hops = []
    for j, ((yy, cc, xx), device) in enumerate(place.group):
        hops.append(send(parts.at[yy, cc, :, xx], from_group.at[j], sems, base + j, device))
    along = [
        send(mine.at[(z + j) % depth], from_z.at[j - 1], sems, base + 6 + j, place.along_z[j - 1])
        for j in range(1, depth)
    ]

    def begin():
        for copy in hops:
            copy.start()

    def turn():
        for copy in hops:
            copy.wait_recv()
        for zz in range(depth):
            mine[zz] = sum_in_group(place, parts[y, c, zz, x], [from_group[j, zz] for j in range(7)])
        for copy in along:
            copy.start()

    def finish():
        for copy in along:
            copy.wait_recv()
        total = mine[z]
        for j in range(depth - 1):
            total = total + from_z[j]
        write(total)
        for copy in hops + along:
            copy.wait_send()

    return [begin, turn, finish]


def small_sum_stages(place, parts, from_group, from_z, full, sems, base):
    y, c, z, x, depth = place.y, place.c, place.z, place.x, place.depth
    hops = []
    for j, ((yy, cc, xx), device) in enumerate(place.group):
        hops.append(send(parts.at[yy, cc, xx], from_group.at[j], sems, base + j, device))
    along = [
        send(from_z.at[z], from_z.at[z], sems, base + 6 + j, place.along_z[j - 1]) for j in range(1, depth)
    ]
    here = full.at[y, c, x]
    spread = [
        send(here, here, sems, base + group_slots(depth) + j, device)
        for j, (_, device) in enumerate(place.group)
    ]

    def begin():
        for copy in hops:
            copy.start()

    def turn():
        for copy in hops:
            copy.wait_recv()
        from_z[z] = sum_in_group(place, parts[y, c, x], from_group)
        for copy in along:
            copy.start()

    def share():
        for copy in along:
            copy.wait_recv()
        total = from_z[0]
        for zz in range(1, depth):
            total = total + from_z[zz]
        full[y, c, x] = total
        for copy in spread:
            copy.start()

    def finish():
        for copy in spread:
            copy.wait_recv()
        for copy in hops + along + spread:
            copy.wait_send()

    return [begin, turn, share, finish]


def held_shapes(depth, rows, columns, dtype, x_first):
    first = (2, depth, rows, columns) if x_first else (depth, 2, rows, columns)
    return [
        pltpu.VMEM((2, depth, 2, rows, columns), dtype),
        pltpu.VMEM(first, dtype),
        pltpu.VMEM((depth, rows, columns), dtype),
        pltpu.VMEM((depth - 1, rows, columns), dtype),
    ]


def spots_of(shape, axis):
    return lax.broadcasted_iota(jnp.int32, shape, axis)


def pack_vectors(vectors):
    rows = spots_of((16, 128), 0)
    block = jnp.zeros((16, 128), F32)
    for i, vector in enumerate(vectors):
        vector = vector.astype(F32)
        if vector.shape[1] < 128:
            vector = jnp.concatenate([vector, jnp.zeros((1, 128 - vector.shape[1]), F32)], axis=1)
        block = jnp.where(rows == i, vector, block)
    return block


def unpack_vectors(blocks, count, small):
    width = count * small
    lanes, columns = spots_of((128, width), 0), spots_of((128, width), 1)
    choice = ((columns & (small - 1)) == lanes).astype(BF16)
    wide = dot_nn(blocks, choice).reshape(count, 16, width)
    owner = spots_of((count, 16, width), 0)
    column = spots_of((count, 16, width), 2)
    low = owner * small
    return jnp.sum(jnp.where((column >= low) & (column < low + small), wide, 0.0), axis=0)


def frame_spots(shape, axis):
    spot = spots_of(shape, axis)
    row = jnp.zeros(shape, jnp.int32)
    for i in range(1, WIN_H):
        row += (spot >= i * WIN_W).astype(jnp.int32)
    return (row + WIN_H - 1) * OFFS_W + spot - row * WIN_W + WIN_W - 1


def table_rows(table):
    span = OFFS_H * OFFS_W
    return jnp.concatenate([table[:, k * span : (k + 1) * span] for k in range(OFFS_T)], axis=0)


def kept(spot, extents_ref, window):
    frame = jnp.zeros(spot.shape, jnp.int32)
    for i in range(1, WIN_T):
        frame += (spot >= i * FLAT).astype(jnp.int32)
    rest = spot - frame * FLAT
    row = jnp.zeros(spot.shape, jnp.int32)
    for i in range(1, WIN_H):
        row += (rest >= i * WIN_W).astype(jnp.int32)
    column = rest - row * WIN_W
    return (
        (frame < extents_ref[window, 0])
        & (row < extents_ref[window, 1])
        & (column < extents_ref[window, 2])
    )


def spread_bias(table, spread_ref, line_ref, begin, end):
    span = OFFS_H * OFFS_W
    base = frame_spots((span, FLAT), 1) - spots_of((span, FLAT), 0)

    def one(v, carry):
        for e in range(WIN_W):
            choice = jnp.where(base == v * OFFS_W + e, 1.0, 0.0).astype(BF16)
            wide = dot_nn(table, choice) * LOG2E
            for k in range(OFFS_T):
                line_ref[e, :, k * FLAT : (k + 1) * FLAT] = wide[k * HEADS : (k + 1) * HEADS]
            for h in range(HEADS):
                spread_ref[h, pl.ds(v * WIN_W + e, 1), :] = line_ref[e, h : h + 1, :]
        return carry

    lax.fori_loop(begin, end, one, 0)


def fold_bias(folded_ref, line_ref, heads):
    base = frame_spots((FLAT, 256), 0) - spots_of((FLAT, 256), 1)

    def one(v, total):
        for e in range(WIN_W):
            choice = jnp.where(base == v * OFFS_W + e, 1.0, 0.0).astype(BF16)
            for i, h in enumerate(heads):
                line_ref[e, i : i + 1, :] = folded_ref[h, pl.ds(v * WIN_W + e, 1), :]
            wide = jnp.concatenate(
                [line_ref[e, :, k * FLAT : (k + 1) * FLAT] for k in range(OFFS_T)], axis=0
            )
            high = wide.astype(BF16)
            total = total + dot_nn(high, choice) + dot_nn((wide - high.astype(F32)).astype(BF16), choice)
        return total

    total = lax.fori_loop(0, WIN_H, one, jnp.zeros((OFFS_T * 8, 256), F32))
    return total.reshape(OFFS_T, 8, 256)


def share_vectors(rows, count, small, lane=0):
    kinds, width = rows.shape
    lanes, columns = spots_of((128, width), 0), spots_of((128, width), 1)
    choice = ((columns & (small - 1)) + lane == lanes).astype(BF16)
    low = spots_of((count, kinds, width), 0) * small
    column = spots_of((count, kinds, width), 2)
    wide = jnp.where((column >= low) & (column < low + small), rows[None], 0.0)
    wide = wide.reshape(count * kinds, width)
    blocks = 0.0
    for _ in range(3):
        part = wide.astype(BF16)
        blocks = blocks + dot_nt(part, choice)
        wide = wide - part.astype(F32)
    return blocks.reshape(count, kinds, 128)


QKV_PIECES = ((1, 0, 256, False), (1, 256, 128, True), (1, 384, 640, True), (1, 1024, 512, False))
OTHER_PIECES = (
    (2, 0, 256, False),
    (2, 256, 256, True),
    (3, 0, 1024, False),
    (3, 1024, 1024, True),
    (4, 0, 256, False),
    (4, 256, 256, True),
)


def head_rows(head):
    late = (head >= FEW).astype(jnp.int32)
    row = head * HDIM + late * (STARTS[1] - FEW * HDIM)
    step = FEW * HDIM + late * ((HEADS - 2 * FEW) * HDIM)
    return [pl.multiple_of(row + part * step, HDIM) for part in range(3)]


def front_kernel(setup, *refs):
    windows, depth, direct, small = setup
    refs = list(refs)
    take = lambda count: [refs.pop(0) for _ in range(count)]
    x_ref, table_ref, extents_ref = take(3)
    if direct:
        vector_refs, shards = take(9), take(4)
    else:
        packed_ref, weight_in = take(2)
    qkvt_out, probs_ref, att_ref, attt_out, inv_ref, vec_ref, fvec_ref = take(7)
    if direct:
        wholes = take(4)
    spread_ref, line_ref, bias_ref, unit_ref, norm_ref, keyrow_ref, qkvt_ref, attt_ref, hand_sem = take(9)
    if direct:
        pack_ref, own_ref, packed_ref, weight_ref, *sems = take(6)
    head = pl.program_id(0)
    count = D // small
    run = lambda stage, *lists: [stages[stage]() for stages in lists]
    hand_on = pltpu.make_async_copy(qkvt_ref, qkvt_out, hand_sem.at[0])

    if direct:
        place = Place(depth)
        views = [packed_ref, weight_ref] + wholes[1:]
        sources = [pack_ref, own_ref] + shards[1:]
        lists = []
        for index, start, size, y_first in ((0, 0, 128, False),) + QKV_PIECES + OTHER_PIECES:
            columns = pl.ds(start, size)
            view = lambda y, c, z, x, whole=views[index], columns=columns: whole.at[y, c, z, x, :, columns]
            base = gather_slots(depth) * len(lists)
            lists.append(gather_stages(place, sources[index].at[:, columns], view, sems, base, y_first))
        few, many, proj, fc1, fc2 = lists[:3], lists[3:5], lists[5:7], lists[7:9], lists[9:]
        keep_weight = pltpu.make_async_copy(weight_ref, wholes[0], sems[0].at[gather_slots(depth) * len(lists)])

    def project(group, weight, vectors):
        head_start, heads = GROUPS[group]
        width = heads * HDIM
        own = slice(head_start * HDIM, head_start * HDIM + width)
        bias = jnp.concatenate(
            [vectors[2:3, own] * (SCALE * LOG2E), jnp.zeros((1, width), F32), vectors[3:4, own]], axis=1
        )
        factor = jnp.where(spots_of((1, 3 * width), 1) < width, SCALE * LOG2E, 1.0)
        for w in range(windows):
            for start in range(0, 3 * width, 256):
                end = min(start + 256, 3 * width)
                got = dot_nn(norm_ref[w], weight[:, start:end])
                got = got * factor[:, start:end] + bias[:, start:end]
                for piece in range((end - start) // 128):
                    at = STARTS[group] + start + piece * 128
                    qkvt_ref[w, at : at + 128, :WIN] = got[:, piece * 128 : (piece + 1) * 128].T.astype(BF16)

    def group_weight(group):
        start, width = STARTS[group], 3 * GROUPS[group][1] * HDIM
        if not direct:
            return weight_in[:, start : start + width]
        return weight_ref[:, :, :, :, :, start : start + width].reshape(D, width)

    def standard():
        for w in range(windows):
            unit_ref[w], _ = standardize(x_ref[w].astype(F32))

    def normalize(vectors):
        for w in range(windows):
            norm_ref[w] = (unit_ref[w] * vectors[0:1] + vectors[1:2]).astype(BF16)

    def biases(begin, end):
        def one(h, carry):
            for u in range(WIN_T):
                start = (WIN_T - 1 - u) * FLAT
                bias_ref[h, u * FLAT : (u + 1) * FLAT, :] = spread_ref[h, :, start : start + WIN]
            return carry

        lax.fori_loop(begin, end, one, 0)

    def key_rows():
        spot, line = spots_of((16, WIN), 1), spots_of((16, WIN), 0)
        for w in range(windows):
            keyrow_ref[w] = jnp.where(kept(spot, extents_ref, w) | (line > 0), 0.0, -1e30).astype(BF16)

    @pl.when(head == 0)
    def _():
        spread = lambda begin, end: spread_bias(table, spread_ref, line_ref, begin, end)
        if direct:
            pack_ref[...] = pack_vectors([ref[...] for ref in vector_refs]).astype(BF16)
            for part in range(3):
                for group, (head_start, heads) in enumerate(GROUPS):
                    width = heads * HDIM
                    start = STARTS[group] + part * width
                    source = part * D + head_start * HDIM
                    own_ref[:, start : start + width] = shards[0][:, source : source + width]
            place.greet()
            run(0, *few)
            table = table_rows(table_ref[...].astype(F32)).astype(BF16)
            key_rows()
            run(0, *many)
            spread(0, 4)
            run(1, *few)
            spread(4, 7)
            run(2, *few)
            run(1, *many)
            run(0, *proj, *fc1)
            standard()
            biases(0, HEADS)
            run(3, *few)
            run(4, *few)
            blocks = packed_ref[...].reshape(count * 16, 128)
        else:
            table = table_rows(table_ref[...].astype(F32)).astype(BF16)
            key_rows()
            spread(0, WIN_H)
            standard()
            biases(0, HEADS)
            blocks = packed_ref[...]
        vectors = unpack_vectors(blocks, count, small)
        vec_ref[...] = vectors
        fvec_ref[...] = unpack_vectors(blocks, count, FF // count)[8:9]
        normalize(vectors)
        if direct:
            run(2, *many)
            run(0, *fc2)
        project(0, group_weight(0), vectors)

    if direct:

        @pl.when(head == FEW - 1)
        def _():
            run(3, *many)
            run(1, *proj, *fc1)

    @pl.when(head == FEW)
    def _():
        if direct:
            run(4, *many)
            keep_weight.start()
        project(1, group_weight(1), vec_ref[...])
        hand_on.start()
        if direct:
            run(1, *fc2)
            run(2, *proj, *fc1)

    if direct:
        steps = (
            (9, (2, fc2)),
            (13, (3, proj + fc1)),
            (15, (3, fc2)),
        )
        for at, (stage, group) in steps:

            @pl.when(head == at)
            def _(stage=stage, group=group):
                run(stage, *group)

    row, key_row, value_row = head_rows(head)
    ones = jnp.ones((16, WIN), BF16)
    scores = []
    for w in range(windows):
        queries = qkvt_ref[w, pl.ds(row, HDIM), :WIN]
        keys = qkvt_ref[w, pl.ds(key_row, HDIM), :WIN]
        scores.append(
            dot_tn(
                jnp.concatenate([keys, keyrow_ref[w]], axis=0), jnp.concatenate([queries, ones], axis=0)
            )
        )
    expos = []
    for w in range(windows):
        score = scores[w] + bias_ref[head]
        top = jnp.max(score, axis=0, keepdims=True)
        expos.append(jnp.exp2(score - top).astype(BF16))
        probs_ref[w, 0, :, :WIN] = expos[w]
    for w in range(windows):
        values = qkvt_ref[w, pl.ds(value_row, HDIM), :WIN]
        mixed = dot_nn(jnp.concatenate([values, ones], axis=0), expos[w])
        inverse = 1.0 / mixed[HDIM : HDIM + 1]
        inv_ref[w, pl.ds(head, 1), :WIN] = inverse
        mixed = (mixed[:HDIM] * inverse).astype(BF16)
        attt_out[w, :, :WIN] = mixed
        attt_ref[w, pl.ds(pl.multiple_of(head * HDIM, HDIM), HDIM), :] = mixed

    @pl.when(head == HEADS - 1)
    def _():
        hand_on.wait()
        for w in range(windows):
            for part in range(4):
                rows = slice(part * 128, (part + 1) * 128)
                att_ref[w, :, rows] = attt_ref[w, rows, :].astype(F32).T.astype(BF16)
        if direct:
            keep_weight.wait()
            run(4, *proj, *fc1, *fc2)


def front(inputs, table, extents, vectors, weights, packed, depth, direct):
    windows = inputs.shape[0]
    once = lambda shape: pl.BlockSpec(shape, lambda h: (0,) * len(shape), pipeline_mode=pl.Buffered(1))
    anywhere = pl.BlockSpec(memory_space=pl.ANY)
    outs = [
        (anywhere, jax.ShapeDtypeStruct((windows, 3 * D, LANES), BF16)),
        (
            pl.BlockSpec((windows, 1, WIN, LANES), lambda h: (0, h, 0, 0)),
            jax.ShapeDtypeStruct((windows, HEADS, WIN, LANES), BF16),
        ),
        (once((windows, WIN, D)), jax.ShapeDtypeStruct((windows, WIN, D), BF16)),
        (
            pl.BlockSpec((windows, HDIM, LANES), lambda h: (0, h, 0)),
            jax.ShapeDtypeStruct((windows, D, LANES), BF16),
        ),
        (once((windows, HEADS, LANES)), jax.ShapeDtypeStruct((windows, HEADS, LANES), F32)),
        (once((16, D)), jax.ShapeDtypeStruct((16, D), F32)),
        (once((1, FF)), jax.ShapeDtypeStruct((1, FF), F32)),
    ]
    scratch = [
        pltpu.VMEM((HEADS, FLAT, SPREAD), F32),
        pltpu.VMEM((WIN_W, HEADS, SPREAD), F32),
        pltpu.VMEM((HEADS, WIN, WIN), F32),
        pltpu.VMEM((windows, WIN, D), F32),
        pltpu.VMEM((windows, WIN, D), BF16),
        pltpu.VMEM((windows, 16, WIN), BF16),
        pltpu.VMEM((windows, 3 * D, LANES), BF16),
        pltpu.VMEM((windows, D, WIN), BF16),
        pltpu.SemaphoreType.DMA((1,)),
    ]
    args = [inputs, table, extents]
    small = vectors[0].shape[1]
    extra = {}
    if direct:
        args += list(vectors) + list(weights)
        specs = [once(item.shape) for item in args]
        specs[2] = pl.BlockSpec(memory_space=pltpu.SMEM)
        wholes = [jax.ShapeDtypeStruct((2, 2, depth, 2) + item.shape, BF16) for item in weights]
        outs += [(anywhere, whole) for whole in wholes]
        slots = gather_slots(depth) * (1 + len(QKV_PIECES) + len(OTHER_PIECES)) + 1
        scratch += [
            pltpu.VMEM((16, 128), BF16),
            pltpu.VMEM(weights[0].shape, BF16),
            pltpu.VMEM((2, 2, depth, 2, 16, 128), BF16),
            pltpu.VMEM(wholes[0].shape, BF16),
            pltpu.SemaphoreType.DMA((slots,)),
            pltpu.SemaphoreType.DMA((slots,)),
        ]
        extra = dict(collective_id=0, has_side_effects=True)
    else:
        args += [packed, weights[0]]
        specs = [once(item.shape) for item in args]
        specs[2] = pl.BlockSpec(memory_space=pltpu.SMEM)
    return pl.pallas_call(
        functools.partial(front_kernel, (windows, depth, direct, small)),
        grid=(HEADS,),
        in_specs=specs,
        out_specs=[spec for spec, _ in outs],
        out_shape=[shape for _, shape in outs],
        scratch_shapes=scratch,
        compiler_params=pltpu.CompilerParams(vmem_limit_bytes=60 * MIB, **extra),
        name="front",
    )(*args)


def mlp_kernel(*refs):
    refs = list(refs)
    take = lambda count: [refs.pop(0) for _ in range(count)]
    x_in, att_in, cot_in, proj_in, fc1_in, fc2_in = take(6)
    extents_ref, vec_ref, fshift1_ref = take(3)
    out_out, rgrad_out, agrad_out, fc1g_out, fc2g_out, projg_out = take(6)
    sums_ref, fsum_ref = take(2)
    x_ref, att_ref, gout_ref, proj_ref, fc1_ref, fc2_ref = take(6)
    out_ref, rgrad_ref, agrad_ref, fc1g_ref, fc2g_ref, projg_ref = take(6)
    act_ref, hid_ref, norm_ref, branch_ref, in_sems, out_sems = take(6)
    rows = x_ref.shape[0]
    block = rows // 2
    pieces = 4
    wide = FF // pieces
    halves = [slice(i * block, (i + 1) * block) for i in range(2)]
    loads, stores = {}, []

    def load(name, source, target):
        copy = pltpu.make_async_copy(source, target, in_sems.at[len(loads)])
        copy.start()
        loads[name] = copy

    def store(source, target):
        copy = pltpu.make_async_copy(source, target, out_sems.at[len(stores)])
        copy.start()
        stores.append(copy)

    load("proj", proj_in, proj_ref)
    load("att0", att_in.at[halves[0]], att_ref.at[halves[0]])
    load("x0", x_in.at[halves[0]], x_ref.at[halves[0]])
    load("fc1", fc1_in, fc1_ref)
    load("cot0", cot_in.at[halves[0]], gout_ref.at[halves[0]])
    load("fc2", fc2_in, fc2_ref)
    load("att1", att_in.at[halves[1]], att_ref.at[halves[1]])
    load("x1", x_in.at[halves[1]], x_ref.at[halves[1]])
    load("cot1", cot_in.at[halves[1]], gout_ref.at[halves[1]])
    pshift, gain, shift, fshift2 = [vec_ref[i : i + 1] for i in range(4, 8)]
    sums_ref[...] = jnp.zeros_like(sums_ref)
    fsum_ref[...] = jnp.zeros_like(fsum_ref)

    def keep_column(i):
        spot = spots_of((WIN, 1), 0)
        each = block // WIN
        keeps = [kept(spot, extents_ref, i * each + w).astype(F32) for w in range(each)]
        return jnp.concatenate(keeps, axis=0)

    for i, at in enumerate(halves):
        keep = keep_column(i)
        if i == 0:
            loads["proj"].wait()
        loads[f"att{i}"].wait()
        loads[f"x{i}"].wait()
        resid = x_ref[at, :].astype(F32) + dot_nn(att_ref[at, :], proj_ref[...]) + pshift
        unit, scale = standardize(resid)
        normed = (unit * gain + shift).astype(BF16)
        norm_ref[at, :] = normed
        loads[f"cot{i}"].wait()
        gout = gout_ref[at, :].astype(F32) * keep
        gout_low = gout.astype(BF16)
        gout_ref[at, :] = gout_low
        if i == 0:
            loads["fc1"].wait()
            loads["fc2"].wait()
        total = resid + fshift2
        grad_two = None
        for part in range(pieces):
            columns = slice(part * wide, (part + 1) * wide)
            hidden = dot_nn(normed, fc1_ref[:, columns]) + fshift1_ref[:, columns]
            active, slope = gelu_parts(hidden)
            active = active.astype(BF16)
            act_ref[at, columns] = active
            total = total + dot_nn(active, fc2_ref[columns, :])
            hgrad = (dot_nt(gout_low, fc2_ref[columns, :]) * slope).astype(BF16)
            hid_ref[at, columns] = hgrad
            fsum_ref[0:1, columns] += jnp.sum(hgrad.astype(F32), axis=0, keepdims=True)
            back = dot_nt(hgrad, fc1_ref[:, columns])
            grad_two = back if grad_two is None else grad_two + back
        out_ref[at, :] = (total * keep).astype(BF16)
        store(out_ref.at[at], out_out.at[at])
        rgrad = gout + norm_backward(grad_two, unit, scale, gain)
        rgrad_ref[at, :] = rgrad
        store(rgrad_ref.at[at], rgrad_out.at[at])
        branch = rgrad.astype(BF16)
        branch_ref[at, :] = branch
        agrad_ref[at, :] = dot_nt(branch, proj_ref[...]).astype(BF16)
        store(agrad_ref.at[at], agrad_out.at[at])
        sums_ref[0:1, :] += jnp.sum(gout, axis=0, keepdims=True)
        sums_ref[1:2, :] += jnp.sum(grad_two * unit, axis=0, keepdims=True)
        sums_ref[2:3, :] += jnp.sum(grad_two, axis=0, keepdims=True)
        sums_ref[3:4, :] += jnp.sum(branch.astype(F32), axis=0, keepdims=True)
    for part in range(pieces):
        columns = slice(part * wide, (part + 1) * wide)
        fc2g_ref[columns, :] = dot_tn(act_ref[:, columns], gout_ref[...]).astype(BF16)
        store(fc2g_ref.at[columns], fc2g_out.at[columns])
    for part in range(pieces):
        columns = slice(part * wide, (part + 1) * wide)
        fc1g_ref[:, columns] = dot_tn(norm_ref[...], hid_ref[:, columns]).astype(BF16)
        store(fc1g_ref.at[:, columns], fc1g_out.at[:, columns])
    projg_ref[...] = dot_tn(att_ref[...], branch_ref[...]).astype(BF16)
    store(projg_ref, projg_out)
    for copy in stores:
        copy.wait()


def feed_forward(x_rows, att_rows, cot_rows, proj, fc1, fc2, extents, vectors, fshift1):
    rows = x_rows.shape[0]
    vmem = pl.BlockSpec(memory_space=pltpu.VMEM)
    anywhere = pl.BlockSpec(memory_space=pl.ANY)
    streamed = [
        jax.ShapeDtypeStruct((rows, D), BF16),
        jax.ShapeDtypeStruct((rows, D), F32),
        jax.ShapeDtypeStruct((rows, D), BF16),
        jax.ShapeDtypeStruct((D, FF), BF16),
        jax.ShapeDtypeStruct((FF, D), BF16),
        jax.ShapeDtypeStruct((D, D), BF16),
    ]
    return pl.pallas_call(
        mlp_kernel,
        in_specs=[anywhere] * 6 + [pl.BlockSpec(memory_space=pltpu.SMEM), vmem, vmem],
        out_specs=[anywhere] * 6 + [vmem] * 2,
        out_shape=streamed + [jax.ShapeDtypeStruct((8, D), F32), jax.ShapeDtypeStruct((8, FF), F32)],
        scratch_shapes=[
            pltpu.VMEM((rows, D), BF16),
            pltpu.VMEM((rows, D), BF16),
            pltpu.VMEM((rows, D), BF16),
            pltpu.VMEM((D, D), BF16),
            pltpu.VMEM((D, FF), BF16),
            pltpu.VMEM((FF, D), BF16),
        ]
        + [pltpu.VMEM(item.shape, item.dtype) for item in streamed]
        + [
            pltpu.VMEM((rows, FF), BF16),
            pltpu.VMEM((rows, FF), BF16),
            pltpu.VMEM((rows, D), BF16),
            pltpu.VMEM((rows, D), BF16),
            pltpu.SemaphoreType.DMA((9,)),
            pltpu.SemaphoreType.DMA((15,)),
        ],
        compiler_params=pltpu.CompilerParams(vmem_limit_bytes=62 * MIB),
        name="feed_forward",
    )(x_rows, att_rows, cot_rows, proj, fc1, fc2, extents, vectors, fshift1)


FEED_PIECES = (
    (2, 0, 256, False),
    (2, 256, 256, True),
    (1, 0, 1024, False),
    (1, 1024, 1024, True),
    (0, 0, 256, False),
    (0, 256, 256, True),
)


def back_kernel(setup, *refs):
    windows, depth, direct, small = setup
    refs = list(refs)
    take = lambda count: [refs.pop(0) for _ in range(count)]
    qkvt_in, attt_ref, agrad_ref, inv_ref, probs_ref, x_in, rgrad_in, weight_in = take(8)
    vec_ref, sums_ref, fsum_ref = take(3)
    if direct:
        grads = take(3)
    igrad_ref, table_ref = take(2)
    if direct:
        vec_own, qkv_own, *owns = take(5)
    else:
        qkv_work, vec_work = take(2)
    dot_ref, dqkvt_ref, sum_ref, folded_ref, line_ref, total_ref, dq_ref, norm_ref, grad_ref, csum_ref = take(10)
    qkvt_ref, x_ref, rgrad_ref, weight_ref, hand_sem = take(5)
    if direct:
        qkv_work, vec_work, table_work, table_full = take(4)
        vec_group, vec_z, vec_mine, table_group, table_z, *works = take(8)
        sems = (refs[-2], refs[-1])
        helds = refs[:-2]
    step = pl.program_id(0)
    head = (step + FEW) % HEADS
    count = D // small
    gain, shift = vec_ref[0:1], vec_ref[1:2]
    run = lambda stage, *lists: [stages[stage]() for stages in lists]
    hands = []
    for source, target in (
        (qkvt_in.at[:, STARTS[1] :], qkvt_ref.at[:, STARTS[1] :]),
        (qkvt_in.at[:, : STARTS[1]], qkvt_ref.at[:, : STARTS[1]]),
        (x_in, x_ref),
        (weight_in, weight_ref),
        (rgrad_in, rgrad_ref),
    ):
        hands.append(pltpu.make_async_copy(source, target, hand_sem.at[len(hands)]))

    if direct:
        place = Place(depth)
        base, spot = len(works) + 1, 0

        def piece(work, write, x_first):
            nonlocal base, spot
            stages = scatter_stages(place, work, helds[spot : spot + 4], sems, base, x_first, write)
            base += scatter_slots(depth)
            spot += 4
            return stages

        def whole(own, columns):
            def write(total):
                own[:, columns] = total

            return write

        def unpermuted(start, size):
            def write(total):
                for at in range(start, start + size, 128):
                    group = int(at >= STARTS[1])
                    width = GROUPS[group][1] * HDIM
                    part, rest = divmod(at - STARTS[group], width)
                    to = part * D + GROUPS[group][0] * HDIM + rest
                    qkv_own[:, to : to + 128] = total[:, at - start : at - start + 128]

            return write

        feed = []
        for i, start, size, x_first in FEED_PIECES:
            columns = pl.ds(start, size)
            feed.append(piece(works[i].at[:, :, :, :, :, columns], whole(owns[i], columns), x_first))
        fc2, fc1 = feed[:2], feed[2:]
        qkv = []
        for _, start, size, x_first in QKV_PIECES:
            view = qkv_work.at[:, :, :, :, :, pl.ds(start, size)]
            qkv.append(piece(view, unpermuted(start, size), x_first))
        vector = small_scatter_stages(
            place, vec_work, vec_group, vec_z, vec_mine, sems, base, whole(vec_own, slice(None))
        )
        base += group_slots(depth)
        table = small_sum_stages(place, table_work, table_group, table_z, table_full, sems, base)
        loads = [pltpu.make_async_copy(grads[i], works[i], sems[0].at[i]) for i in range(len(works))]

    def turn_over(group):
        for part in range(3 * GROUPS[group][1] * HDIM // 128):
            rows = slice(STARTS[group] + part * 128, STARTS[group] + (part + 1) * 128)
            columns = slice(part * 128, (part + 1) * 128)
            total = 0.0
            for w in range(windows):
                low = dqkvt_ref[w, rows, :WIN].astype(F32).T
                dq_ref[w, :, columns] = low.astype(BF16)
                total = total + jnp.sum(low, axis=0, keepdims=True)
            csum_ref[0:1, rows] = total

    def weight_grad(index):
        _, start, size, _ = QKV_PIECES[index]
        local = start - STARTS[index // 2]
        total = 0.0
        for w in range(windows):
            total = total + dot_tn(norm_ref[w], dq_ref[w, :, local : local + size])
        columns = slice(start, start + size)
        if direct:
            qkv_work[:, :, :, :, :, columns] = total.astype(BF16).reshape(2, 2, depth, 2, small, size)
        else:
            qkv_work[:, columns] = total.astype(BF16)

    def norm_grad(group, w):
        width = 3 * GROUPS[group][1] * HDIM
        return dot_nt(dq_ref[w, :, :width], weight_ref[:, STARTS[group] : STARTS[group] + width])

    @pl.when(step == 0)
    def _():
        hands[0].start()
        if direct:
            for load in loads:
                load.start()
        for hand in hands[1:]:
            hand.start()
        if direct:
            place.greet(group=True)
        for w in range(windows):
            for part in range(4):
                rows = slice(part * 128, (part + 1) * 128)
                dot_ref[w, rows, :] = agrad_ref[w, :, rows].astype(F32).T.astype(BF16)
        if direct:
            for load in loads:
                load.wait()
            run(0, *fc2, *fc1)
        hands[0].wait()

    @pl.when(step == HEADS - FEW)
    def _():
        if direct:
            run(3, *fc1)
        for hand in hands[1:4]:
            hand.wait()
        for w in range(windows):
            unit, _ = standardize(x_ref[w].astype(F32))
            norm_ref[w] = (unit * gain + shift).astype(BF16)
        turn_over(1)
        for index in (2, 3):
            weight_grad(index)
            if direct:
                run(0, qkv[index])
        total_ref[...] = fold_bias(folded_ref, line_ref, range(FEW, FEW + 8))
        if direct:
            run(1, *qkv[2:])
            run(4, *fc2)
        for w in range(windows):
            grad_ref[w] = norm_grad(1, w)
        if direct:
            run(2, *qkv[2:])
            run(4, *fc1)

    if direct:
        steps = (
            (2, ((1, fc2),)),
            (4, ((1, fc1),)),
            (8, ((2, fc2),)),
            (10, ((2, fc1), (3, fc2))),
            (15, ((3, qkv[2:]),)),
        )
        for at, group in steps:

            @pl.when(step == at)
            def _(group=group):
                for stage, lists in group:
                    run(stage, *lists)

    row, key_row, value_row = head_rows(head)
    own_row = pl.multiple_of(head * HDIM, HDIM)
    ones = jnp.ones((16, WIN), BF16)
    order = spots_of((16, WIN), 0)

    def prepare(w):
        grad = dot_ref[w, pl.ds(own_row, HDIM), :].astype(F32) * inv_ref[w, pl.ds(head, 1), :WIN]
        mixed = attt_ref[w, :, :WIN].astype(F32)
        inner = -jnp.sum(grad * mixed, axis=0, keepdims=True)
        high = inner.astype(BF16).astype(F32)
        middle = (inner - high).astype(BF16).astype(F32)
        lowest = inner - high - middle
        extra = jnp.where(
            order == 0, high, jnp.where(order == 1, middle, jnp.where(order == 2, lowest, 0.0))
        ).astype(BF16)
        grad = grad.astype(BF16)
        values = qkvt_ref[w, pl.ds(value_row, HDIM), :WIN]
        probs_grad = dot_tn(
            jnp.concatenate([values, ones], axis=0), jnp.concatenate([grad, extra], axis=0)
        )
        return grad, probs_grad

    for first in range(0, windows, 2):
        pair = range(first, min(first + 2, windows))
        prepared = [prepare(w) for w in pair]
        expos = [probs_ref[w, 0, :, :WIN] for w in pair]
        grads_s = [expo.astype(F32) * item[1] for expo, item in zip(expos, prepared)]
        total = sum(grads_s[1:], grads_s[0])
        if first == 0:
            sum_ref[...] = total
        else:
            sum_ref[...] += total
        for w, expo, (grad, _), scores_grad in zip(pair, expos, prepared, grads_s):
            low = scores_grad.astype(BF16)
            queries = qkvt_ref[w, pl.ds(row, HDIM), :WIN]
            keys = qkvt_ref[w, pl.ds(key_row, HDIM), :WIN]
            dqkvt_ref[w, pl.ds(row, HDIM), :WIN] = (dot_nn(keys, low) * SCALE).astype(BF16)
            dqkvt_ref[w, pl.ds(key_row, HDIM), :WIN] = (dot_nt(queries, low) * LN2).astype(BF16)
            dqkvt_ref[w, pl.ds(value_row, HDIM), :WIN] = dot_nt(grad, expo).astype(BF16)

    folded_ref[head] = jnp.zeros((FLAT, SPREAD), F32)
    for u in range(WIN_T):
        start = (WIN_T - 1 - u) * FLAT
        folded_ref[head, :, start : start + WIN] += sum_ref[u * FLAT : (u + 1) * FLAT, :]

    @pl.when(step == HEADS - 1)
    def _():
        gain_sum, shift_sum = 0.0, 0.0

        def input_grad(w):
            nonlocal gain_sum, shift_sum
            unit, scale = standardize(x_ref[w].astype(F32))
            grad = grad_ref[w] + norm_grad(0, w)
            igrad_ref[w] = (rgrad_ref[w] + norm_backward(grad, unit, scale, gain)).astype(BF16)
            gain_sum = gain_sum + jnp.sum(grad * unit, axis=0, keepdims=True)
            shift_sum = shift_sum + jnp.sum(grad, axis=0, keepdims=True)

        def vector_block():
            sums = lambda part: jnp.concatenate(
                [
                    csum_ref[0:1, start + part * heads * HDIM : start + (part + 1) * heads * HDIM]
                    for start, (_, heads) in zip(STARTS, GROUPS)
                ],
                axis=1,
            )
            rows = [
                gain_sum,
                shift_sum,
                sums(0),
                sums(2),
                sums_ref[3:4],
                sums_ref[1:2],
                sums_ref[2:3],
                sums_ref[0:1],
            ]
            block = share_vectors(jnp.concatenate(rows, axis=0), count, small)
            last = share_vectors(fsum_ref[0:1], count, FF // count, lane=64)
            return jnp.where(spots_of((count, 8, 128), 1) == 0, block + last, block)

        def write_table(total):
            span = OFFS_H * OFFS_W
            for k in range(OFFS_T):
                table_ref[:, k * span : (k + 1) * span] = total[k * HEADS : (k + 1) * HEADS, :span]

        outer = fold_bias(folded_ref, line_ref, list(range(FEW)) + list(range(FEW + 8, HEADS)))
        total = jnp.concatenate([outer[:, :FEW], total_ref[...], outer[:, FEW:]], axis=1)
        total = total.reshape(OFFS_T * HEADS, 256)
        hands[4].wait()
        if direct:
            total = jnp.concatenate([total, jnp.zeros((256 - OFFS_T * HEADS, 256), F32)], axis=0)
            table_work[...] = total.reshape(table_work.shape)
            run(0, table)
            turn_over(0)
            for index in range(2):
                weight_grad(index)
                run(0, qkv[index])
            input_grad(0)
            run(1, *qkv[:2])
            run(1, table)
            input_grad(1)
            input_grad(2)
            run(2, *qkv[:2])
            input_grad(3)
            vec_work[...] = vector_block().reshape(vec_work.shape)
            run(0, vector)
            run(2, table)
            run(3, *qkv[:2])
            run(4, *qkv[2:])
            run(1, vector)
            run(3, table)
            write_table(table_full[...].reshape(256, 256))
            run(4, *qkv[:2])
            run(2, vector)
        else:
            turn_over(0)
            weight_grad(0)
            weight_grad(1)
            for w in range(windows):
                input_grad(w)
            vec_work[...] = vector_block()
            write_table(total)


def back(qkvt, attt, agrad, inverse, probs, inputs, rgrad, weight, vectors, sums, fsum, grads, depth, direct):
    windows = qkvt.shape[0]
    count = lax.axis_size("dp") * lax.axis_size("fsdp")
    small = D // count
    once = lambda shape: pl.BlockSpec(shape, lambda h: (0,) * len(shape), pipeline_mode=pl.Buffered(1))
    anywhere = pl.BlockSpec(memory_space=pl.ANY)
    args = [qkvt, attt, agrad, inverse, probs, inputs, rgrad, weight, vectors, sums, fsum]
    specs = [once(item.shape) for item in args]
    specs[1] = pl.BlockSpec((windows, HDIM, LANES), lambda h: (0, (h + FEW) % HEADS, 0))
    specs[4] = pl.BlockSpec((windows, 1, WIN, LANES), lambda h: (0, (h + FEW) % HEADS, 0, 0))
    for i in (0, 5, 6, 7):
        specs[i] = anywhere
    shapes = [
        jax.ShapeDtypeStruct(inputs.shape, BF16),
        jax.ShapeDtypeStruct((HEADS, OFFS_T * OFFS_H * OFFS_W), F32),
    ]
    scratch = [
        pltpu.VMEM((windows, D, WIN), BF16),
        pltpu.VMEM((windows, 3 * D, LANES), BF16),
        pltpu.VMEM((WIN, WIN), F32),
        pltpu.VMEM((HEADS, FLAT, SPREAD), F32),
        pltpu.VMEM((WIN_W, 8, SPREAD), F32),
        pltpu.VMEM((OFFS_T, 8, 256), F32),
        pltpu.VMEM((windows, WIN, WIDE), BF16),
        pltpu.VMEM((windows, WIN, D), BF16),
        pltpu.VMEM((windows, WIN, D), F32),
        pltpu.VMEM((8, 3 * D), F32),
        pltpu.VMEM(qkvt.shape, BF16),
        pltpu.VMEM(inputs.shape, BF16),
        pltpu.VMEM(rgrad.shape, F32),
        pltpu.VMEM(weight.shape, BF16),
        pltpu.SemaphoreType.DMA((5,)),
    ]
    extra = {}
    if direct:
        lead = (2, 2, depth, 2)
        views = [item.reshape(lead + (-1, item.shape[1])) for item in grads]
        args += views
        specs += [anywhere] * len(views)
        shapes += [
            jax.ShapeDtypeStruct((8, 128), F32),
            jax.ShapeDtypeStruct((small, 3 * D), F32),
        ] + [jax.ShapeDtypeStruct(item.shape[-2:], F32) for item in views]
        scratch += [
            pltpu.VMEM(lead + (small, 3 * D), BF16),
            pltpu.VMEM(lead + (8, 128), F32),
            pltpu.VMEM((2, 2, 2, 32, 256), F32),
            pltpu.VMEM((2, 2, 2, 32, 256), F32),
            pltpu.VMEM((7, depth, 8, 128), F32),
            pltpu.VMEM((depth - 1, 8, 128), F32),
            pltpu.VMEM((depth, 8, 128), F32),
            pltpu.VMEM((7, 32, 256), F32),
            pltpu.VMEM((depth, 32, 256), F32),
        ] + [pltpu.VMEM(item.shape, BF16) for item in views]
        for i, _, size, x_first in FEED_PIECES:
            scratch += held_shapes(depth, views[i].shape[-2], size, BF16, x_first)
        for _, _, size, x_first in QKV_PIECES:
            scratch += held_shapes(depth, small, size, BF16, x_first)
        exchanges = len(FEED_PIECES) + len(QKV_PIECES)
        slots = len(views) + 1 + scatter_slots(depth) * exchanges + 2 * group_slots(depth) + 7
        scratch += [pltpu.SemaphoreType.DMA((slots,)), pltpu.SemaphoreType.DMA((slots,))]
        extra = dict(collective_id=1, has_side_effects=True)
    else:
        shapes += [
            jax.ShapeDtypeStruct((D, 3 * D), BF16),
            jax.ShapeDtypeStruct((count, 8, 128), F32),
        ]
    return pl.pallas_call(
        functools.partial(back_kernel, (windows, depth, direct, small)),
        grid=(HEADS,),
        in_specs=specs,
        out_specs=[once(item.shape) for item in shapes],
        out_shape=shapes,
        scratch_shapes=scratch,
        compiler_params=pltpu.CompilerParams(vmem_limit_bytes=63 * MIB, **extra),
        name="back",
    )(*args)


def hand_kernel(small, vec_ref, *refs):
    count = (len(refs) - 11) // 3
    sources, vectors, targets = refs[:count], refs[count : count + 9], refs[count + 9 : 2 * count + 9]
    holds, ins, outs = refs[2 * count + 9 : -2], refs[-2], refs[-1]
    first = [pltpu.make_async_copy(sources[i], holds[i], ins.at[i]) for i in range(count)]
    second = [pltpu.make_async_copy(holds[i], targets[i], outs.at[i]) for i in range(count)]
    for copy in first:
        copy.start()
    for i in range(8):
        vectors[i][...] = vec_ref[i : i + 1, :small]
    vectors[8][...] = vec_ref[0:1, 64 : 64 + vectors[8].shape[1]]
    for one, two in zip(first, second):
        one.wait()
        two.start()
    for copy in second:
        copy.wait()


def hand_over(vector_own, items, small):
    vmem = pl.BlockSpec(memory_space=pltpu.VMEM)
    anywhere = pl.BlockSpec(memory_space=pl.ANY)
    vectors = [jax.ShapeDtypeStruct((1, small), F32)] * 8 + [jax.ShapeDtypeStruct((1, 4 * small), F32)]
    semaphores = pltpu.SemaphoreType.DMA((len(items),))
    return pl.pallas_call(
        functools.partial(hand_kernel, small),
        in_specs=[vmem] + [anywhere] * len(items),
        out_specs=[vmem] * 9 + [anywhere] * len(items),
        out_shape=vectors + [jax.ShapeDtypeStruct(item.shape, item.dtype) for item in items],
        scratch_shapes=[pltpu.VMEM(item.shape, item.dtype) for item in items] + [semaphores, semaphores],
        compiler_params=pltpu.CompilerParams(vmem_limit_bytes=62 * MIB),
        name="hand_over",
    )(vector_own, *items)


def gathered(value):
    return lax.all_gather(value, AXES, axis=0, tiled=True)


def scattered(value):
    return lax.psum_scatter(value, AXES, scatter_dimension=0, tiled=True)


def per_device(
    inputs,
    extents,
    cotangent,
    ln1_gain,
    ln1_shift,
    qkv_weight,
    query_bias,
    value_bias,
    bias_table,
    proj_weight,
    proj_shift,
    ln2_gain,
    ln2_shift,
    fc1_weight,
    fc1_shift,
    fc2_weight,
    fc2_shift,
):
    windows = inputs.shape[0]
    rows = windows * WIN
    small = ln1_gain.shape[0]
    count = D // small
    depth = lax.axis_size("fsdp") // 2
    direct = small % 16 == 0 and lax.axis_size("dp") == 4
    vectors = [
        item[None]
        for item in (
            ln1_gain,
            ln1_shift,
            query_bias,
            value_bias,
            proj_shift,
            ln2_gain,
            ln2_shift,
            fc2_shift,
            fc1_shift,
        )
    ]
    weights = (qkv_weight, proj_weight, fc1_weight, fc2_weight)
    packed = None
    if not direct:
        packed = jnp.concatenate([jnp.pad(item, ((0, 0), (0, 128 - item.shape[1]))) for item in vectors])
        packed = gathered(jnp.pad(packed, ((0, 16 - len(vectors)), (0, 0))))
        weights = [gathered(item) for item in weights]
        parts = weights[0].reshape(D, 3, D)
        cut = FEW * HDIM
        weights[0] = jnp.concatenate(
            [parts[:, :, :cut].reshape(D, 3 * cut), parts[:, :, cut:].reshape(D, 3 * (D - cut))], axis=1
        )
    x_rows = inputs.reshape(rows, D)
    qkvt, probs, att, attt, inverse, full_vectors, fshift1, *wholes = front(
        inputs, bias_table.T, extents, vectors, weights, packed, depth, direct
    )
    if direct:
        weights = [item.reshape(-1, item.shape[-1]) for item in wholes]
    qkv_full, proj_full, fc1_full, fc2_full = weights
    output, rgrad, agrad, fc1_grad, fc2_grad, proj_grad, sums, fsum = feed_forward(
        x_rows,
        att.reshape(rows, D),
        cotangent.reshape(rows, D),
        proj_full,
        fc1_full,
        fc2_full,
        extents,
        full_vectors,
        fshift1,
    )
    matrices = (proj_grad, fc1_grad, fc2_grad)
    input_grad, table_grad, *rest = back(
        qkvt,
        attt,
        agrad.reshape(windows, WIN, D),
        inverse,
        probs,
        inputs,
        rgrad.reshape(windows, WIN, D),
        qkv_full,
        full_vectors,
        sums,
        fsum,
        matrices,
        depth,
        direct,
    )
    if direct:
        vector_own, *items = rest
        items = [input_grad, table_grad] + items
        *owned, input_grad, table_grad, qkv_own, proj_own, fc1_own, fc2_own = hand_over(
            vector_own, items, small
        )
        owned = [item.reshape(-1) for item in owned]
    else:
        cut = FEW * HDIM
        qkv_grad = jnp.concatenate(
            [rest[0][:, : 3 * cut].reshape(D, 3, cut), rest[0][:, 3 * cut :].reshape(D, 3, D - cut)], axis=2
        ).reshape(D, 3 * D)
        qkv_own, proj_own, fc1_own, fc2_own = [
            scattered(item.astype(F32)) for item in (qkv_grad,) + matrices
        ]
        vector_own = scattered(rest[1])[0]
        owned = [vector_own[i, :small] for i in range(8)] + [vector_own[0, 64 : 64 + FF // count]]
        table_grad = lax.psum(table_grad, AXES)
    return (
        output.reshape(inputs.shape),
        input_grad.reshape(inputs.shape),
        owned[0],
        owned[1],
        qkv_own,
        owned[2],
        owned[3],
        table_grad.T,
        proj_own,
        owned[4],
        owned[5],
        owned[6],
        fc1_own,
        owned[8],
        fc2_own,
        owned[7],
    )


def solution(mesh):
    rows = P(AXES, None)
    vector = P(AXES)
    block = P(AXES, None, None)
    in_specs = (
        block,
        rows,
        block,
        vector,
        vector,
        rows,
        vector,
        vector,
        P(),
        rows,
        vector,
        vector,
        vector,
        rows,
        vector,
        rows,
        vector,
    )
    out_specs = (
        block,
        block,
        vector,
        vector,
        rows,
        vector,
        vector,
        P(),
        rows,
        vector,
        vector,
        vector,
        rows,
        vector,
        rows,
        vector,
    )
    return jax.shard_map(
        per_device, mesh=mesh, in_specs=in_specs, out_specs=out_specs, check_vma=False
    )
```

```python
import functools
import math

import jax
import jax.numpy as jnp
import numpy as np
from jax import lax
from jax.experimental import pallas as pl
from jax.experimental.pallas import tpu as pltpu
from jax.sharding import PartitionSpec as P

D = 512
HEADS = 16
HDIM = 32
FF = 2048
WIN_T = 8
WIN_H = 7
WIN_W = 7
WIN = WIN_T * WIN_H * WIN_W
FLAT = WIN_H * WIN_W
OFFS_T = 2 * WIN_T - 1
OFFS_H = 2 * WIN_H - 1
OFFS_W = 2 * WIN_W - 1
SPREAD = OFFS_T * FLAT
LANES = 512
FEW = 4
GROUPS = ((0, FEW), (FEW, HEADS - FEW))
STARTS = (0, 3 * FEW * HDIM)
WIDE = 3 * (HEADS - FEW) * HDIM
EPS = 1e-05
LOG2E = math.log2(math.e)
LN2 = math.log(2.0)
SCALE = HDIM ** (-0.5)
AXES = ("dp", "fsdp")
BF16 = jnp.bfloat16
F32 = jnp.float32
MIB = 2**20


def dot(left, right, left_dim, right_dim):
    return lax.dot_general(
        left, right, (((left_dim,), (right_dim,)), ((), ())), preferred_element_type=F32
    )


def dot_nn(left, right):
    return dot(left, right, 1, 0)


def dot_nt(left, right):
    return dot(left, right, 1, 1)


def dot_tn(left, right):
    return dot(left, right, 0, 0)


def standardize(rows):
    average = jnp.mean(rows, axis=-1, keepdims=True)
    centered = rows - average
    variance = jnp.mean(centered * centered, axis=-1, keepdims=True)
    scale = lax.rsqrt(variance + EPS)
    return centered * scale, scale


def norm_backward(grad, unit, scale, gain):
    scaled = grad * gain
    first = jnp.mean(scaled, axis=-1, keepdims=True)
    second = jnp.mean(scaled * unit, axis=-1, keepdims=True)
    return (scaled - first - unit * second) * scale


def gelu_parts(hidden):
    below = 0.5 * lax.erf(hidden * (0.5**0.5)) + 0.5
    bell = jnp.exp2(hidden * hidden * (-0.5 * LOG2E)) * (1.0 / math.sqrt(2 * math.pi))
    return hidden * below, below + hidden * bell


class Place:
    def __init__(self, depth):
        dp, fsdp = lax.axis_index("dp"), lax.axis_index("fsdp")
        self.depth = depth
        self.y, self.c = dp // 2, dp % 2
        self.z, self.x = fsdp // 2, fsdp % 2
        self.core = (self.y * 2 + 1 - self.c, fsdp)
        self.across_x = (dp, self.z * 2 + 1 - self.x)
        self.across_y = ((1 - self.y) * 2 + self.c, fsdp)
        self.along_z = [(dp, ((self.z + j) % depth) * 2 + self.x) for j in range(1, depth)]
        self.group = []
        for j in range(1, 8):
            y = 1 - self.y if j & 4 else self.y
            c = 1 - self.c if j & 2 else self.c
            x = 1 - self.x if j & 1 else self.x
            self.group.append(((y, c, x), (y * 2 + c, self.z * 2 + x)))

    def greet(self, group=False):
        barrier = pltpu.get_barrier_semaphore()
        partners = [self.core, self.across_x, self.across_y] + self.along_z
        if group:
            partners = [device for _, device in self.group] + self.along_z
        for partner in partners:
            pl.semaphore_signal(barrier, inc=1, device_id=partner, device_id_type=pl.DeviceIdType.MESH)
        return lambda: pl.semaphore_wait(barrier, len(partners))


def send(source, target, sems, slot, device):
    return pltpu.make_async_remote_copy(
        src_ref=source,
        dst_ref=target,
        send_sem=sems[0].at[slot],
        recv_sem=sems[1].at[slot],
        device_id=device,
        device_id_type=pl.DeviceIdType.MESH,
    )


def gather_slots(depth):
    return depth + 5


def gather_stages(place, own, full, sems, base, y_first):
    y, c, z, x, depth = place.y, place.c, place.z, place.x, place.depth
    every = slice(None)
    here = full(y, c, z, x)
    local = pltpu.make_async_copy(own, here, sems[0].at[base])
    along = [send(own, here, sems, base + j, place.along_z[j - 1]) for j in range(1, depth)]
    column = full(y, c, every, x)
    if y_first:
        first = send(column, column, sems, base + depth, place.across_y)
        both = full(every, c, every, x)
        second = send(both, both, sems, base + depth + 1, place.across_x)
        one = full(1 - y, c, every, x)
        two = full(every, c, every, 1 - x)
    else:
        first = send(column, column, sems, base + depth, place.across_x)
        both = full(y, c, every, every)
        second = send(both, both, sems, base + depth + 1, place.across_y)
        one = full(y, c, every, 1 - x)
        two = full(1 - y, c, every, every)
    shares = [
        send(part, part, sems, base + depth + 2 + k, place.core) for k, part in enumerate((column, one, two))
    ]

    def begin():
        local.start()
        for copy in along:
            copy.start()

    def turn():
        local.wait()
        for copy in along:
            copy.wait_recv()
        first.start()
        shares[0].start()

    def cross():
        first.wait_recv()
        second.start()
        shares[1].start()

    def share():
        second.wait_recv()
        shares[2].start()

    def finish():
        for copy in shares:
            copy.wait()
        for copy in along + [first, second]:
            copy.wait_send()

    return [begin, turn, cross, share, finish]


def scatter_slots(depth):
    return depth + 2


def add_into(target, index, extra):
    target[index] = (target[index].astype(F32) + extra.astype(F32)).astype(target.dtype)


def scatter_stages(place, parts, held, sems, base, x_first, write):
    y, c, z, x, depth = place.y, place.c, place.z, place.x, place.depth
    every = slice(None)
    from_core, from_first, from_second, from_z = held
    share = send(parts.at[:, 1 - c], from_core, sems, base, place.core)
    if x_first:
        first = send(parts.at[:, c, :, 1 - x], from_first, sems, base + 1, place.across_x)
        second = send(parts.at[1 - y, c, :, x], from_second, sems, base + 2, place.across_y)
    else:
        first = send(parts.at[1 - y, c], from_first, sems, base + 1, place.across_y)
        second = send(parts.at[y, c, :, 1 - x], from_second, sems, base + 2, place.across_x)
    along = [
        send(
            parts.at[y, c, (z + j) % depth, x],
            from_z.at[j - 1],
            sems,
            base + 2 + j,
            place.along_z[j - 1],
        )
        for j in range(1, depth)
    ]

    def begin():
        share.start()

    def cross():
        share.wait_recv()
        for yy in range(2):
            add_into(parts, (yy, c), from_core[yy])
        first.start()

    def turn():
        first.wait_recv()
        if x_first:
            for yy in range(2):
                for zz in range(depth):
                    add_into(parts, (yy, c, zz, x), from_first[yy, zz])
        else:
            add_into(parts, (y, c), from_first[...])
        second.start()

    def spread():
        second.wait_recv()
        for zz in range(depth):
            add_into(parts, (y, c, zz, x), from_second[zz])
        for copy in along:
            copy.start()

    def finish():
        for copy in along:
            copy.wait_recv()
        total = parts[y, c, z, x].astype(F32)
        for j in range(depth - 1):
            total = total + from_z[j].astype(F32)
        write(total)
        for copy in along + [share, first, second]:
            copy.wait_send()

    return [begin, cross, turn, spread, finish]


def group_slots(depth):
    return 7 + depth - 1


def sum_in_group(place, own, others):
    total = own
    for j in range(7):
        total = total + others[j]
    return total


def small_scatter_stages(place, parts, from_group, from_z, mine, sems, base, write):
    y, c, z, x, depth = place.y, place.c, place.z, place.x, place.depth
    hops = []
    for j, ((yy, cc, xx), device) in enumerate(place.group):
        hops.append(send(parts.at[yy, cc, :, xx], from_group.at[j], sems, base + j, device))
    along = [
        send(mine.at[(z + j) % depth], from_z.at[j - 1], sems, base + 6 + j, place.along_z[j - 1])
        for j in range(1, depth)
    ]

    def begin():
        for copy in hops:
            copy.start()

    def turn():
        for copy in hops:
            copy.wait_recv()
        for zz in range(depth):
            mine[zz] = sum_in_group(place, parts[y, c, zz, x], [from_group[j, zz] for j in range(7)])
        for copy in along:
            copy.start()

    def finish():
        for copy in along:
            copy.wait_recv()
        total = mine[z]
        for j in range(depth - 1):
            total = total + from_z[j]
        write(total)
        for copy in hops + along:
            copy.wait_send()

    return [begin, turn, finish]


def small_sum_stages(place, parts, from_group, from_z, full, sems, base):
    y, c, z, x, depth = place.y, place.c, place.z, place.x, place.depth
    hops = []
    for j, ((yy, cc, xx), device) in enumerate(place.group):
        hops.append(send(parts.at[yy, cc, xx], from_group.at[j], sems, base + j, device))
    along = [
        send(from_z.at[z], from_z.at[z], sems, base + 6 + j, place.along_z[j - 1]) for j in range(1, depth)
    ]
    here = full.at[y, c, x]
    spread = [
        send(here, here, sems, base + group_slots(depth) + j, device)
        for j, (_, device) in enumerate(place.group)
    ]

    def begin():
        for copy in hops:
            copy.start()

    def turn():
        for copy in hops:
            copy.wait_recv()
        from_z[z] = sum_in_group(place, parts[y, c, x], from_group)
        for copy in along:
            copy.start()

    def share():
        for copy in along:
            copy.wait_recv()
        total = from_z[0]
        for zz in range(1, depth):
            total = total + from_z[zz]
        full[y, c, x] = total
        for copy in spread:
            copy.start()

    def finish():
        for copy in spread:
            copy.wait_recv()
        for copy in hops + along + spread:
            copy.wait_send()

    return [begin, turn, share, finish]


def held_shapes(depth, rows, columns, dtype, x_first):
    first = (2, depth, rows, columns) if x_first else (depth, 2, rows, columns)
    return [
        pltpu.VMEM((2, depth, 2, rows, columns), dtype),
        pltpu.VMEM(first, dtype),
        pltpu.VMEM((depth, rows, columns), dtype),
        pltpu.VMEM((depth - 1, rows, columns), dtype),
    ]


def spots_of(shape, axis):
    return lax.broadcasted_iota(jnp.int32, shape, axis)


def pack_vectors(vectors):
    rows = spots_of((16, 128), 0)
    block = jnp.zeros((16, 128), F32)
    for i, vector in enumerate(vectors):
        vector = vector.astype(F32)
        if vector.shape[1] < 128:
            vector = jnp.concatenate([vector, jnp.zeros((1, 128 - vector.shape[1]), F32)], axis=1)
        block = jnp.where(rows == i, vector, block)
    return block


def unpack_vectors(blocks, count, small):
    width = count * small
    lanes, columns = spots_of((128, width), 0), spots_of((128, width), 1)
    choice = ((columns & (small - 1)) == lanes).astype(BF16)
    wide = dot_nn(blocks, choice).reshape(count, 16, width)
    owner = spots_of((count, 16, width), 0)
    column = spots_of((count, 16, width), 2)
    low = owner * small
    return jnp.sum(jnp.where((column >= low) & (column < low + small), wide, 0.0), axis=0)


def unpack_row(blocks, row, count, small):
    width = count * small
    lanes, columns = spots_of((128, width), 0), spots_of((128, width), 1)
    choice = ((columns & (small - 1)) == lanes).astype(BF16)
    wide = dot_nn(blocks.astype(F32).reshape(count, 16, 128)[:, row].astype(BF16), choice)
    low, column = spots_of((count, width), 0) * small, spots_of((count, width), 1)
    return jnp.sum(jnp.where((column >= low) & (column < low + small), wide, 0.0), axis=0, keepdims=True)


def share_row(row, count, small, lane):
    width = count * small
    lanes, columns = spots_of((128, width), 0), spots_of((128, width), 1)
    choice = ((columns & (small - 1)) + lane == lanes).astype(BF16)
    low, column = spots_of((count, width), 0) * small, spots_of((count, width), 1)
    wide = jnp.where((column >= low) & (column < low + small), row, 0.0)
    block = 0.0
    for _ in range(3):
        part = wide.astype(BF16)
        block = block + dot_nt(part, choice)
        wide = wide - part.astype(F32)
    return block


def frame_spots(shape, axis):
    spot = spots_of(shape, axis)
    row = jnp.zeros(shape, jnp.int32)
    for i in range(1, WIN_H):
        row += (spot >= i * WIN_W).astype(jnp.int32)
    return (row + WIN_H - 1) * OFFS_W + spot - row * WIN_W + WIN_W - 1


def table_rows(table):
    span = OFFS_H * OFFS_W
    return jnp.concatenate([table[:, k * span : (k + 1) * span] for k in range(OFFS_T)], axis=0)


def kept(spot, extents_ref, window):
    frame = jnp.zeros(spot.shape, jnp.int32)
    for i in range(1, WIN_T):
        frame += (spot >= i * FLAT).astype(jnp.int32)
    rest = spot - frame * FLAT
    row = jnp.zeros(spot.shape, jnp.int32)
    for i in range(1, WIN_H):
        row += (rest >= i * WIN_W).astype(jnp.int32)
    column = rest - row * WIN_W
    return (
        (frame < extents_ref[window, 0])
        & (row < extents_ref[window, 1])
        & (column < extents_ref[window, 2])
    )


def spread_bias(table, spread_ref, line_ref, begin, end):
    span = OFFS_H * OFFS_W
    base = frame_spots((span, FLAT), 1) - spots_of((span, FLAT), 0)

    def one(v, carry):
        for e in range(WIN_W):
            choice = jnp.where(base == v * OFFS_W + e, 1.0, 0.0).astype(BF16)
            wide = dot_nn(table, choice) * LOG2E
            for k in range(OFFS_T):
                line_ref[e, :, k * FLAT : (k + 1) * FLAT] = wide[k * HEADS : (k + 1) * HEADS]
            for h in range(HEADS):
                spread_ref[h, pl.ds(v * WIN_W + e, 1), :] = line_ref[e, h : h + 1, :]
        return carry

    lax.fori_loop(begin, end, one, 0)


def fold_bias(folded_ref, line_ref, heads):
    base = frame_spots((FLAT, 256), 0) - spots_of((FLAT, 256), 1)

    def one(v, total):
        for e in range(WIN_W):
            choice = jnp.where(base == v * OFFS_W + e, 1.0, 0.0).astype(BF16)
            for i, h in enumerate(heads):
                line_ref[e, i : i + 1, :] = folded_ref[h, pl.ds(v * WIN_W + e, 1), :]
            wide = jnp.concatenate(
                [line_ref[e, :, k * FLAT : (k + 1) * FLAT] for k in range(OFFS_T)], axis=0
            )
            high = wide.astype(BF16)
            total = total + dot_nn(high, choice) + dot_nn((wide - high.astype(F32)).astype(BF16), choice)
        return total

    total = lax.fori_loop(0, WIN_H, one, jnp.zeros((OFFS_T * 8, 256), F32))
    return total.reshape(OFFS_T, 8, 256)


def share_vectors(rows, count, small):
    kinds, width = rows.shape
    lanes, columns = spots_of((128, width), 0), spots_of((128, width), 1)
    choice = ((columns & (small - 1)) == lanes).astype(BF16)
    low = spots_of((count, kinds, width), 0) * small
    column = spots_of((count, kinds, width), 2)
    wide = jnp.where((column >= low) & (column < low + small), rows[None], 0.0)
    wide = wide.reshape(count * kinds, width)
    blocks = 0.0
    for _ in range(3):
        part = wide.astype(BF16)
        blocks = blocks + dot_nt(part, choice)
        wide = wide - part.astype(F32)
    return blocks.reshape(count, kinds, 128)


QKV_PIECES = ((1, 0, 256, False), (1, 256, 128, True), (1, 384, 640, True), (1, 1024, 512, False))
OTHER_PIECES = (
    (2, 0, 256, False),
    (2, 256, 256, True),
    (3, 0, 1024, False),
    (3, 1024, 1024, True),
    (4, 0, 256, False),
    (4, 256, 256, True),
)


def head_rows(head):
    late = (head >= FEW).astype(jnp.int32)
    row = head * HDIM + late * (STARTS[1] - FEW * HDIM)
    step = FEW * HDIM + late * ((HEADS - 2 * FEW) * HDIM)
    return [pl.multiple_of(row + part * step, HDIM) for part in range(3)]


def front_kernel(setup, *refs):
    windows, depth, direct, small = setup
    refs = list(refs)
    take = lambda count: [refs.pop(0) for _ in range(count)]
    x_in, table_ref, extents_ref = take(3)
    if direct:
        vector_refs, shards = take(9), take(4)
    else:
        packed_ref, weight_in = take(2)
    qkvt_out, probs_ref, att_ref, attt_out, inv_ref, vec_ref, fvec_ref = take(7)
    if direct:
        wholes = take(4)
    spread_ref, line_ref, bias_ref, unit_ref, norm_ref, keyrow_ref, qkvt_ref, attt_ref, x_ref, hand_sem = take(10)
    if direct:
        pack_ref, own_ref, packed_ref, weight_ref, *sems = take(6)
    head = pl.program_id(0)
    count = D // small
    run = lambda stage, *lists: [stages[stage]() for stages in lists]
    hand_on = pltpu.make_async_copy(qkvt_ref, qkvt_out, hand_sem.at[0])
    bring = pltpu.make_async_copy(x_in, x_ref, hand_sem.at[1])

    if direct:
        place = Place(depth)
        views = [packed_ref, weight_ref] + wholes[1:]
        sources = [pack_ref, own_ref] + shards[1:]
        lists = []
        for index, start, size, y_first in ((0, 0, 128, False),) + QKV_PIECES + OTHER_PIECES:
            columns = pl.ds(start, size)
            view = lambda y, c, z, x, whole=views[index], columns=columns: whole.at[y, c, z, x, :, columns]
            base = gather_slots(depth) * len(lists)
            lists.append(gather_stages(place, sources[index].at[:, columns], view, sems, base, y_first))
        few, many, proj, fc1, fc2 = lists[:3], lists[3:5], lists[5:7], lists[7:9], lists[9:]
        keep_weight = pltpu.make_async_copy(weight_ref, wholes[0], sems[0].at[gather_slots(depth) * len(lists)])

    def project(group, weight, vectors):
        head_start, heads = GROUPS[group]
        width = heads * HDIM
        own = slice(head_start * HDIM, head_start * HDIM + width)
        bias = jnp.concatenate(
            [vectors[2:3, own] * (SCALE * LOG2E), jnp.zeros((1, width), F32), vectors[3:4, own]], axis=1
        )
        factor = jnp.where(spots_of((1, 3 * width), 1) < width, SCALE * LOG2E, 1.0)
        for w in range(windows):
            for start in range(0, 3 * width, 256):
                end = min(start + 256, 3 * width)
                got = dot_nn(norm_ref[w], weight[:, start:end])
                got = got * factor[:, start:end] + bias[:, start:end]
                for piece in range((end - start) // 128):
                    at = STARTS[group] + start + piece * 128
                    qkvt_ref[w, at : at + 128, :WIN] = got[:, piece * 128 : (piece + 1) * 128].T.astype(BF16)

    def group_weight(group):
        start, width = STARTS[group], 3 * GROUPS[group][1] * HDIM
        if not direct:
            return weight_in[:, start : start + width]
        return weight_ref[:, :, :, :, :, start : start + width].reshape(D, width)

    def standard():
        bring.wait()
        for w in range(windows):
            unit_ref[w], _ = standardize(x_ref[w].astype(F32))

    def normalize(vectors):
        for w in range(windows):
            norm_ref[w] = (unit_ref[w] * vectors[0:1] + vectors[1:2]).astype(BF16)

    def biases(begin, end):
        def one(h, carry):
            for u in range(WIN_T):
                start = (WIN_T - 1 - u) * FLAT
                bias_ref[h, u * FLAT : (u + 1) * FLAT, :] = spread_ref[h, :, start : start + WIN]
            return carry

        lax.fori_loop(begin, end, one, 0)

    def key_rows():
        spot, line = spots_of((16, WIN), 1), spots_of((16, WIN), 0)
        for w in range(windows):
            keyrow_ref[w] = jnp.where(kept(spot, extents_ref, w) | (line > 0), 0.0, -1e30).astype(BF16)

    @pl.when(head == 0)
    def _():
        spread = lambda begin, end: spread_bias(table, spread_ref, line_ref, begin, end)
        if direct:
            welcome = place.greet()
        bring.start()
        if direct:
            pack_ref[...] = pack_vectors([ref[...] for ref in vector_refs]).astype(BF16)
            for part in range(3):
                for group, (head_start, heads) in enumerate(GROUPS):
                    width = heads * HDIM
                    start = STARTS[group] + part * width
                    source = part * D + head_start * HDIM
                    own_ref[:, start : start + width] = shards[0][:, source : source + width]
            welcome()
            run(0, *few)
            table = table_rows(table_ref[...].astype(F32)).astype(BF16)
            key_rows()
            run(0, *many)
            spread(0, 4)
            run(1, *few)
            spread(4, 7)
            run(2, *few)
            run(1, *many)
            run(0, *proj, *fc1)
            standard()
            biases(0, HEADS)
            run(3, *few)
            run(4, *few)
            blocks = packed_ref[...].reshape(count * 16, 128)
        else:
            table = table_rows(table_ref[...].astype(F32)).astype(BF16)
            key_rows()
            spread(0, WIN_H)
            standard()
            biases(0, HEADS)
            blocks = packed_ref[...]
        vectors = unpack_vectors(blocks, count, small)
        vec_ref[...] = vectors
        fvec_ref[...] = unpack_row(blocks, 8, count, FF // count)
        normalize(vectors)
        if direct:
            run(2, *many)
            run(0, *fc2)
        project(0, group_weight(0), vectors)

    if direct:

        @pl.when(head == FEW - 1)
        def _():
            run(3, *many)

        @pl.when(head == FEW - 2)
        def _():
            run(1, *proj, *fc1)

    @pl.when(head == FEW)
    def _():
        if direct:
            run(4, *many)
            keep_weight.start()
        project(1, group_weight(1), vec_ref[...])
        hand_on.start()
        if direct:
            run(1, *fc2)
            run(2, *proj, *fc1)

    if direct:
        steps = (
            (8, (2, fc2)),
            (12, (3, proj + fc1)),
            (15, (3, fc2)),
        )
        for at, (stage, group) in steps:

            @pl.when(head == at)
            def _(stage=stage, group=group):
                run(stage, *group)

    row, key_row, value_row = head_rows(head)
    ones = jnp.ones((16, WIN), BF16)
    scores = []
    for w in range(windows):
        queries = qkvt_ref[w, pl.ds(row, HDIM), :WIN]
        keys = qkvt_ref[w, pl.ds(key_row, HDIM), :WIN]
        scores.append(
            dot_tn(
                jnp.concatenate([keys, keyrow_ref[w]], axis=0), jnp.concatenate([queries, ones], axis=0)
            )
        )
    expos = []
    for w in range(windows):
        score = scores[w] + bias_ref[head]
        top = jnp.max(score, axis=0, keepdims=True)
        expos.append(jnp.exp2(score - top).astype(BF16))
        probs_ref[w, 0, :, :WIN] = expos[w]
    for w in range(windows):
        values = qkvt_ref[w, pl.ds(value_row, HDIM), :WIN]
        mixed = dot_nn(jnp.concatenate([values, ones], axis=0), expos[w])
        inverse = 1.0 / mixed[HDIM : HDIM + 1]
        inv_ref[w, pl.ds(head, 1), :WIN] = inverse
        mixed = (mixed[:HDIM] * inverse).astype(BF16)
        attt_out[w, :, :WIN] = mixed
        attt_ref[w, pl.ds(pl.multiple_of(head * HDIM, HDIM), HDIM), :] = mixed

    @pl.when(head == HEADS - 1)
    def _():
        hand_on.wait()
        for w in range(windows):
            for part in range(4):
                rows = slice(part * 128, (part + 1) * 128)
                att_ref[w, :, rows] = attt_ref[w, rows, :].astype(F32).T.astype(BF16)
        if direct:
            keep_weight.wait()
            run(4, *proj, *fc1, *fc2)


def front(inputs, table, extents, vectors, weights, packed, depth, direct):
    windows = inputs.shape[0]
    once = lambda shape: pl.BlockSpec(shape, lambda h: (0,) * len(shape), pipeline_mode=pl.Buffered(1))
    anywhere = pl.BlockSpec(memory_space=pl.ANY)
    outs = [
        (anywhere, jax.ShapeDtypeStruct((windows, 3 * D, LANES), BF16)),
        (
            pl.BlockSpec((windows, 1, WIN, LANES), lambda h: (0, h, 0, 0)),
            jax.ShapeDtypeStruct((windows, HEADS, WIN, LANES), BF16),
        ),
        (once((windows, WIN, D)), jax.ShapeDtypeStruct((windows, WIN, D), BF16)),
        (
            pl.BlockSpec((windows, HDIM, LANES), lambda h: (0, h, 0)),
            jax.ShapeDtypeStruct((windows, D, LANES), BF16),
        ),
        (once((windows, HEADS, LANES)), jax.ShapeDtypeStruct((windows, HEADS, LANES), F32)),
        (once((16, D)), jax.ShapeDtypeStruct((16, D), F32)),
        (once((1, FF)), jax.ShapeDtypeStruct((1, FF), F32)),
    ]
    scratch = [
        pltpu.VMEM((HEADS, FLAT, SPREAD), F32),
        pltpu.VMEM((WIN_W, HEADS, SPREAD), F32),
        pltpu.VMEM((HEADS, WIN, WIN), F32),
        pltpu.VMEM((windows, WIN, D), F32),
        pltpu.VMEM((windows, WIN, D), BF16),
        pltpu.VMEM((windows, 16, WIN), BF16),
        pltpu.VMEM((windows, 3 * D, LANES), BF16),
        pltpu.VMEM((windows, D, WIN), BF16),
        pltpu.VMEM(inputs.shape, BF16),
        pltpu.SemaphoreType.DMA((2,)),
    ]
    args = [inputs, table, extents]
    small = vectors[0].shape[1]
    extra = {}
    if direct:
        args += list(vectors) + list(weights)
        specs = [once(item.shape) for item in args]
        specs[0], specs[2] = anywhere, pl.BlockSpec(memory_space=pltpu.SMEM)
        wholes = [jax.ShapeDtypeStruct((2, 2, depth, 2) + item.shape, BF16) for item in weights]
        outs += [(anywhere, whole) for whole in wholes]
        slots = gather_slots(depth) * (1 + len(QKV_PIECES) + len(OTHER_PIECES)) + 1
        scratch += [
            pltpu.VMEM((16, 128), BF16),
            pltpu.VMEM(weights[0].shape, BF16),
            pltpu.VMEM((2, 2, depth, 2, 16, 128), BF16),
            pltpu.VMEM(wholes[0].shape, BF16),
            pltpu.SemaphoreType.DMA((slots,)),
            pltpu.SemaphoreType.DMA((slots,)),
        ]
        extra = dict(collective_id=0, has_side_effects=True)
    else:
        args += [packed, weights[0]]
        specs = [once(item.shape) for item in args]
        specs[0], specs[2] = anywhere, pl.BlockSpec(memory_space=pltpu.SMEM)
    return pl.pallas_call(
        functools.partial(front_kernel, (windows, depth, direct, small)),
        grid=(HEADS,),
        in_specs=specs,
        out_specs=[spec for spec, _ in outs],
        out_shape=[shape for _, shape in outs],
        scratch_shapes=scratch,
        compiler_params=pltpu.CompilerParams(vmem_limit_bytes=60 * MIB, **extra),
        name="front",
    )(*args)


def mlp_kernel(*refs):
    refs = list(refs)
    take = lambda count: [refs.pop(0) for _ in range(count)]
    x_in, att_in, cot_in, proj_in, fc1_in, fc2_in = take(6)
    extents_ref, vec_ref, fshift1_ref = take(3)
    out_out, rgrad_out, agrad_out, fc1g_out, fc2g_out, projg_out = take(6)
    sums_ref, fsum_ref = take(2)
    x_ref, att_ref, gout_ref, proj_ref, fc1_ref, fc2_ref = take(6)
    out_ref, rgrad_ref, agrad_ref, fc1g_ref, fc2g_ref, projg_ref = take(6)
    act_ref, hid_ref, norm_ref, branch_ref, in_sems, out_sems = take(6)
    rows = x_ref.shape[0]
    block = rows // 2
    pieces = 4
    wide = FF // pieces
    halves = [slice(i * block, (i + 1) * block) for i in range(2)]
    loads, stores = {}, []

    def load(name, source, target):
        copy = pltpu.make_async_copy(source, target, in_sems.at[len(loads)])
        copy.start()
        loads[name] = copy

    def store(source, target):
        copy = pltpu.make_async_copy(source, target, out_sems.at[len(stores)])
        copy.start()
        stores.append(copy)

    load("proj", proj_in, proj_ref)
    load("att0", att_in.at[halves[0]], att_ref.at[halves[0]])
    load("x0", x_in.at[halves[0]], x_ref.at[halves[0]])
    load("fc1", fc1_in, fc1_ref)
    load("cot0", cot_in.at[halves[0]], gout_ref.at[halves[0]])
    load("fc2", fc2_in, fc2_ref)
    load("att1", att_in.at[halves[1]], att_ref.at[halves[1]])
    load("x1", x_in.at[halves[1]], x_ref.at[halves[1]])
    load("cot1", cot_in.at[halves[1]], gout_ref.at[halves[1]])
    pshift, gain, shift, fshift2 = [vec_ref[i : i + 1] for i in range(4, 8)]
    sums_ref[...] = jnp.zeros_like(sums_ref)
    fsum_ref[...] = jnp.zeros_like(fsum_ref)

    def keep_column(i):
        spot = spots_of((WIN, 1), 0)
        each = block // WIN
        keeps = [kept(spot, extents_ref, i * each + w).astype(F32) for w in range(each)]
        return jnp.concatenate(keeps, axis=0)

    for i, at in enumerate(halves):
        keep = keep_column(i)
        if i == 0:
            loads["proj"].wait()
        loads[f"att{i}"].wait()
        loads[f"x{i}"].wait()
        resid = x_ref[at, :].astype(F32) + dot_nn(att_ref[at, :], proj_ref[...]) + pshift
        unit, scale = standardize(resid)
        normed = (unit * gain + shift).astype(BF16)
        norm_ref[at, :] = normed
        loads[f"cot{i}"].wait()
        gout = gout_ref[at, :].astype(F32) * keep
        gout_low = gout.astype(BF16)
        gout_ref[at, :] = gout_low
        if i == 0:
            loads["fc1"].wait()
            loads["fc2"].wait()
        total = resid + fshift2
        grad_two = None
        for part in range(pieces):
            columns = slice(part * wide, (part + 1) * wide)
            hidden = dot_nn(normed, fc1_ref[:, columns]) + fshift1_ref[:, columns]
            active, slope = gelu_parts(hidden)
            active = active.astype(BF16)
            act_ref[at, columns] = active
            total = total + dot_nn(active, fc2_ref[columns, :])
            hgrad = (dot_nt(gout_low, fc2_ref[columns, :]) * slope).astype(BF16)
            hid_ref[at, columns] = hgrad
            fsum_ref[0:1, columns] += jnp.sum(hgrad.astype(F32), axis=0, keepdims=True)
            back = dot_nt(hgrad, fc1_ref[:, columns])
            grad_two = back if grad_two is None else grad_two + back
        out_ref[at, :] = (total * keep).astype(BF16)
        store(out_ref.at[at], out_out.at[at])
        rgrad = gout + norm_backward(grad_two, unit, scale, gain)
        rgrad_ref[at, :] = rgrad
        store(rgrad_ref.at[at], rgrad_out.at[at])
        branch = rgrad.astype(BF16)
        branch_ref[at, :] = branch
        each = block // WIN
        for w in range(each):
            low = rgrad[w * WIN : (w + 1) * WIN].astype(BF16)
            agrad_ref[i * each + w, :, :WIN] = dot_nt(proj_ref[...], low).astype(BF16)
        store(agrad_ref.at[i * each : (i + 1) * each], agrad_out.at[i * each : (i + 1) * each])
        sums_ref[0:1, :] += jnp.sum(gout, axis=0, keepdims=True)
        sums_ref[1:2, :] += jnp.sum(grad_two * unit, axis=0, keepdims=True)
        sums_ref[2:3, :] += jnp.sum(grad_two, axis=0, keepdims=True)
        sums_ref[3:4, :] += jnp.sum(branch.astype(F32), axis=0, keepdims=True)
    for part in range(pieces):
        columns = slice(part * wide, (part + 1) * wide)
        fc2g_ref[columns, :] = dot_tn(act_ref[:, columns], gout_ref[...]).astype(BF16)
        store(fc2g_ref.at[columns], fc2g_out.at[columns])
    for part in range(pieces):
        columns = slice(part * wide, (part + 1) * wide)
        fc1g_ref[:, columns] = dot_tn(norm_ref[...], hid_ref[:, columns]).astype(BF16)
        store(fc1g_ref.at[:, columns], fc1g_out.at[:, columns])
    projg_ref[...] = dot_tn(att_ref[...], branch_ref[...]).astype(BF16)
    store(projg_ref, projg_out)
    for copy in stores:
        copy.wait()


def feed_forward(x_rows, att_rows, cot_rows, proj, fc1, fc2, extents, vectors, fshift1):
    rows = x_rows.shape[0]
    vmem = pl.BlockSpec(memory_space=pltpu.VMEM)
    anywhere = pl.BlockSpec(memory_space=pl.ANY)
    streamed = [
        jax.ShapeDtypeStruct((rows, D), BF16),
        jax.ShapeDtypeStruct((rows, D), F32),
        jax.ShapeDtypeStruct((rows // WIN, D, LANES), BF16),
        jax.ShapeDtypeStruct((D, FF), BF16),
        jax.ShapeDtypeStruct((FF, D), BF16),
        jax.ShapeDtypeStruct((D, D), BF16),
    ]
    return pl.pallas_call(
        mlp_kernel,
        in_specs=[anywhere] * 6 + [pl.BlockSpec(memory_space=pltpu.SMEM), vmem, vmem],
        out_specs=[anywhere] * 6 + [vmem] * 2,
        out_shape=streamed + [jax.ShapeDtypeStruct((8, D), F32), jax.ShapeDtypeStruct((8, FF), F32)],
        scratch_shapes=[
            pltpu.VMEM((rows, D), BF16),
            pltpu.VMEM((rows, D), BF16),
            pltpu.VMEM((rows, D), BF16),
            pltpu.VMEM((D, D), BF16),
            pltpu.VMEM((D, FF), BF16),
            pltpu.VMEM((FF, D), BF16),
        ]
        + [pltpu.VMEM(item.shape, item.dtype) for item in streamed]
        + [
            pltpu.VMEM((rows, FF), BF16),
            pltpu.VMEM((rows, FF), BF16),
            pltpu.VMEM((rows, D), BF16),
            pltpu.VMEM((rows, D), BF16),
            pltpu.SemaphoreType.DMA((9,)),
            pltpu.SemaphoreType.DMA((15,)),
        ],
        compiler_params=pltpu.CompilerParams(vmem_limit_bytes=62 * MIB),
        name="feed_forward",
    )(x_rows, att_rows, cot_rows, proj, fc1, fc2, extents, vectors, fshift1)


FEED_PIECES = (
    (2, 0, 256, False),
    (2, 256, 256, True),
    (1, 0, 1024, False),
    (1, 1024, 1024, True),
    (0, 0, 256, False),
    (0, 256, 256, True),
)


def back_kernel(setup, *refs):
    windows, depth, direct, small = setup
    refs = list(refs)
    take = lambda count: [refs.pop(0) for _ in range(count)]
    qkvt_in, attt_ref, agrad_ref, inv_ref, probs_ref, x_in, rgrad_in, weight_in = take(8)
    vec_ref, sums_ref, fsum_ref = take(3)
    if direct:
        grads = take(3)
    igrad_ref, table_ref = take(2)
    if direct:
        vec_own, qkv_own, *owns = take(5)
    else:
        qkv_work, vec_work = take(2)
    dqkvt_ref, sum_ref, folded_ref, line_ref, total_ref, dq_ref, norm_ref, grad_ref, csum_ref = take(9)
    qkvt_ref, x_ref, rgrad_ref, weight_ref, last_ref, hand_sem = take(6)
    if direct:
        qkv_work, vec_work, table_work, table_full = take(4)
        vec_group, vec_z, vec_mine, table_group, table_z, *works = take(8)
        sems = (refs[-2], refs[-1])
        helds = refs[:-2]
    step = pl.program_id(0)
    head = (step + FEW) % HEADS
    count = D // small
    gain, shift = vec_ref[0:1], vec_ref[1:2]
    run = lambda stage, *lists: [stages[stage]() for stages in lists]
    hands = []
    for source, target in (
        (qkvt_in.at[:, STARTS[1] :], qkvt_ref.at[:, STARTS[1] :]),
        (qkvt_in.at[:, : STARTS[1]], qkvt_ref.at[:, : STARTS[1]]),
        (x_in, x_ref),
        (weight_in, weight_ref),
        (rgrad_in, rgrad_ref),
    ):
        hands.append(pltpu.make_async_copy(source, target, hand_sem.at[len(hands)]))

    if direct:
        place = Place(depth)
        base, spot = len(works) + 1, 0

        def piece(work, write, x_first):
            nonlocal base, spot
            stages = scatter_stages(place, work, helds[spot : spot + 4], sems, base, x_first, write)
            base += scatter_slots(depth)
            spot += 4
            return stages

        def whole(own, columns):
            def write(total):
                own[:, columns] = total

            return write

        def unpermuted(start, size):
            def write(total):
                for at in range(start, start + size, 128):
                    group = int(at >= STARTS[1])
                    width = GROUPS[group][1] * HDIM
                    part, rest = divmod(at - STARTS[group], width)
                    to = part * D + GROUPS[group][0] * HDIM + rest
                    qkv_own[:, to : to + 128] = total[:, at - start : at - start + 128]

            return write

        feed = []
        for i, start, size, x_first in FEED_PIECES:
            columns = pl.ds(start, size)
            feed.append(piece(works[i].at[:, :, :, :, :, columns], whole(owns[i], columns), x_first))
        fc2, fc1 = feed[:2], feed[2:]
        qkv = []
        for _, start, size, x_first in QKV_PIECES:
            view = qkv_work.at[:, :, :, :, :, pl.ds(start, size)]
            qkv.append(piece(view, unpermuted(start, size), x_first))
        vector = small_scatter_stages(
            place, vec_work, vec_group, vec_z, vec_mine, sems, base, whole(vec_own, slice(None))
        )
        base += group_slots(depth)
        table = small_sum_stages(place, table_work, table_group, table_z, table_full, sems, base)
        loads = [pltpu.make_async_copy(grads[i], works[i], sems[0].at[i]) for i in range(len(works))]

    def turn_over(group):
        for part in range(3 * GROUPS[group][1] * HDIM // 128):
            rows = slice(STARTS[group] + part * 128, STARTS[group] + (part + 1) * 128)
            columns = slice(part * 128, (part + 1) * 128)
            total = 0.0
            for w in range(windows):
                low = dqkvt_ref[w, rows, :WIN].astype(F32).T
                dq_ref[w, :, columns] = low.astype(BF16)
                total = total + jnp.sum(low, axis=0, keepdims=True)
            csum_ref[0:1, rows] = total

    def weight_grad(index):
        _, start, size, _ = QKV_PIECES[index]
        local = start - STARTS[index // 2]
        total = 0.0
        for w in range(windows):
            total = total + dot_tn(norm_ref[w], dq_ref[w, :, local : local + size])
        columns = slice(start, start + size)
        if direct:
            qkv_work[:, :, :, :, :, columns] = total.astype(BF16).reshape(2, 2, depth, 2, small, size)
        else:
            qkv_work[:, columns] = total.astype(BF16)

    def norm_grad(group, w):
        width = 3 * GROUPS[group][1] * HDIM
        return dot_nt(dq_ref[w, :, :width], weight_ref[:, STARTS[group] : STARTS[group] + width])

    @pl.when(step == 0)
    def _():
        if direct:
            welcome = place.greet(group=True)
        hands[0].start()
        if direct:
            for load in loads:
                load.start()
        for hand in hands[1:]:
            hand.start()
        if direct:
            for load in loads:
                load.wait()
            welcome()
            run(0, *fc2, *fc1)
        hands[0].wait()

    @pl.when(step == HEADS - FEW)
    def _():
        for hand in hands[1:4]:
            hand.wait()
        for w in range(windows):
            unit, _ = standardize(x_ref[w].astype(F32))
            norm_ref[w] = (unit * gain + shift).astype(BF16)
        turn_over(1)
        if direct:
            run(2, *fc1)
        for index in (2, 3):
            weight_grad(index)
            if direct:
                run(0, qkv[index])
        total_ref[...] = fold_bias(folded_ref, line_ref, range(FEW, FEW + 8))
        if direct:
            run(3, *fc2)
        for w in range(windows):
            grad_ref[w] = norm_grad(1, w)
        last_ref[...] = share_row(fsum_ref[0:1], count, FF // count, 64)
        if direct:
            run(1, *qkv[2:])
            run(3, *fc1)

    if direct:
        steps = (
            (3, ((1, fc2),)),
            (5, ((1, fc1),)),
            (10, ((2, fc2),)),
            (15, ((2, qkv[2:]),)),
        )
        for at, group in steps:

            @pl.when(step == at)
            def _(group=group):
                for stage, lists in group:
                    run(stage, *lists)

    row, key_row, value_row = head_rows(head)
    ones = jnp.ones((16, WIN), BF16)
    order = spots_of((16, WIN), 0)

    def prepare(w):
        grad = agrad_ref[w, :, :WIN].astype(F32) * inv_ref[w, pl.ds(head, 1), :WIN]
        mixed = attt_ref[w, :, :WIN].astype(F32)
        inner = -jnp.sum(grad * mixed, axis=0, keepdims=True)
        high = inner.astype(BF16).astype(F32)
        middle = (inner - high).astype(BF16).astype(F32)
        lowest = inner - high - middle
        extra = jnp.where(
            order == 0, high, jnp.where(order == 1, middle, jnp.where(order == 2, lowest, 0.0))
        ).astype(BF16)
        grad = grad.astype(BF16)
        values = qkvt_ref[w, pl.ds(value_row, HDIM), :WIN]
        probs_grad = dot_tn(
            jnp.concatenate([values, ones], axis=0), jnp.concatenate([grad, extra], axis=0)
        )
        return grad, probs_grad

    for first in range(0, windows, 2):
        pair = range(first, min(first + 2, windows))
        prepared = [prepare(w) for w in pair]
        expos = [probs_ref[w, 0, :, :WIN] for w in pair]
        grads_s = [expo.astype(F32) * item[1] for expo, item in zip(expos, prepared)]
        total = sum(grads_s[1:], grads_s[0])
        if first == 0:
            sum_ref[...] = total
        else:
            sum_ref[...] += total
        for w, expo, (grad, _), scores_grad in zip(pair, expos, prepared, grads_s):
            low = scores_grad.astype(BF16)
            queries = qkvt_ref[w, pl.ds(row, HDIM), :WIN]
            keys = qkvt_ref[w, pl.ds(key_row, HDIM), :WIN]
            dqkvt_ref[w, pl.ds(row, HDIM), :WIN] = (dot_nn(keys, low) * SCALE).astype(BF16)
            dqkvt_ref[w, pl.ds(key_row, HDIM), :WIN] = (dot_nt(queries, low) * LN2).astype(BF16)
            dqkvt_ref[w, pl.ds(value_row, HDIM), :WIN] = dot_nt(grad, expo).astype(BF16)

    folded_ref[head] = jnp.zeros((FLAT, SPREAD), F32)
    for u in range(WIN_T):
        start = (WIN_T - 1 - u) * FLAT
        folded_ref[head, :, start : start + WIN] += sum_ref[u * FLAT : (u + 1) * FLAT, :]

    @pl.when(step == HEADS - 1)
    def _():
        gain_sum, shift_sum = 0.0, 0.0

        def norm_sums(w):
            nonlocal gain_sum, shift_sum
            unit, _ = standardize(x_ref[w].astype(F32))
            grad = grad_ref[w] + norm_grad(0, w)
            grad_ref[w] = grad
            gain_sum = gain_sum + jnp.sum(grad * unit, axis=0, keepdims=True)
            shift_sum = shift_sum + jnp.sum(grad, axis=0, keepdims=True)

        def input_grad(w):
            unit, scale = standardize(x_ref[w].astype(F32))
            back = norm_backward(grad_ref[w], unit, scale, gain)
            igrad_ref[w] = (rgrad_ref[w] + back).astype(BF16)

        def vector_block():
            sums = lambda part: jnp.concatenate(
                [
                    csum_ref[0:1, start + part * heads * HDIM : start + (part + 1) * heads * HDIM]
                    for start, (_, heads) in zip(STARTS, GROUPS)
                ],
                axis=1,
            )
            rows = [
                gain_sum,
                shift_sum,
                sums(0),
                sums(2),
                sums_ref[3:4],
                sums_ref[1:2],
                sums_ref[2:3],
                sums_ref[0:1],
            ]
            block = share_vectors(jnp.concatenate(rows, axis=0), count, small)
            last = last_ref[...].reshape(count, 1, 128)
            return jnp.where(spots_of((count, 8, 128), 1) == 0, block + last, block)

        def write_table(total):
            span = OFFS_H * OFFS_W
            for k in range(OFFS_T):
                table_ref[:, k * span : (k + 1) * span] = total[k * HEADS : (k + 1) * HEADS, :span]

        outer = fold_bias(folded_ref, line_ref, list(range(FEW)) + list(range(FEW + 8, HEADS)))
        total = jnp.concatenate([outer[:, :FEW], total_ref[...], outer[:, FEW:]], axis=1)
        total = total.reshape(OFFS_T * HEADS, 256)
        hands[4].wait()
        if direct:
            total = jnp.concatenate([total, jnp.zeros((256 - OFFS_T * HEADS, 256), F32)], axis=0)
            table_work[...] = total.reshape(table_work.shape)
            run(0, table)
            turn_over(0)
            for index in range(2):
                weight_grad(index)
                run(0, qkv[index])
            norm_sums(0)
            run(1, *qkv[:2])
            norm_sums(1)
            run(1, table)
            norm_sums(2)
            norm_sums(3)
            vec_work[...] = vector_block().reshape(vec_work.shape)
            run(0, vector)
            run(2, *qkv[:2])
            run(3, *qkv[2:])
            input_grad(0)
            input_grad(1)
            run(2, table)
            input_grad(2)
            run(3, *qkv[:2])
            run(1, vector)
            input_grad(3)
            run(4, *fc2, *fc1)
            run(4, *qkv[2:])
            run(3, table)
            write_table(table_full[...].reshape(256, 256))
            run(4, *qkv[:2])
            run(2, vector)
        else:
            turn_over(0)
            weight_grad(0)
            weight_grad(1)
            for w in range(windows):
                norm_sums(w)
                input_grad(w)
            vec_work[...] = vector_block()
            write_table(total)


def back(qkvt, attt, agrad, inverse, probs, inputs, rgrad, weight, vectors, sums, fsum, grads, depth, direct):
    windows = qkvt.shape[0]
    count = lax.axis_size("dp") * lax.axis_size("fsdp")
    small = D // count
    once = lambda shape: pl.BlockSpec(shape, lambda h: (0,) * len(shape), pipeline_mode=pl.Buffered(1))
    anywhere = pl.BlockSpec(memory_space=pl.ANY)
    args = [qkvt, attt, agrad, inverse, probs, inputs, rgrad, weight, vectors, sums, fsum]
    specs = [once(item.shape) for item in args]
    for i in (1, 2):
        specs[i] = pl.BlockSpec((windows, HDIM, LANES), lambda h: (0, (h + FEW) % HEADS, 0))
    specs[4] = pl.BlockSpec((windows, 1, WIN, LANES), lambda h: (0, (h + FEW) % HEADS, 0, 0))
    for i in (0, 5, 6, 7):
        specs[i] = anywhere
    shapes = [
        jax.ShapeDtypeStruct(inputs.shape, BF16),
        jax.ShapeDtypeStruct((HEADS, OFFS_T * OFFS_H * OFFS_W), F32),
    ]
    scratch = [
        pltpu.VMEM((windows, 3 * D, LANES), BF16),
        pltpu.VMEM((WIN, WIN), F32),
        pltpu.VMEM((HEADS, FLAT, SPREAD), F32),
        pltpu.VMEM((WIN_W, 8, SPREAD), F32),
        pltpu.VMEM((OFFS_T, 8, 256), F32),
        pltpu.VMEM((windows, WIN, WIDE), BF16),
        pltpu.VMEM((windows, WIN, D), BF16),
        pltpu.VMEM((windows, WIN, D), F32),
        pltpu.VMEM((8, 3 * D), F32),
        pltpu.VMEM(qkvt.shape, BF16),
        pltpu.VMEM(inputs.shape, BF16),
        pltpu.VMEM(rgrad.shape, F32),
        pltpu.VMEM(weight.shape, BF16),
        pltpu.VMEM((count, 128), F32),
        pltpu.SemaphoreType.DMA((5,)),
    ]
    extra = {}
    if direct:
        lead = (2, 2, depth, 2)
        views = [item.reshape(lead + (-1, item.shape[1])) for item in grads]
        args += views
        specs += [anywhere] * len(views)
        shapes += [
            jax.ShapeDtypeStruct((8, 128), F32),
            jax.ShapeDtypeStruct((small, 3 * D), F32),
        ] + [jax.ShapeDtypeStruct(item.shape[-2:], F32) for item in views]
        scratch += [
            pltpu.VMEM(lead + (small, 3 * D), BF16),
            pltpu.VMEM(lead + (8, 128), F32),
            pltpu.VMEM((2, 2, 2, 32, 256), F32),
            pltpu.VMEM((2, 2, 2, 32, 256), F32),
            pltpu.VMEM((7, depth, 8, 128), F32),
            pltpu.VMEM((depth - 1, 8, 128), F32),
            pltpu.VMEM((depth, 8, 128), F32),
            pltpu.VMEM((7, 32, 256), F32),
            pltpu.VMEM((depth, 32, 256), F32),
        ] + [pltpu.VMEM(item.shape, BF16) for item in views]
        for i, _, size, x_first in FEED_PIECES:
            scratch += held_shapes(depth, views[i].shape[-2], size, BF16, x_first)
        for _, _, size, x_first in QKV_PIECES:
            scratch += held_shapes(depth, small, size, BF16, x_first)
        exchanges = len(FEED_PIECES) + len(QKV_PIECES)
        slots = len(views) + 1 + scatter_slots(depth) * exchanges + 2 * group_slots(depth) + 7
        scratch += [pltpu.SemaphoreType.DMA((slots,)), pltpu.SemaphoreType.DMA((slots,))]
        extra = dict(collective_id=1, has_side_effects=True)
    else:
        shapes += [
            jax.ShapeDtypeStruct((D, 3 * D), BF16),
            jax.ShapeDtypeStruct((count, 8, 128), F32),
        ]
    return pl.pallas_call(
        functools.partial(back_kernel, (windows, depth, direct, small)),
        grid=(HEADS,),
        in_specs=specs,
        out_specs=[once(item.shape) for item in shapes],
        out_shape=shapes,
        scratch_shapes=scratch,
        compiler_params=pltpu.CompilerParams(vmem_limit_bytes=63 * MIB, **extra),
        name="back",
    )(*args)


def hand_kernel(small, vec_ref, *refs):
    count = (len(refs) - 11) // 3
    sources, vectors, targets = refs[:count], refs[count : count + 9], refs[count + 9 : 2 * count + 9]
    holds, ins, outs = refs[2 * count + 9 : -2], refs[-2], refs[-1]
    first, second = [], []
    for source, hold, target in zip(sources, holds, targets):
        parts = range(source.shape[0]) if len(source.shape) == 3 else (slice(None),)
        for part in parts:
            i = len(first)
            first.append(pltpu.make_async_copy(source.at[part], hold.at[part], ins.at[i]))
            second.append(pltpu.make_async_copy(hold.at[part], target.at[part], outs.at[i]))
    for copy in first:
        copy.start()
    for i in range(8):
        vectors[i][...] = vec_ref[i : i + 1, :small]
    vectors[8][...] = vec_ref[0:1, 64 : 64 + vectors[8].shape[1]]
    for one, two in zip(first, second):
        one.wait()
        two.start()
    for copy in second:
        copy.wait()


def hand_over(vector_own, items, small):
    vmem = pl.BlockSpec(memory_space=pltpu.VMEM)
    anywhere = pl.BlockSpec(memory_space=pl.ANY)
    vectors = [jax.ShapeDtypeStruct((1, small), F32)] * 8 + [jax.ShapeDtypeStruct((1, 4 * small), F32)]
    semaphores = pltpu.SemaphoreType.DMA((len(items) + items[0].shape[0],))
    return pl.pallas_call(
        functools.partial(hand_kernel, small),
        in_specs=[vmem] + [anywhere] * len(items),
        out_specs=[vmem] * 9 + [anywhere] * len(items),
        out_shape=vectors + [jax.ShapeDtypeStruct(item.shape, item.dtype) for item in items],
        scratch_shapes=[pltpu.VMEM(item.shape, item.dtype) for item in items] + [semaphores, semaphores],
        compiler_params=pltpu.CompilerParams(vmem_limit_bytes=62 * MIB),
        name="hand_over",
    )(vector_own, *items)


def gathered(value):
    return lax.all_gather(value, AXES, axis=0, tiled=True)


def scattered(value):
    return lax.psum_scatter(value, AXES, scatter_dimension=0, tiled=True)


def per_device(
    inputs,
    extents,
    cotangent,
    ln1_gain,
    ln1_shift,
    qkv_weight,
    query_bias,
    value_bias,
    bias_table,
    proj_weight,
    proj_shift,
    ln2_gain,
    ln2_shift,
    fc1_weight,
    fc1_shift,
    fc2_weight,
    fc2_shift,
):
    windows = inputs.shape[0]
    rows = windows * WIN
    small = ln1_gain.shape[0]
    count = D // small
    depth = lax.axis_size("fsdp") // 2
    direct = small % 16 == 0 and lax.axis_size("dp") == 4
    vectors = [
        item[None]
        for item in (
            ln1_gain,
            ln1_shift,
            query_bias,
            value_bias,
            proj_shift,
            ln2_gain,
            ln2_shift,
            fc2_shift,
            fc1_shift,
        )
    ]
    weights = (qkv_weight, proj_weight, fc1_weight, fc2_weight)
    packed = None
    if not direct:
        packed = jnp.concatenate([jnp.pad(item, ((0, 0), (0, 128 - item.shape[1]))) for item in vectors])
        packed = gathered(jnp.pad(packed, ((0, 16 - len(vectors)), (0, 0))))
        weights = [gathered(item) for item in weights]
        parts = weights[0].reshape(D, 3, D)
        cut = FEW * HDIM
        weights[0] = jnp.concatenate(
            [parts[:, :, :cut].reshape(D, 3 * cut), parts[:, :, cut:].reshape(D, 3 * (D - cut))], axis=1
        )
    x_rows = inputs.reshape(rows, D)
    qkvt, probs, att, attt, inverse, full_vectors, fshift1, *wholes = front(
        inputs, bias_table.T, extents, vectors, weights, packed, depth, direct
    )
    if direct:
        weights = [item.reshape(-1, item.shape[-1]) for item in wholes]
    qkv_full, proj_full, fc1_full, fc2_full = weights
    output, rgrad, agrad, fc1_grad, fc2_grad, proj_grad, sums, fsum = feed_forward(
        x_rows,
        att.reshape(rows, D),
        cotangent.reshape(rows, D),
        proj_full,
        fc1_full,
        fc2_full,
        extents,
        full_vectors,
        fshift1,
    )
    matrices = (proj_grad, fc1_grad, fc2_grad)
    input_grad, table_grad, *rest = back(
        qkvt,
        attt,
        agrad,
        inverse,
        probs,
        inputs,
        rgrad.reshape(windows, WIN, D),
        qkv_full,
        full_vectors,
        sums,
        fsum,
        matrices,
        depth,
        direct,
    )
    if direct:
        vector_own, *items = rest
        items = [input_grad, table_grad] + items
        *owned, input_grad, table_grad, qkv_own, proj_own, fc1_own, fc2_own = hand_over(
            vector_own, items, small
        )
        owned = [item.reshape(-1) for item in owned]
    else:
        cut = FEW * HDIM
        qkv_grad = jnp.concatenate(
            [rest[0][:, : 3 * cut].reshape(D, 3, cut), rest[0][:, 3 * cut :].reshape(D, 3, D - cut)], axis=2
        ).reshape(D, 3 * D)
        qkv_own, proj_own, fc1_own, fc2_own = [
            scattered(item.astype(F32)) for item in (qkv_grad,) + matrices
        ]
        vector_own = scattered(rest[1])[0]
        owned = [vector_own[i, :small] for i in range(8)] + [vector_own[0, 64 : 64 + FF // count]]
        table_grad = lax.psum(table_grad, AXES)
    return (
        output.reshape(inputs.shape),
        input_grad.reshape(inputs.shape),
        owned[0],
        owned[1],
        qkv_own,
        owned[2],
        owned[3],
        table_grad.T,
        proj_own,
        owned[4],
        owned[5],
        owned[6],
        fc1_own,
        owned[8],
        fc2_own,
        owned[7],
    )


def solution(mesh):
    rows = P(AXES, None)
    vector = P(AXES)
    block = P(AXES, None, None)
    in_specs = (
        block,
        rows,
        block,
        vector,
        vector,
        rows,
        vector,
        vector,
        P(),
        rows,
        vector,
        vector,
        vector,
        rows,
        vector,
        rows,
        vector,
    )
    out_specs = (
        block,
        block,
        vector,
        vector,
        rows,
        vector,
        vector,
        P(),
        rows,
        vector,
        vector,
        vector,
        rows,
        vector,
        rows,
        vector,
    )
    return jax.shard_map(
        per_device, mesh=mesh, in_specs=in_specs, out_specs=out_specs, check_vma=False
    )
```
